128 devices in a mesh: dp: 32 (over y, z_hi, x), seq: 4 (over z_lo, core).
Axes of the slice: x: 4, y: 4, z: 4 (z_hi: 2, z_lo: 2; z = z_hi * 2 + z_lo), core: 2. Of those that a mesh axis runs over, the one named last changes fastest.
Arguments:
- normed: bfloat16 [32768, 7168], P(('dp', 'seq')), may hold values from -24 to 24
- queries: bfloat16 [32768, 3584], P(('dp', 'seq')), may hold values from -32 to 32
- output_gradient: bfloat16 [32768, 3584], P(('dp', 'seq')), may hold values from -6 to 6
- doc_lengths: int32 [32, 8], P('dp'), may hold values from 1 to 512, 1024 in all within a row
- master: float32 [7168, 1024], P('dp'), may hold values from -0.0625 to 0.0625
- moment_one: bfloat16 [7168, 1024], P('dp'), may hold values from -2 to 2
- moment_two: bfloat16 [7168, 1024], P('dp'), may hold values from 0.0009994507 to 0.099609375
Outputs:
- d_queries: bfloat16 [32768, 3584], P(('dp', 'seq'))
- d_normed: bfloat16 [32768, 7168], P(('dp', 'seq'))
- new_master: float32 [7168, 1024], P('dp')
- new_moment_one: bfloat16 [7168, 1024], P('dp')
- new_moment_two: bfloat16 [7168, 1024], P('dp')
The draws below stay inside these ranges and needn't reach their ends.
All inputs are finite; a program needn't handle non-finite values.
Results may differ from the reference program's by a relative error of at most 0.039.
The reference program's roundings to bfloat16 on the way count: a program that leaves them out, or rounds other values in their place, can miss the bound.
Values may be sent and summed in bfloat16 or wider, within the bound.
A program may use at most 192 MiB of HBM per device.

```python
import math
import jax
import jax.numpy as jnp
import numpy as np
from jax import lax

D = 7168
HEAD_SIZE = 128
QUERY_HEADS = 28
KEY_VALUE_HEADS = 4
DOCS = 8
TOK_DEV = 256
KVW = 1024
SEQUENCE_TOKENS = 1024
TOKENS = 32768
N_DP = 32
N_SEQ = 4


def draw_queries(key, part):
    key = jax.random.fold_in(key, 7)
    key_base = jax.random.fold_in(key, 0)
    base = jax.random.normal(key_base, (TOKENS, QUERY_HEADS * HEAD_SIZE), jnp.float32)
    values = jnp.clip(base, -4.0, 4.0)
    return values.astype(jnp.bfloat16)


def raised(entries, own_key, source, target, blocks, factor):
    owner, partner = [(jnp.arange(entries.shape[axis_at]) // (entries.shape[axis_at] // blocks)).reshape([-1 if axis == axis_at else 1 for axis in range(entries.ndim)]) for axis_at in (source, target)]
    chosen = jax.random.permutation(own_key, blocks)[partner]
    strong = (owner == chosen) | (owner == (partner + blocks // 2) % blocks)
    return jnp.where(strong, factor * entries, entries)


def level_of(key, shape, pieces, least, high):
    gain = 1.0
    for position, shards_of in pieces:
        draws = jax.random.uniform(jax.random.fold_in(jax.random.fold_in(key, 6), position), (shards_of,), jnp.float32, least / len(pieces), high / len(pieces))
        gain = gain * jnp.repeat(jnp.exp(draws), shape[position] // shards_of).reshape((-1,) + (1,) * (len(shape) - 1 - position))
    return gain


def length_profile(number_of, total, limit, skew):
    portions = [(1 << 20) // math.isqrt(rank ** skew) + 1 for rank in range(2, number_of + 1)]
    rest, given = total - limit - (number_of - 1), [1] * (number_of - 1)
    while rest > 0:
        movable = [i for i in range(number_of - 1) if given[i] < limit]
        mass, budget = sum([portions[i] for i in movable]), rest
        for i in movable:
            more = min(limit - given[i], max(1, budget * portions[i] // mass), rest)
            given[i] = given[i] + more
            rest = rest - more
    return np.array([limit] + given)


def ragged_sizes(key, number_of, total, reach, lean):
    if number_of == 2:
        one = jax.random.randint(key, (), max(1, total - reach), min(reach, total - 1) + 1)
        return jnp.stack([one, total - one])
    tallies = jnp.asarray(length_profile(number_of, total, reach, lean), jnp.int32)
    twos = (number_of - 1) // 2
    source_of, taker = tallies[1:1 + 2 * twos:2], tallies[2:2 + 2 * twos:2]
    room = jnp.minimum(source_of - 1, reach - taker)
    shifted = jax.random.randint(jax.random.fold_in(key, 1), (twos,), 0, 1 << 20) % (room + 1)
    tallies = tallies.at[1:1 + 2 * twos:2].set(source_of - shifted).at[2:2 + 2 * twos:2].set(taker + shifted)
    return tallies[jax.random.permutation(jax.random.fold_in(key, 2), number_of)]


def scatter_about(own_key, extent, deviation, limit, shards=(), kind=jnp.bfloat16):
    loudness = level_of(own_key, extent, shards, -0.22, 0.18) if shards else 1.0
    drawn = jax.random.normal(own_key, extent, jnp.float32) * deviation * loudness
    return jnp.minimum(jnp.maximum(drawn, -limit), limit).astype(kind)


def bell_draw_with(key, extent, scale, reach, shards, heavy, held_as=jnp.bfloat16):
    entries = scale * jax.random.normal(key, extent, jnp.float32)
    if shards:
        entries = entries * level_of(key, extent, shards, -0.22, 0.18)
    return jnp.clip(raised(entries, jax.random.fold_in(key, 3), *heavy), -reach, reach).astype(held_as)


def setup_inputs(seed: int = 0) -> dict:
    key_of = jax.random.split(jax.random.key(seed), 8)
    return {
        "normed": bell_draw_with(key_of[0], (TOKENS, D), 1.0, 24.0, ((0, 128),), (0, 1, 128, 5.5)),
        "queries": draw_queries(jax.random.fold_in(key_of[7], 71), 0),
        "output_gradient": scatter_about(key_of[2], (TOKENS, QUERY_HEADS * HEAD_SIZE), 1.0, 6.0, ((0, 128),)),
        "doc_lengths": jax.vmap(lambda own: ragged_sizes(own, DOCS, SEQUENCE_TOKENS, SEQUENCE_TOKENS // 2, 2))(jax.random.split(key_of[3], N_DP)).reshape((N_DP, DOCS)).astype(jnp.int32),
        "master": scatter_about(key_of[4], (D, KVW), D ** -0.5, 0.0625, ((0, 32),), jnp.float32),
        "moment_one": scatter_about(key_of[5], (D, KVW), 0.3, 2.0, ((0, 32),)),
        "moment_two": jnp.clip(jnp.exp(math.log(0.099609375) - 4.6018058 * jax.random.uniform(key_of[6], (D, KVW), jnp.float32) ** level_of(key_of[6], (D, KVW), ((0, 32),), -0.2, 0.2)), 0.0009994507, 0.099609375).astype(jnp.bfloat16),
    }


def doc_mask(length_row, seq_len):
    doc_ends = jnp.cumsum(length_row).astype(jnp.int32)
    positions = jnp.arange(seq_len, dtype=jnp.int32)
    doc_ids = lax.optimization_barrier(jnp.sum((positions[:, None] >= doc_ends[None, :]).astype(jnp.int32), axis=1))
    return (positions, doc_ids)

def reference(normed, queries, output_gradient, doc_lengths, master, moment_one, moment_two):
    weights = master.astype(jnp.bfloat16)
    key_value_full = jnp.dot(normed, weights, preferred_element_type=jnp.float32).astype(jnp.bfloat16)
    query_groups = QUERY_HEADS // KEY_VALUE_HEADS
    score_scale = HEAD_SIZE ** (-0.5)
    query_sequence = queries.reshape(N_DP, SEQUENCE_TOKENS, KEY_VALUE_HEADS, query_groups, HEAD_SIZE)
    output_grad_sequence = output_gradient.reshape(N_DP, SEQUENCE_TOKENS, KEY_VALUE_HEADS, query_groups, HEAD_SIZE)
    key_value_sequence = key_value_full.reshape(N_DP, SEQUENCE_TOKENS, KEY_VALUE_HEADS, 2, HEAD_SIZE)

    def one_sequence(packed):
        q_part, do_part, kv_part, length_row = packed
        positions, doc_ids = doc_mask(length_row, SEQUENCE_TOKENS)
        allowed = (doc_ids[:, None] == doc_ids[None, :]) & (positions[:, None] >= positions[None, :])
        keys = kv_part[:, :, 0, :].astype(jnp.float32)
        values = kv_part[:, :, 1, :].astype(jnp.float32)
        q_wide = q_part.astype(jnp.float32)
        do_wide = do_part.astype(jnp.float32)
        scores = jnp.einsum('qhgd,khd->hgqk', q_wide, keys) * score_scale
        scores = jnp.where(allowed, scores, -1e+30)
        row_top = lax.optimization_barrier(jnp.max(scores, axis=-1, keepdims=True))
        raw = jnp.where(allowed, jnp.exp(scores - row_top), 0.0)
        probability = raw / lax.optimization_barrier(jnp.sum(raw, axis=-1, keepdims=True))
        prob_half = lax.optimization_barrier(probability.astype(jnp.bfloat16)).astype(jnp.float32)
        attended = jnp.einsum('hgqk,khd->qhgd', prob_half, values)
        row_delta = jnp.transpose(lax.optimization_barrier(jnp.sum(do_wide * attended, axis=-1)), (1, 2, 0))
        d_values = jnp.einsum('hgqk,qhgd->khd', prob_half, do_wide)
        d_probs = jnp.einsum('qhgd,khd->hgqk', do_wide, values)
        d_scores = (probability * (d_probs - row_delta[..., None])).astype(jnp.bfloat16)
        ds_wide = lax.optimization_barrier(d_scores).astype(jnp.float32)
        d_q = (jnp.einsum('hgqk,khd->qhgd', ds_wide, keys) * score_scale).astype(jnp.bfloat16)
        d_keys = jnp.einsum('hgqk,qhgd->khd', ds_wide, q_wide) * score_scale
        d_kv = jnp.stack([d_keys, d_values], axis=2).astype(jnp.bfloat16)
        return (d_q, d_kv)
    d_q_all, d_kv_all = lax.map(one_sequence, (query_sequence, output_grad_sequence, key_value_sequence, doc_lengths))
    d_queries = d_q_all.reshape(TOKENS, QUERY_HEADS * HEAD_SIZE)
    d_kv = d_kv_all.reshape(TOKENS, KVW)
    d_normed = jnp.dot(d_kv, weights.T, preferred_element_type=jnp.float32).astype(jnp.bfloat16)
    dev_rows = normed.reshape(N_DP * N_SEQ, TOK_DEV, D)
    dev_grads = d_kv.reshape(N_DP * N_SEQ, TOK_DEV, KVW)

    def add_term(grad_total, pair):
        term = jnp.dot(pair[0].T, pair[1], preferred_element_type=jnp.float32)
        rounded = lax.optimization_barrier(term.astype(jnp.bfloat16)).astype(jnp.float32)
        return (grad_total + rounded, None)
    grad_total, unused = lax.scan(add_term, jnp.zeros((D, KVW), jnp.float32), (dev_rows, dev_grads))
    grad = grad_total * float(TOKENS) ** (-0.5)
    first = 0.9 * moment_one.astype(jnp.float32) + 0.1 * grad
    second = 0.999 * moment_two.astype(jnp.float32) + 0.001 * grad * grad
    new_master = master - 0.001 * (first / (1.0 - 0.9 ** 3)) / (jnp.sqrt(second / (1.0 - 0.999 ** 3)) + 1e-08)
    return (d_queries, d_normed, new_master, first.astype(jnp.bfloat16), second.astype(jnp.bfloat16))
```

```python
import functools
import math

import jax
import jax.numpy as jnp
from jax import lax
from jax.experimental import pallas as pl
from jax.experimental.pallas import tpu as pltpu
from jax.sharding import PartitionSpec as P

HEAD = 128
GROUP = 7
X, Y, ZH = 4, 4, 2
TOK = 256
CT = 512
D = 7168
SHARDS = X * Y * ZH
ROWS = D // SHARDS
HR = ROWS // 2
COLS = 512
HC = COLS // 2
QW = 1792
ROW_BLOCK = X * ROWS
N_BLOCKS = Y * ZH
CHUNK = 128
N_CHUNKS = 5
LANES = GROUP * CHUNK
VMEM_LIMIT = 58 * 1024 * 1024
MESH = pl.DeviceIdType.MESH
ANY = pl.BlockSpec(memory_space=pl.ANY)
F32 = jnp.float32
BF16 = jnp.bfloat16


def dot(a, b, dims=((1,), (0,))):
    return lax.dot_general(a, b, (dims, ((), ())), preferred_element_type=F32)


class Place:
    def __init__(self):
        dp = lax.axis_index("dp")
        sq = lax.axis_index("seq")
        self.dp, self.sq = dp, sq
        self.x = lax.rem(dp, X)
        self.zh = lax.rem(lax.div(dp, X), ZH)
        self.y = lax.div(dp, X * ZH)
        self.core = lax.rem(sq, 2)
        self.zl = lax.div(sq, 2)

    def dev(self, x=None, y=None, zh=None, zl=None, core=None):
        x = self.x if x is None else x
        y = self.y if y is None else y
        zh = self.zh if zh is None else zh
        zl = self.zl if zl is None else zl
        core = self.core if core is None else core
        return ((y * ZH + zh) * X + x, zl * 2 + core)

    def along(self, axis, step):
        if axis == "x":
            return self.dev(x=lax.rem(self.x + step + X, X))
        return self.dev(y=lax.rem(self.y + step + Y, Y))

    def cross(self):
        return self.dev(zh=1 - self.zh, zl=1 - self.zl)

    def partner(self):
        return self.dev(zl=1 - self.zl)

    def other_core(self):
        return self.dev(core=1 - self.core)

    def greet(self):
        barrier = pltpu.get_barrier_semaphore()
        near = [self.along(a, s) for a in ("x", "y") for s in (1, -1)]
        near += [self.cross(), self.partner(), self.other_core()]
        for d in near:
            pl.semaphore_signal(barrier, inc=1, device_id=d, device_id_type=MESH)
        pl.semaphore_wait(barrier, len(near))


class Links:
    def __init__(self, send_sem, recv_sem, place):
        self.send_sem, self.recv_sem, self.place = send_sem, recv_sem, place
        self.index = {}
        self.sent = []

    def _copy(self, key, src, dst, dev):
        k = self.index.setdefault(key, len(self.index))
        return pltpu.make_async_remote_copy(
            src_ref=src,
            dst_ref=dst,
            send_sem=self.send_sem.at[k],
            recv_sem=self.recv_sem.at[k],
            device_id=dev,
            device_id_type=MESH,
        )

    def send(self, key, src, dst, dev):
        copy = self._copy(key, src, dst, dev)
        copy.start()
        self.sent.append(copy)

    def recv(self, key, dst):
        self._copy(key, dst, dst, self.place.other_core()).wait_recv()

    def drain(self):
        for copy in self.sent:
            copy.wait_send()


N_GATHER_SEMS = 96
N_LOCAL_SEMS = 24


def gather_kernel(
    normed, queries, out_grad, master,
    w_out, xt_out, q_out, do_out, kv_out,
    w, xs, xt, mas, kv, acc, send_sem, recv_sem, loc_sem,
):
    here = Place()
    links = Links(send_sem, recv_sem, here)
    n_local = [0]

    def local(src, dst):
        copy = pltpu.make_async_copy(src, dst, loc_sem.at[n_local[0]])
        n_local[0] += 1
        copy.start()
        return copy

    core = here.core
    col = pl.multiple_of(core * COLS, COLS)
    far_col = pl.multiple_of((1 - core) * COLS, COLS)
    del far_col
    own_rows = pl.ds(pl.multiple_of(core * TOK, TOK), TOK)
    far_rows = pl.ds(pl.multiple_of((1 - core) * TOK, TOK), TOK)
    get_master = local(master.at[:, pl.ds(col, COLS)], mas)
    own_normed = local(normed, xs.at[own_rows, :])
    own_q = pl.ds(pl.multiple_of(core * QW, QW), QW)
    far_q = pl.ds(pl.multiple_of((1 - core) * QW, QW), QW)
    pending = [
        local(queries.at[:, own_q], q_out.at[own_rows, :]),
        local(out_grad.at[:, own_q], do_out.at[own_rows, :]),
    ]
    here.greet()
    get_master.wait()

    pos = {"x": here.x, "y": here.y}
    size = {"x": X, "y": Y}

    def slot(p, da, db, zr, half=None):
        first, second = ("x", "y") if p == 0 else ("y", "x")
        at = {
            first: lax.rem(pos[first] + da + size[first], size[first]),
            second: lax.rem(pos[second] + db + size[second], size[second]),
        }
        zh = here.zh if zr == 0 else 1 - here.zh
        s = (at["y"] * ZH + zh) * X + at["x"]
        cols = pl.ds(0, COLS) if half is None else pl.ds(half * HC, HC)
        return w.at[s, pl.ds(p * HR, HR), cols]

    axes = (("x", "y"), ("y", "x"))
    own = (here.y * ZH + here.zh) * X + here.x
    w[own] = mas[...].astype(BF16)

    def send(key, ref, dev):
        links.send(key, ref, ref, dev)

    def second_from(p, da, zr):
        b = axes[p][1]
        for step in (1, -1):
            send(("b", p, zr, da, step, 0), slot(p, da, 0, zr), here.along(b, step))

    def start(zr):
        for p in range(2):
            a = axes[p][0]
            for step in (1, -1):
                send(("a", p, zr, step, 0), slot(p, 0, 0, zr), here.along(a, step))
        for p in range(2):
            second_from(p, 0, zr)

    def forward_first(zr):
        for p in range(2):
            a = axes[p][0]
            for step in (1, -1):
                links.recv(("a", p, zr, step, 0), slot(p, -step, 0, zr))
                half = 0 if step == 1 else 1
                send(("a", p, zr, step, 1), slot(p, -step, 0, zr, half), here.along(a, step))
            for step in (1, -1):
                second_from(p, -step, zr)

    def finish_first(zr):
        for p in range(2):
            for step in (1, -1):
                half = 0 if step == 1 else 1
                links.recv(("a", p, zr, step, 1), slot(p, 2, 0, zr, half))
            second_from(p, 2, zr)

    def forward_second(zr):
        for da in (0, -1, 1, 2):
            for p in range(2):
                b = axes[p][1]
                for step in (1, -1):
                    links.recv(("b", p, zr, da, step, 0), slot(p, da, -step, zr))
                    half = 0 if step == 1 else 1
                    send(
                        ("b", p, zr, da, step, 1),
                        slot(p, da, -step, zr, half),
                        here.along(b, step),
                    )

    def finish_second(zr):
        for da in (0, -1, 1, 2):
            for p in range(2):
                for step in (1, -1):
                    half = 0 if step == 1 else 1
                    links.recv(("b", p, zr, da, step, 1), slot(p, da, 2, zr, half))

    def turn(first, last):
        @pl.loop(first, last)
        def _(b):
            at = pl.ds(pl.multiple_of(b * HEAD, HEAD), HEAD)
            xt[at, :] = xs[:, at].T

    start(0)
    for p in range(2):
        send(("z", p), slot(p, 0, 0, 0), here.cross())
    links.send("normed", normed, xs.at[own_rows, :], here.other_core())
    links.send("q", queries.at[:, far_q], q_out.at[own_rows, :], here.other_core())
    links.send("do", out_grad.at[:, far_q], do_out.at[own_rows, :], here.other_core())
    forward_first(0)
    for p in range(2):
        links.recv(("z", p), slot(p, 0, 0, 1))
    start(1)
    finish_first(0)
    own_normed.wait()
    links.recv("normed", xs.at[far_rows, :])
    turn(0, 14)
    forward_first(1)
    turn(14, 28)
    finish_first(1)
    forward_second(0)
    turn(28, 42)
    forward_second(1)
    turn(42, 56)
    pending.append(local(xt, xt_out))
    finish_second(0)
    finish_second(1)
    pending.append(local(w, w_out))

    acc[...] = jnp.zeros_like(acc)

    @pl.loop(0, N_BLOCKS)
    def _(t):
        at = pl.ds(pl.multiple_of(t * ROW_BLOCK, 128), ROW_BLOCK)
        acc[...] += dot(xs[:, at], w[pl.ds(t * X, X)].reshape(ROW_BLOCK, COLS))

    kv[...] = acc[...].astype(BF16)
    links.send("kv", kv, kv_out.at[pl.ds(0, CT), :], here.partner())
    pending.append(local(kv, kv_out.at[pl.ds(CT, CT), :]))
    links.recv("q", q_out.at[far_rows, :])
    links.recv("do", do_out.at[far_rows, :])
    links.recv("kv", kv_out.at[pl.ds(0, CT), :])
    for copy in pending:
        copy.wait()
    links.drain()


def gather(normed, queries, out_grad, master):
    return pl.pallas_call(
        gather_kernel,
        out_shape=(
            jax.ShapeDtypeStruct((SHARDS, ROWS, COLS), BF16),
            jax.ShapeDtypeStruct((D, CT), BF16),
            jax.ShapeDtypeStruct((CT, QW), BF16),
            jax.ShapeDtypeStruct((CT, QW), BF16),
            jax.ShapeDtypeStruct((2 * CT, COLS), BF16),
        ),
        in_specs=[ANY] * 4,
        out_specs=(ANY,) * 5,
        scratch_shapes=[
            pltpu.VMEM((SHARDS, ROWS, COLS), BF16),
            pltpu.VMEM((CT, D), BF16),
            pltpu.VMEM((D, CT), BF16),
            pltpu.VMEM((ROWS, COLS), F32),
            pltpu.VMEM((CT, COLS), BF16),
            pltpu.VMEM((CT, COLS), F32),
            pltpu.SemaphoreType.DMA((N_GATHER_SEMS,)),
            pltpu.SemaphoreType.DMA((N_GATHER_SEMS,)),
            pltpu.SemaphoreType.DMA((N_LOCAL_SEMS,)),
        ],
        compiler_params=pltpu.CompilerParams(
            collective_id=0, has_side_effects=True, vmem_limit_bytes=VMEM_LIMIT
        ),
        name="gather_project",
    )(normed, queries, out_grad, master)


def attention_kernel(
    lengths, q_ref, do_ref, kv_ref, dq_ref, dkv_ref,
    qs, dos, prob, dprob, dq_t, dk_acc, dv_acc,
):
    zl = lax.div(lax.axis_index("seq"), 2)
    first_abs = zl * CT
    scale = HEAD ** (-0.5)
    to_base2 = scale * math.log2(math.e)
    ends = []
    total = lengths[0, 0]
    ends.append(total)
    for j in range(1, lengths.shape[1]):
        total = total + lengths[0, j]
        ends.append(total)
    dk_acc[...] = jnp.zeros_like(dk_acc)
    dv_acc[...] = jnp.zeros_like(dv_acc)
    lane = lax.broadcasted_iota(jnp.int32, (1, LANES), 1)
    lane_tok = lax.rem(lane, CHUNK)
    sub = lax.broadcasted_iota(jnp.int32, (CHUNK, 1), 0)

    @pl.loop(0, CT // CHUNK)
    def _(i):
        q_abs = first_abs + i * CHUNK + lane_tok
        doc_start = jnp.zeros_like(q_abs)
        first_q = first_abs + i * CHUNK
        first_start = jnp.int32(0)
        for e in ends:
            doc_start = jnp.where(q_abs >= e, jnp.maximum(doc_start, e), doc_start)
            first_start = jnp.where(first_q >= e, jnp.maximum(first_start, e), first_start)
        shift = CT - first_abs
        doc_start = doc_start + shift
        q_row = q_abs + shift
        last = CT // CHUNK + i
        lowest = lax.div(first_start + shift, CHUNK)
        lowest = jnp.maximum(lowest, last - (N_CHUNKS - 1))
        rows = pl.ds(pl.multiple_of(i * CHUNK, CHUNK), CHUNK)
        for a in range(GROUP):
            qs[a * CHUNK : (a + 1) * CHUNK, :] = q_ref[rows, a * HEAD : (a + 1) * HEAD]
            dos[a * CHUNK : (a + 1) * CHUNK, :] = do_ref[rows, a * HEAD : (a + 1) * HEAD]
        dq_t[...] = jnp.zeros_like(dq_t)

        def scores(j, top):
            at = pl.ds(pl.multiple_of(j * CHUNK, CHUNK), CHUNK)
            s = dot(kv_ref[at, 0:HEAD], qs[...], ((1,), (1,)))
            k_row = j * CHUNK + sub
            s = jnp.where((k_row >= doc_start) & (k_row <= q_row), s, -1e30)
            prob[j - lowest] = s
            return jnp.maximum(top, jnp.max(s, axis=0, keepdims=True))

        top = lax.fori_loop(lowest, last + 1, scores, jnp.full((1, LANES), -3e38, F32))

        def weigh(j, sums):
            mass, delta = sums
            at = pl.ds(pl.multiple_of(j * CHUNK, CHUNK), CHUNK)
            p = jnp.exp2((prob[j - lowest] - top) * to_base2)
            dp = dot(kv_ref[at, HEAD : 2 * HEAD], dos[...], ((1,), (1,)))
            prob[j - lowest] = p
            dprob[j - lowest] = dp
            mass = mass + jnp.sum(p, axis=0, keepdims=True)
            delta = delta + jnp.sum(p * dp, axis=0, keepdims=True)
            return mass, delta

        zero = jnp.zeros((1, LANES), F32)
        mass, delta = lax.fori_loop(lowest, last + 1, weigh, (zero, zero))
        inv = 1.0 / mass
        delta = delta * inv

        def back(j, carry):
            at = pl.ds(pl.multiple_of(j * CHUNK, CHUNK), CHUNK)
            p = prob[j - lowest] * inv
            ds = (p * (dprob[j - lowest] - delta)).astype(BF16)
            dv_acc[at, :] += dot(p.astype(BF16), dos[...])
            dk_acc[at, :] += dot(ds, qs[...])
            dq_t[...] += dot(kv_ref[at, 0:HEAD], ds, ((0,), (0,)))
            return carry

        lax.fori_loop(lowest, last + 1, back, 0)
        for a in range(GROUP):
            part = dq_t[:, a * CHUNK : (a + 1) * CHUNK].T * scale
            dq_ref[rows, a * HEAD : (a + 1) * HEAD] = part.astype(BF16)

    dkv_ref[:, 0:HEAD] = (dk_acc[...] * scale).astype(BF16)
    dkv_ref[:, HEAD : 2 * HEAD] = dv_acc[...].astype(BF16)


def attention(lengths, q, do, kv):
    heads = COLS // (2 * HEAD)
    width = GROUP * HEAD
    return pl.pallas_call(
        attention_kernel,
        grid=(heads,),
        out_shape=(
            jax.ShapeDtypeStruct((CT, QW), BF16),
            jax.ShapeDtypeStruct((2 * CT, COLS), BF16),
        ),
        in_specs=[
            pl.BlockSpec(memory_space=pltpu.SMEM),
            pl.BlockSpec((CT, width), lambda g: (0, g)),
            pl.BlockSpec((CT, width), lambda g: (0, g)),
            pl.BlockSpec((2 * CT, 2 * HEAD), lambda g: (0, g)),
        ],
        out_specs=(
            pl.BlockSpec((CT, width), lambda g: (0, g)),
            pl.BlockSpec((2 * CT, 2 * HEAD), lambda g: (0, g)),
        ),
        scratch_shapes=[
            pltpu.VMEM((LANES, HEAD), BF16),
            pltpu.VMEM((LANES, HEAD), BF16),
            pltpu.VMEM((N_CHUNKS, CHUNK, LANES), F32),
            pltpu.VMEM((N_CHUNKS, CHUNK, LANES), F32),
            pltpu.VMEM((HEAD, LANES), F32),
            pltpu.VMEM((2 * CT, HEAD), F32),
            pltpu.VMEM((2 * CT, HEAD), F32),
        ],
        compiler_params=pltpu.CompilerParams(vmem_limit_bytes=VMEM_LIMIT),
        name="attention_back",
    )(lengths, q, do, kv)


N_REDUCE_SEMS = 96


def reduce_kernel(
    xt_in, w_in, dkv_in, dq_in, master, moment_one, moment_two,
    dq_out, dn_out, master_out, one_out, two_out,
    xt, w, term, dkv, dkv_far,
    opp_a, low_a, high_a, opp_b, low_b, high_b,
    opp2_a, low2_a, high2_a, opp2_b, low2_b, high2_b,
    z_in, l_in, mine, total, dn_send, dn_recv, dn_own,
    mas, one, two, send_sem, recv_sem, loc_sem,
):
    here = Place()
    links = Links(send_sem, recv_sem, here)
    n_local = [0]

    def local(src, dst):
        copy = pltpu.make_async_copy(src, dst, loc_sem.at[n_local[0]])
        n_local[0] += 1
        copy.start()
        return copy

    core = here.core
    own_rows = pl.ds(pl.multiple_of(core * TOK, TOK), TOK)
    far_rows = pl.ds(pl.multiple_of((1 - core) * TOK, TOK), TOK)
    own_q = pl.ds(pl.multiple_of(core * QW, QW), QW)
    get_dkv = local(dkv_in.at[pl.ds(CT, CT), :], dkv)
    get_xt = local(xt_in, xt)
    here.greet()

    @pl.when(here.zl == 1)
    def _():
        pltpu.make_async_remote_copy(
            src_ref=dkv_in.at[pl.ds(0, CT), :],
            dst_ref=dkv_far,
            send_sem=send_sem.at[N_REDUCE_SEMS - 1],
            recv_sem=recv_sem.at[N_REDUCE_SEMS - 1],
            device_id=here.partner(),
            device_id_type=MESH,
        ).start()

    get_w = local(w_in, w)
    pending = [local(dq_in.at[own_rows, :], dq_out.at[:, own_q])]
    links.send("dq", dq_in.at[far_rows, :], dq_out.at[:, own_q], here.other_core())
    get_master = local(master, mas)
    get_one = local(moment_one, one)
    get_two = local(moment_two, two)
    get_dkv.wait()

    @pl.when(here.zl == 0)
    def _():
        pltpu.make_async_remote_copy(
            src_ref=dkv_far,
            dst_ref=dkv_far,
            send_sem=send_sem.at[N_REDUCE_SEMS - 1],
            recv_sem=recv_sem.at[N_REDUCE_SEMS - 1],
            device_id=here.partner(),
            device_id_type=MESH,
        ).wait_recv()
        dkv[...] = (dkv[...].astype(F32) + dkv_far[...].astype(F32)).astype(BF16)

    get_xt.wait()

    pos = {"x": here.x, "y": here.y}
    size = {"x": X, "y": Y}
    axes = (("x", "y"), ("y", "x"))

    def at_axis(axis, off):
        return lax.rem(pos[axis] + off + size[axis], size[axis])

    class Ring:
        def __init__(self, name, axis, slot, opp, low, high):
            self.name, self.axis, self.slot = name, axis, slot
            self.opp, self.low, self.high = opp, low, high

        def half(self, ref, h):
            return ref.at[:, :, pl.ds(h * HC, HC)]

        def send_far(self):
            for h, step in ((0, 1), (1, -1)):
                links.send(
                    (self.name, "far", step),
                    self.half(self.slot(2), h), self.opp(h), here.along(self.axis, step),
                )

        def send_near(self, step):
            h, land = (1, self.low) if step == 1 else (0, self.high)
            links.send(
                (self.name, "near", step),
                self.half(self.slot(step), h), self.half(land(), h), here.along(self.axis, step),
            )

        def forward(self):
            for h, step in ((0, 1), (1, -1)):
                links.recv((self.name, "far", step), self.opp(h))
                here_sum = self.half(self.slot(step), h)
                here_sum[...] = (
                    here_sum[...].astype(F32) + self.opp(h)[...].astype(F32)
                ).astype(BF16)
                land = self.low if step == 1 else self.high
                links.send(
                    (self.name, "sum", step),
                    here_sum, self.half(land(), h), here.along(self.axis, step),
                )

        def finish(self):
            for h, step in ((1, 1), (0, -1)):
                land = self.low if step == 1 else self.high
                links.recv((self.name, "near", step), self.half(land(), h))
                links.recv((self.name, "sum", step), self.half(land(), 1 - h))
            mine_ref = self.slot(0)
            mine_ref[...] = (
                mine_ref[...].astype(F32)
                + self.low()[...].astype(F32)
                + self.high()[...].astype(F32)
            ).astype(BF16)

    def rows_of(p):
        return pl.ds(p * HR, HR)

    def term_at(y, x, p):
        return term.at[y, :, x, rows_of(p), :]

    def first_ring(p, k, off):
        a, b = axes[p]
        opp, low, high = ((opp_a, low_a, high_a), (opp_b, low_b, high_b))[p]

        def slot(da):
            at = {a: at_axis(a, da), b: at_axis(b, off)}
            return term_at(at["y"], at["x"], p)

        return Ring(("first", p, k), a, slot, lambda h: opp.at[k, h], lambda: low.at[k], lambda: high.at[k])

    def second_ring(p):
        a, b = axes[p]
        opp, low, high = ((opp2_a, low2_a, high2_a), (opp2_b, low2_b, high2_b))[p]

        def slot(db):
            at = {a: pos[a], b: at_axis(b, db)}
            return term_at(at["y"], at["x"], p)

        return Ring(("second", p), b, slot, lambda h: opp.at[h], lambda: low, lambda: high)

    offs = (2, 1, -1, 0)
    rings = [[first_ring(p, k, off) for k, off in enumerate(offs)] for p in range(2)]
    finals = [second_ring(p) for p in range(2)]

    def make_terms(off):
        y = at_axis("y", off)
        for z in range(ZH):
            at = pl.ds(pl.multiple_of((y * ZH + z) * ROW_BLOCK, 128), ROW_BLOCK)
            t = dot(xt[at, :], dkv[...]).astype(BF16)
            term[y, z] = t.reshape(X, ROWS, COLS)

    def dn_far(t):
        at = pl.ds(t * ROW_BLOCK, ROW_BLOCK)
        w_t = w[pl.ds(t * X, X)].reshape(ROW_BLOCK, COLS)
        dn_send[:, at] = dot(dkv[far_rows, :], w_t, ((1,), (1,))).astype(BF16)
        links.send(("dn", t), dn_send.at[:, at], dn_recv.at[:, at], here.other_core())

    def dn_near(t):
        at = pl.ds(t * ROW_BLOCK, ROW_BLOCK)
        w_t = w[pl.ds(t * X, X)].reshape(ROW_BLOCK, COLS)
        near = dot(dkv[own_rows, :], w_t, ((1,), (1,)))
        links.recv(("dn", t), dn_recv.at[:, at])
        dn_own[:, at] = (near + dn_recv[:, at].astype(F32)).astype(BF16)
        pending.append(local(dn_own.at[:, at], dn_out.at[:, at]))

    make_terms(2)
    rings[0][0].send_far()
    for k in range(4):
        rings[1][k].send_far()
    for step in (1, -1):
        rings[0][0].send_near(step)
    make_terms(1)
    rings[0][1].send_far()
    for k in range(4):
        rings[1][k].send_near(1)
    make_terms(-1)
    rings[0][2].send_far()
    for k in range(4):
        rings[1][k].send_near(-1)
    make_terms(0)
    rings[0][3].send_far()
    for k in range(1, 4):
        for step in (1, -1):
            rings[0][k].send_near(step)
    get_w.wait()
    for k in range(4):
        for p in range(2):
            rings[p][k].forward()
        dn_far(2 * k)
        dn_far(2 * k + 1)
    for k in range(4):
        for p in range(2):
            rings[p][k].finish()
            if k == 0:
                finals[p].send_far()
            elif k == 1:
                finals[p].send_near(1)
            elif k == 2:
                finals[p].send_near(-1)
        dn_near(2 * k)
        dn_near(2 * k + 1)
    for p in range(2):
        finals[p].forward()

    own_z = here.zh
    far_z = 1 - here.zh
    for p in range(2):
        finals[p].finish()
        links.send(
            ("z", p),
            term.at[here.y, far_z, here.x, rows_of(p), :], z_in.at[rows_of(p), :], here.cross(),
        )
    for p in range(2):
        rows = rows_of(p)
        links.recv(("z", p), z_in.at[rows, :])
        mine[rows, :] = (
            term[here.y, own_z, here.x, rows, :].astype(F32) + z_in[rows, :].astype(F32)
        ).astype(BF16)
        links.send(("l", p), mine.at[rows, :], l_in.at[rows, :], here.partner())
    for p in range(2):
        rows = rows_of(p)
        links.recv(("l", p), l_in.at[rows, :])
        total[core, rows, :] = mine[rows, :].astype(F32) + l_in[rows, :].astype(F32)
        links.send(
            ("c", p), total.at[core, rows, :], total.at[core, rows, :], here.other_core()
        )
    for p in range(2):
        links.recv(("c", p), total.at[1 - core, rows_of(p), :])
    get_master.wait()
    get_one.wait()
    get_two.wait()
    tokens = TOK * lax.axis_size("dp") * lax.axis_size("seq")
    for h in range(2):
        cols = pl.ds(h * COLS, COLS)
        grad = total[h] * float(tokens) ** (-0.5)
        first = 0.9 * one[:, cols].astype(F32) + 0.1 * grad
        second = 0.999 * two[:, cols].astype(F32) + 0.001 * grad * grad
        mas[:, cols] = mas[:, cols] - 0.001 * (first / (1.0 - 0.9**3)) / (
            jnp.sqrt(second / (1.0 - 0.999**3)) + 1e-08
        )
        one[:, cols] = first.astype(BF16)
        two[:, cols] = second.astype(BF16)
    pending.append(local(mas, master_out))
    pending.append(local(one, one_out))
    pending.append(local(two, two_out))
    links.recv("dq", dq_out.at[:, pl.ds(pl.multiple_of((1 - core) * QW, QW), QW)])
    for copy in pending:
        copy.wait()
    links.drain()

    @pl.when(here.zl == 1)
    def _():
        pltpu.make_async_remote_copy(
            src_ref=dkv_in.at[pl.ds(0, CT), :],
            dst_ref=dkv_far,
            send_sem=send_sem.at[N_REDUCE_SEMS - 1],
            recv_sem=recv_sem.at[N_REDUCE_SEMS - 1],
            device_id=here.partner(),
            device_id_type=MESH,
        ).wait_send()


def reduce_update(xt, w, dkv, dq, master, moment_one, moment_two):
    ring4 = [
        pltpu.VMEM((4, 2, ZH, HR, HC), BF16),
        pltpu.VMEM((4, ZH, HR, COLS), BF16),
        pltpu.VMEM((4, ZH, HR, COLS), BF16),
    ]
    ring1 = [
        pltpu.VMEM((2, ZH, HR, HC), BF16),
        pltpu.VMEM((ZH, HR, COLS), BF16),
        pltpu.VMEM((ZH, HR, COLS), BF16),
    ]
    width = master.shape[1]
    return pl.pallas_call(
        reduce_kernel,
        out_shape=(
            jax.ShapeDtypeStruct((TOK, 2 * QW), BF16),
            jax.ShapeDtypeStruct((TOK, D), BF16),
            jax.ShapeDtypeStruct((ROWS, width), F32),
            jax.ShapeDtypeStruct((ROWS, width), BF16),
            jax.ShapeDtypeStruct((ROWS, width), BF16),
        ),
        in_specs=[ANY] * 7,
        out_specs=(ANY,) * 5,
        scratch_shapes=[
            pltpu.VMEM((D, CT), BF16),
            pltpu.VMEM((SHARDS, ROWS, COLS), BF16),
            pltpu.VMEM((Y, ZH, X, ROWS, COLS), BF16),
            pltpu.VMEM((CT, COLS), BF16),
            pltpu.VMEM((CT, COLS), BF16),
            *ring4, *ring4, *ring1, *ring1,
            pltpu.VMEM((ROWS, COLS), BF16),
            pltpu.VMEM((ROWS, COLS), BF16),
            pltpu.VMEM((ROWS, COLS), BF16),
            pltpu.VMEM((2, ROWS, COLS), F32),
            pltpu.VMEM((TOK, D), BF16),
            pltpu.VMEM((TOK, D), BF16),
            pltpu.VMEM((TOK, D), BF16),
            pltpu.VMEM((ROWS, width), F32),
            pltpu.VMEM((ROWS, width), BF16),
            pltpu.VMEM((ROWS, width), BF16),
            pltpu.SemaphoreType.DMA((N_REDUCE_SEMS,)),
            pltpu.SemaphoreType.DMA((N_REDUCE_SEMS,)),
            pltpu.SemaphoreType.DMA((N_LOCAL_SEMS,)),
        ],
        compiler_params=pltpu.CompilerParams(
            collective_id=1, has_side_effects=True, vmem_limit_bytes=VMEM_LIMIT
        ),
        name="reduce_update",
    )(xt, w, dkv, dq, master, moment_one, moment_two)


def on_device(normed, queries, output_gradient, doc_lengths, master, moment_one, moment_two):
    w, xt, q, do, kv = gather(normed, queries, output_gradient, master)
    dq, dkv = attention(doc_lengths, q, do, kv)
    return reduce_update(xt, w, dkv, dq, master, moment_one, moment_two)


def solution(mesh):
    rows = P(("dp", "seq"), None)
    shard = P("dp", None)
    return jax.shard_map(
        on_device,
        mesh=mesh,
        in_specs=(rows, rows, rows, shard, shard, shard, shard),
        out_specs=(rows, rows, shard, shard, shard),
        check_vma=False,
    )
```

```python
import functools
import math

import jax
import jax.numpy as jnp
from jax import lax
from jax.experimental import pallas as pl
from jax.experimental.pallas import tpu as pltpu
from jax.sharding import PartitionSpec as P

HEAD = 128
GROUP = 7
X, Y, ZH = 4, 4, 2
TOK = 256
CT = 512
D = 7168
SHARDS = X * Y * ZH
ROWS = D // SHARDS
PARTS = (
    (0, 80, ("x", "y"), True),
    (80, 64, ("y", "x"), True),
    (144, 32, ("x", "y"), False),
    (176, 48, ("y", "x"), False),
)
Z_FIRST = (0, 1)
Z_LAST = (2, 3)
SEQ = 1024
COLS = 512
HC = COLS // 2
QW = 896
ROW_BLOCK = X * ROWS
N_BLOCKS = Y * ZH
CHUNK = 128
N_CHUNKS = 5
LANES = GROUP * CHUNK
VMEM_LIMIT = 58 * 1024 * 1024
MESH = pl.DeviceIdType.MESH
ANY = pl.BlockSpec(memory_space=pl.ANY)
F32 = jnp.float32
BF16 = jnp.bfloat16


def dot(a, b, dims=((1,), (0,))):
    return lax.dot_general(a, b, (dims, ((), ())), preferred_element_type=F32)


class Place:
    def __init__(self):
        dp = lax.axis_index("dp")
        sq = lax.axis_index("seq")
        self.dp, self.sq = dp, sq
        self.x = lax.rem(dp, X)
        self.zh = lax.rem(lax.div(dp, X), ZH)
        self.y = lax.div(dp, X * ZH)
        self.core = lax.rem(sq, 2)
        self.zl = lax.div(sq, 2)

    def dev(self, x=None, y=None, zh=None, zl=None, core=None):
        x = self.x if x is None else x
        y = self.y if y is None else y
        zh = self.zh if zh is None else zh
        zl = self.zl if zl is None else zl
        core = self.core if core is None else core
        return ((y * ZH + zh) * X + x, zl * 2 + core)

    def along(self, axis, step):
        if axis == "x":
            return self.dev(x=lax.rem(self.x + step + X, X))
        return self.dev(y=lax.rem(self.y + step + Y, Y))

    def cross(self):
        return self.dev(zh=1 - self.zh, zl=1 - self.zl)

    def partner(self):
        return self.dev(zl=1 - self.zl)

    def other_core(self):
        return self.dev(core=1 - self.core)

    def greet(self):
        barrier = pltpu.get_barrier_semaphore()
        near = [self.along(a, s) for a in ("x", "y") for s in (1, -1)]
        near += [self.cross(), self.partner(), self.other_core()]
        near.append(self.dev(zl=1 - self.zl, core=1 - self.core))
        for d in near:
            pl.semaphore_signal(barrier, inc=1, device_id=d, device_id_type=MESH)
        pl.semaphore_wait(barrier, len(near))


class Links:
    def __init__(self, send_sem, recv_sem, place):
        self.send_sem, self.recv_sem, self.place = send_sem, recv_sem, place
        self.index = {}
        self.sent = []

    def _copy(self, key, src, dst, dev):
        k = self.index.setdefault(key, len(self.index))
        return pltpu.make_async_remote_copy(
            src_ref=src,
            dst_ref=dst,
            send_sem=self.send_sem.at[k],
            recv_sem=self.recv_sem.at[k],
            device_id=dev,
            device_id_type=MESH,
        )

    def send(self, key, src, dst, dev):
        copy = self._copy(key, src, dst, dev)
        copy.start()
        self.sent.append(copy)

    def recv(self, key, dst):
        self._copy(key, dst, dst, self.place.other_core()).wait_recv()

    def drain(self):
        for copy in self.sent:
            copy.wait_send()


N_GATHER_SEMS = 176
N_LOCAL_SEMS = 40


def gather_kernel(
    normed, queries, out_grad, master,
    w_out, xt_out, q_out, do_out, kv_out,
    w, xs, xt, mas, kv, acc, q_src, do_src, q_all, do_all, send_sem, recv_sem, loc_sem,
):
    here = Place()
    links = Links(send_sem, recv_sem, here)
    n_local = [0]

    def local(src, dst):
        copy = pltpu.make_async_copy(src, dst, loc_sem.at[n_local[0]])
        n_local[0] += 1
        copy.start()
        return copy

    core, zl = here.core, here.zl
    own_rows = pl.ds(pl.multiple_of(core * TOK, TOK), TOK)
    far_rows = pl.ds(pl.multiple_of((1 - core) * TOK, TOK), TOK)

    def seq_rows(sq):
        return pl.ds(pl.multiple_of(sq * TOK, TOK), TOK)

    def head_cols(zl_to, core_to):
        return pl.ds(pl.multiple_of((core_to * 2 + zl_to) * QW, 128), QW)

    get_master = local(master.at[:, pl.ds(pl.multiple_of(core * COLS, COLS), COLS)], mas)
    get_q = local(queries, q_src)
    get_do = local(out_grad, do_src)
    own_normed = local(normed, xs.at[own_rows, :])
    own_q = local(queries.at[:, head_cols(zl, core)], q_all.at[seq_rows(here.sq), :])
    own_do = local(out_grad.at[:, head_cols(zl, core)], do_all.at[seq_rows(here.sq), :])
    pending = []
    here.greet()
    get_master.wait()

    pos = {"x": here.x, "y": here.y}
    size = {"x": X, "y": Y}

    def at_axis(axis, off):
        return lax.rem(pos[axis] + off + size[axis], size[axis])

    def slot(p, da, db, zr, half=None):
        row, rows, axes, _ = PARTS[p]
        at = {axes[0]: at_axis(axes[0], da), axes[1]: at_axis(axes[1], db)}
        zh = here.zh if zr == 0 else 1 - here.zh
        s = (at["y"] * ZH + zh) * X + at["x"]
        cols = pl.ds(0, COLS) if half is None else pl.ds(half * HC, HC)
        return w.at[s, pl.ds(row, rows), cols]

    own = (here.y * ZH + here.zh) * X + here.x
    w[own] = mas[...].astype(BF16)

    def send(key, ref, dev):
        links.send(key, ref, ref, dev)

    def second_from(p, da, zr):
        b = PARTS[p][2][1]
        for step in (1, -1):
            send(("b", p, zr, da, step, 0), slot(p, da, 0, zr), here.along(b, step))

    def start(parts, zr):
        for p in parts:
            a = PARTS[p][2][0]
            for step in (1, -1):
                send(("a", p, zr, step, 0), slot(p, 0, 0, zr), here.along(a, step))
        for p in parts:
            second_from(p, 0, zr)

    def over_z(p, da, db):
        if p in Z_LAST:
            send(("z", p, da, db), slot(p, da, db, 0), here.cross())

    def forward_first(parts, zr):
        for p in parts:
            a = PARTS[p][2][0]
            for step in (1, -1):
                links.recv(("a", p, zr, step, 0), slot(p, -step, 0, zr))
                half = 0 if step == 1 else 1
                send(("a", p, zr, step, 1), slot(p, -step, 0, zr, half), here.along(a, step))
            for step in (1, -1):
                second_from(p, -step, zr)
                over_z(p, -step, 0)

    def finish_first(parts, zr):
        for p in parts:
            for step in (1, -1):
                half = 0 if step == 1 else 1
                links.recv(("a", p, zr, step, 1), slot(p, 2, 0, zr, half))
            second_from(p, 2, zr)
            over_z(p, 2, 0)

    def forward_second(parts, zr):
        for da in (0, -1, 1, 2):
            for p in parts:
                b = PARTS[p][2][1]
                for step in (1, -1):
                    links.recv(("b", p, zr, da, step, 0), slot(p, da, -step, zr))
                    half = 0 if step == 1 else 1
                    send(
                        ("b", p, zr, da, step, 1),
                        slot(p, da, -step, zr, half),
                        here.along(b, step),
                    )
                    over_z(p, da, -step)

    def finish_second(parts, zr):
        for da in (0, -1, 1, 2):
            for p in parts:
                for step in (1, -1):
                    half = 0 if step == 1 else 1
                    links.recv(("b", p, zr, da, step, 1), slot(p, da, 2, zr, half))
                over_z(p, da, 2)

    def turn(first, last):
        @pl.loop(first, last)
        def _(b):
            at = pl.ds(pl.multiple_of(b * HEAD, HEAD), HEAD)
            xt[at, :] = xs[:, at].T

    start(Z_LAST, 0)
    start(Z_FIRST, 0)
    for p in Z_FIRST:
        send(("z", p), slot(p, 0, 0, 0), here.cross())
    for p in Z_LAST:
        over_z(p, 0, 0)
    links.send("normed", normed, xs.at[own_rows, :], here.other_core())
    get_q.wait()
    get_do.wait()
    others = (("p", 1 - zl, core), ("c", zl, 1 - core), ("d", 1 - zl, 1 - core))
    for name, src, dst in (("q", q_src, q_all), ("do", do_src, do_all)):
        for way, zl_to, core_to in others:
            links.send(
                (name, way),
                src.at[:, head_cols(zl_to, core_to)], dst.at[seq_rows(here.sq), :],
                here.dev(zl=zl_to, core=core_to),
            )
    forward_first(Z_LAST, 0)
    forward_first(Z_FIRST, 0)
    finish_first(Z_LAST, 0)
    for p in Z_FIRST:
        links.recv(("z", p), slot(p, 0, 0, 1))
    start(Z_FIRST, 1)
    finish_first(Z_FIRST, 0)
    own_normed.wait()
    links.recv("normed", xs.at[far_rows, :])
    turn(0, 14)
    forward_second(Z_LAST, 0)
    forward_first(Z_FIRST, 1)
    turn(14, 28)
    finish_second(Z_LAST, 0)
    finish_first(Z_FIRST, 1)
    turn(28, 42)
    forward_second(Z_FIRST, 0)
    turn(42, 56)
    pending.append(local(xt, xt_out))
    forward_second(Z_FIRST, 1)
    finish_second(Z_FIRST, 0)
    finish_second(Z_FIRST, 1)
    for p in Z_LAST:
        for da in (0, -1, 1, 2):
            for db in (0, -1, 1, 2):
                links.recv(("z", p, da, db), slot(p, da, db, 1))
    pending.append(local(w, w_out))

    own_tokens = pl.ds(pl.multiple_of(zl * CT, CT), CT)
    for far in (True, False):
        head = 1 - zl if far else zl
        cols = pl.ds(pl.multiple_of(head * HC, HC), HC)
        acc[...] = jnp.zeros_like(acc)

        @pl.loop(0, N_BLOCKS)
        def _(t):
            at = pl.ds(pl.multiple_of(t * ROW_BLOCK, 128), ROW_BLOCK)
            w_t = w[pl.ds(t * X, X), :, cols].reshape(ROW_BLOCK, HC)
            acc[...] += dot(xs[:, at], w_t)

        if far:
            kv[0] = acc[...].astype(BF16)
            links.send("kv", kv.at[0], kv_out.at[own_tokens, :], here.partner())
        else:
            kv[1] = acc[...].astype(BF16)
            pending.append(local(kv.at[1], kv_out.at[own_tokens, :]))
    own_q.wait()
    own_do.wait()
    for name, dst in (("q", q_all), ("do", do_all)):
        for way, zl_to, core_to in others:
            links.recv((name, way), dst.at[seq_rows(zl_to * 2 + core_to), :])
    pending.append(local(q_all, q_out))
    pending.append(local(do_all, do_out))
    links.recv("kv", kv_out.at[pl.ds(pl.multiple_of((1 - zl) * CT, CT), CT), :])
    for copy in pending:
        copy.wait()
    links.drain()


def gather(normed, queries, out_grad, master):
    return pl.pallas_call(
        gather_kernel,
        out_shape=(
            jax.ShapeDtypeStruct((SHARDS, ROWS, COLS), BF16),
            jax.ShapeDtypeStruct((D, CT), BF16),
            jax.ShapeDtypeStruct((SEQ, QW), BF16),
            jax.ShapeDtypeStruct((SEQ, QW), BF16),
            jax.ShapeDtypeStruct((SEQ, HC), BF16),
        ),
        in_specs=[ANY] * 4,
        out_specs=(ANY,) * 5,
        scratch_shapes=[
            pltpu.VMEM((SHARDS, ROWS, COLS), BF16),
            pltpu.VMEM((CT, D), BF16),
            pltpu.VMEM((D, CT), BF16),
            pltpu.VMEM((ROWS, COLS), F32),
            pltpu.VMEM((2, CT, HC), BF16),
            pltpu.VMEM((CT, HC), F32),
            pltpu.VMEM(queries.shape, BF16),
            pltpu.VMEM(queries.shape, BF16),
            pltpu.VMEM((SEQ, QW), BF16),
            pltpu.VMEM((SEQ, QW), BF16),
            pltpu.SemaphoreType.DMA((N_GATHER_SEMS,)),
            pltpu.SemaphoreType.DMA((N_GATHER_SEMS,)),
            pltpu.SemaphoreType.DMA((N_LOCAL_SEMS,)),
        ],
        compiler_params=pltpu.CompilerParams(
            collective_id=0, has_side_effects=True, vmem_limit_bytes=VMEM_LIMIT
        ),
        name="gather_project",
    )(normed, queries, out_grad, master)


def attention_kernel(
    lengths, q_ref, do_ref, kv_ref, dq_ref, dkv_ref,
    qs, dos, prob, dprob, dq_t, dk_acc, dv_acc,
):
    i = pl.program_id(0)
    scale = HEAD ** (-0.5)
    to_base2 = scale * math.log2(math.e)
    ends = []
    total = lengths[0, 0]
    ends.append(total)
    for j in range(1, lengths.shape[1]):
        total = total + lengths[0, j]
        ends.append(total)

    @pl.when(i == 0)
    def _():
        dk_acc[...] = jnp.zeros_like(dk_acc)
        dv_acc[...] = jnp.zeros_like(dv_acc)

    lane = lax.broadcasted_iota(jnp.int32, (1, LANES), 1)
    sub = lax.broadcasted_iota(jnp.int32, (CHUNK, 1), 0)
    q_row = i * CHUNK + lax.rem(lane, CHUNK)
    doc_start = jnp.zeros_like(q_row)
    first_start = jnp.int32(0)
    for e in ends:
        doc_start = jnp.where(q_row >= e, jnp.maximum(doc_start, e), doc_start)
        first_start = jnp.where(i * CHUNK >= e, jnp.maximum(first_start, e), first_start)
    lowest = lax.div(first_start, CHUNK)
    lowest = jnp.maximum(lowest, i - (N_CHUNKS - 1))
    for a in range(GROUP):
        qs[a * CHUNK : (a + 1) * CHUNK, :] = q_ref[:, a * HEAD : (a + 1) * HEAD]
        dos[a * CHUNK : (a + 1) * CHUNK, :] = do_ref[:, a * HEAD : (a + 1) * HEAD]
    dq_t[...] = jnp.zeros_like(dq_t)

    def scores(j, top):
        at = pl.ds(pl.multiple_of(j * CHUNK, CHUNK), CHUNK)
        s = dot(kv_ref[at, 0:HEAD], qs[...], ((1,), (1,)))
        k_row = j * CHUNK + sub
        s = jnp.where((k_row >= doc_start) & (k_row <= q_row), s, -1e30)
        prob[j - lowest] = s
        return jnp.maximum(top, jnp.max(s, axis=0, keepdims=True))

    top = lax.fori_loop(lowest, i + 1, scores, jnp.full((1, LANES), -3e38, F32))

    def weigh(j, sums):
        mass, delta = sums
        at = pl.ds(pl.multiple_of(j * CHUNK, CHUNK), CHUNK)
        p = jnp.exp2((prob[j - lowest] - top) * to_base2)
        dp = dot(kv_ref[at, HEAD : 2 * HEAD], dos[...], ((1,), (1,)))
        prob[j - lowest] = p
        dprob[j - lowest] = dp
        mass = mass + jnp.sum(p, axis=0, keepdims=True)
        delta = delta + jnp.sum(p * dp, axis=0, keepdims=True)
        return mass, delta

    zero = jnp.zeros((1, LANES), F32)
    mass, delta = lax.fori_loop(lowest, i + 1, weigh, (zero, zero))
    inv = 1.0 / mass
    delta = delta * inv

    def back(j, carry):
        at = pl.ds(pl.multiple_of(j * CHUNK, CHUNK), CHUNK)
        p = prob[j - lowest] * inv
        ds = (p * (dprob[j - lowest] - delta)).astype(BF16)
        dv_acc[at, :] += dot(p.astype(BF16), dos[...])
        dk_acc[at, :] += dot(ds, qs[...])
        dq_t[...] += dot(kv_ref[at, 0:HEAD], ds, ((0,), (0,)))
        return carry

    lax.fori_loop(lowest, i + 1, back, 0)
    for a in range(GROUP):
        part = dq_t[:, a * CHUNK : (a + 1) * CHUNK].T * scale
        dq_ref[:, a * HEAD : (a + 1) * HEAD] = part.astype(BF16)

    @pl.when(i == pl.num_programs(0) - 1)
    def _():
        dkv_ref[:, 0:HEAD] = (dk_acc[...] * scale).astype(BF16)
        dkv_ref[:, HEAD : 2 * HEAD] = dv_acc[...].astype(BF16)


def attention(lengths, q, do, kv):
    return pl.pallas_call(
        attention_kernel,
        grid=(SEQ // CHUNK,),
        out_shape=(
            jax.ShapeDtypeStruct((SEQ, QW), BF16),
            jax.ShapeDtypeStruct((SEQ, HC), BF16),
        ),
        in_specs=[
            pl.BlockSpec(memory_space=pltpu.SMEM),
            pl.BlockSpec((CHUNK, QW), lambda i: (i, 0)),
            pl.BlockSpec((CHUNK, QW), lambda i: (i, 0)),
            pl.BlockSpec((SEQ, HC), lambda i: (0, 0)),
        ],
        out_specs=(
            pl.BlockSpec((CHUNK, QW), lambda i: (i, 0)),
            pl.BlockSpec((SEQ, HC), lambda i: (0, 0)),
        ),
        scratch_shapes=[
            pltpu.VMEM((LANES, HEAD), BF16),
            pltpu.VMEM((LANES, HEAD), BF16),
            pltpu.VMEM((N_CHUNKS, CHUNK, LANES), F32),
            pltpu.VMEM((N_CHUNKS, CHUNK, LANES), F32),
            pltpu.VMEM((HEAD, LANES), F32),
            pltpu.VMEM((SEQ, HEAD), F32),
            pltpu.VMEM((SEQ, HEAD), F32),
        ],
        compiler_params=pltpu.CompilerParams(vmem_limit_bytes=VMEM_LIMIT),
        name="attention_back",
    )(lengths, q, do, kv)


N_REDUCE_SEMS = 176


def reduce_kernel(
    xt_in, w_in, dkv_in, dq_in,
    dq_out, dn_out, grad_out,
    xt, w, term, dkv, dq_src, dq_all, z_early, z_in, l_in, mine, total, dn_send, dn_recv, dn_own,
    *rest,
):
    bufs = [rest[6 * p : 6 * p + 6] for p in range(4)]
    send_sem, recv_sem, loc_sem = rest[24:]
    here = Place()
    links = Links(send_sem, recv_sem, here)
    n_local = [0]

    def local(src, dst):
        copy = pltpu.make_async_copy(src, dst, loc_sem.at[n_local[0]])
        n_local[0] += 1
        copy.start()
        return copy

    core, zl = here.core, here.zl
    own_z, far_z = here.zh, 1 - here.zh
    own_rows = pl.ds(pl.multiple_of(core * TOK, TOK), TOK)
    far_rows = pl.ds(pl.multiple_of((1 - core) * TOK, TOK), TOK)
    own_tokens = pl.ds(pl.multiple_of(zl * CT, CT), CT)
    far_tokens = pl.ds(pl.multiple_of((1 - zl) * CT, CT), CT)

    def seq_rows(sq):
        return pl.ds(pl.multiple_of(sq * TOK, TOK), TOK)

    def head_cols(zl_of, core_of):
        return pl.ds(pl.multiple_of((core_of * 2 + zl_of) * QW, 128), QW)

    get_dkv = local(dkv_in.at[own_tokens, :], dkv.at[zl])
    get_xt = local(xt_in, xt)
    get_dq = local(dq_in, dq_src)
    own_dq = local(dq_in.at[seq_rows(here.sq), :], dq_all.at[:, head_cols(zl, core)])
    here.greet()
    links.send("dkv", dkv_in.at[far_tokens, :], dkv.at[zl], here.partner())
    get_w = local(w_in, w)
    pending = []
    get_dkv.wait()
    get_xt.wait()
    links.recv("dkv", dkv.at[1 - zl])

    pos = {"x": here.x, "y": here.y}
    size = {"x": X, "y": Y}

    def at_axis(axis, off):
        return lax.rem(pos[axis] + off + size[axis], size[axis])

    class Ring:
        def __init__(self, name, axis, slot, opp, low, high):
            self.name, self.axis, self.slot = name, axis, slot
            self.opp, self.low, self.high = opp, low, high

        def half(self, ref, h):
            return ref.at[:, :, pl.ds(h * HC, HC)]

        def send_far(self):
            for h, step in ((0, 1), (1, -1)):
                links.send(
                    (self.name, "far", step),
                    self.half(self.slot(2), h), self.opp(h), here.along(self.axis, step),
                )

        def send_near(self, step):
            h, land = (1, self.low) if step == 1 else (0, self.high)
            links.send(
                (self.name, "near", step),
                self.half(self.slot(step), h), self.half(land(), h), here.along(self.axis, step),
            )

        def forward(self):
            for h, step in ((0, 1), (1, -1)):
                links.recv((self.name, "far", step), self.opp(h))
                here_sum = self.half(self.slot(step), h)
                here_sum[...] = (
                    here_sum[...].astype(F32) + self.opp(h)[...].astype(F32)
                ).astype(BF16)
                land = self.low if step == 1 else self.high
                links.send(
                    (self.name, "sum", step),
                    here_sum, self.half(land(), h), here.along(self.axis, step),
                )

        def finish(self):
            for h, step in ((1, 1), (0, -1)):
                land = self.low if step == 1 else self.high
                links.recv((self.name, "near", step), self.half(land(), h))
                links.recv((self.name, "sum", step), self.half(land(), 1 - h))
            mine_ref = self.slot(0)
            mine_ref[...] = (
                mine_ref[...].astype(F32)
                + self.low()[...].astype(F32)
                + self.high()[...].astype(F32)
            ).astype(BF16)

    def rows_of(p):
        return pl.ds(PARTS[p][0], PARTS[p][1])

    def term_at(at, p):
        zs = pl.ds(0, ZH) if p in Z_FIRST else pl.ds(own_z, 1)
        return term.at[at["y"], zs, at["x"], rows_of(p), :]

    def first_ring(p, k, off):
        a, b = PARTS[p][2]
        opp, low, high = bufs[p][:3]

        def slot(da):
            return term_at({a: at_axis(a, da), b: at_axis(b, off)}, p)

        return Ring(
            ("first", p, k), a, slot,
            lambda h: opp.at[k, h], lambda: low.at[k], lambda: high.at[k],
        )

    def second_ring(p):
        a, b = PARTS[p][2]
        opp, low, high = bufs[p][3:]

        def slot(db):
            return term_at({a: pos[a], b: at_axis(b, db)}, p)

        return Ring(("second", p), b, slot, lambda h: opp.at[h], lambda: low, lambda: high)

    offs = (2, 1, -1, 0)
    rings = [[first_ring(p, k, off) for k, off in enumerate(offs)] for p in range(4)]
    finals = [second_ring(p) for p in range(4)]
    late = pl.ds(PARTS[2][0], PARTS[2][1] + PARTS[3][1])

    def make_terms(k):
        y = at_axis("y", offs[k])
        for z in (far_z, own_z):
            at = pl.ds(pl.multiple_of((y * ZH + z) * ROW_BLOCK, 128), ROW_BLOCK)
            for h in range(2):
                t = dot(xt[at, :], dkv[h]).astype(BF16)
                term[y, z, :, :, h * HC : (h + 1) * HC] = t.reshape(X, ROWS, HC)
        links.send(
            ("early", k), term.at[y, far_z, :, late, :], z_early.at[k], here.cross()
        )

    def add_early(k):
        y = at_axis("y", offs[k])
        links.recv(("early", k), z_early.at[k])
        into = term.at[y, own_z, :, late, :]
        into[...] = (into[...].astype(F32) + z_early[k].astype(F32)).astype(BF16)

    def launch(k, p_x, p_y):
        rings[p_x][k].send_far()
        for step in (1, -1):
            rings[p_x][k].send_near(step)
        for piece in rings[p_y]:
            if k == 0:
                piece.send_far()
            elif k < 3:
                piece.send_near(offs[k])

    def dn_far(t):
        at = pl.ds(t * ROW_BLOCK, ROW_BLOCK)
        partial = jnp.zeros((TOK, ROW_BLOCK), F32)
        for h in range(2):
            w_t = w[pl.ds(t * X, X), :, h * HC : (h + 1) * HC].reshape(ROW_BLOCK, HC)
            partial += dot(dkv[h, far_rows, :], w_t, ((1,), (1,)))
        dn_send[:, at] = partial.astype(BF16)
        links.send(("dn", t), dn_send.at[:, at], dn_recv.at[:, at], here.other_core())

    def dn_near(t):
        at = pl.ds(t * ROW_BLOCK, ROW_BLOCK)
        links.recv(("dn", t), dn_recv.at[:, at])
        partial = dn_recv[:, at].astype(F32)
        for h in range(2):
            w_t = w[pl.ds(t * X, X), :, h * HC : (h + 1) * HC].reshape(ROW_BLOCK, HC)
            partial += dot(dkv[h, own_rows, :], w_t, ((1,), (1,)))
        dn_own[:, at] = partial.astype(BF16)
        pending.append(local(dn_own.at[:, at], dn_out.at[:, at]))

    for k in range(4):
        make_terms(k)
        launch(k, 0, 1)
    get_dq.wait()
    others = (("p", 1 - zl, core), ("c", zl, 1 - core), ("d", 1 - zl, 1 - core))
    for way, zl_to, core_to in others:
        links.send(
            ("dq", way),
            dq_src.at[seq_rows(zl_to * 2 + core_to), :], dq_all.at[:, head_cols(zl, core)],
            here.dev(zl=zl_to, core=core_to),
        )
    get_w.wait()
    for k in range(4):
        for p in Z_FIRST:
            rings[p][k].forward()
        add_early(k)
        launch(k, 2, 3)
        dn_far(2 * k)
        dn_far(2 * k + 1)

    def end_first(k, parts):
        for p in parts:
            rings[p][k].finish()
            if k == 0:
                finals[p].send_far()
            elif k < 3:
                finals[p].send_near(offs[k])

    for k in range(4):
        for p in Z_LAST:
            rings[p][k].forward()
        end_first(k, Z_FIRST)
        dn_near(2 * k)
        dn_near(2 * k + 1)
    for p in Z_FIRST:
        finals[p].forward()
    for k in range(4):
        end_first(k, Z_LAST)
    for p in Z_FIRST:
        finals[p].finish()
        rows = rows_of(p)
        links.send(
            ("z", p), term.at[here.y, far_z, here.x, rows, :], z_in.at[rows, :], here.cross()
        )
    for p in Z_LAST:
        finals[p].forward()

    def to_partner(p):
        rows = rows_of(p)
        links.send(("l", p), mine.at[rows, :], l_in.at[rows, :], here.partner())

    for p in Z_FIRST:
        rows = rows_of(p)
        links.recv(("z", p), z_in.at[rows, :])
        mine[rows, :] = (
            term[here.y, own_z, here.x, rows, :].astype(F32) + z_in[rows, :].astype(F32)
        ).astype(BF16)
        to_partner(p)
    for p in Z_LAST:
        finals[p].finish()
        rows = rows_of(p)
        mine[rows, :] = term[here.y, own_z, here.x, rows, :]
        to_partner(p)
    for p in range(4):
        rows = rows_of(p)
        links.recv(("l", p), l_in.at[rows, :])
        total[core, rows, :] = mine[rows, :].astype(F32) + l_in[rows, :].astype(F32)
        links.send(
            ("c", p), total.at[core, rows, :], total.at[core, rows, :], here.other_core()
        )
    own_dq.wait()
    for way, zl_to, core_to in others:
        links.recv(("dq", way), dq_all.at[:, head_cols(zl_to, core_to)])
    pending.append(local(dq_all, dq_out))
    for p in range(4):
        links.recv(("c", p), total.at[1 - core, rows_of(p), :])
    pending.append(local(total, grad_out))
    for copy in pending:
        copy.wait()
    links.drain()


def reduce_terms(xt, w, dkv, dq):
    rings = []
    for p, (_, rows, _, both) in enumerate(PARTS):
        nz = ZH if both else 1
        rings += [
            pltpu.VMEM((4, 2, nz, rows, HC), BF16),
            pltpu.VMEM((4, nz, rows, COLS), BF16),
            pltpu.VMEM((4, nz, rows, COLS), BF16),
            pltpu.VMEM((2, nz, rows, HC), BF16),
            pltpu.VMEM((nz, rows, COLS), BF16),
            pltpu.VMEM((nz, rows, COLS), BF16),
        ]
    late = PARTS[2][1] + PARTS[3][1]
    return pl.pallas_call(
        reduce_kernel,
        out_shape=(
            jax.ShapeDtypeStruct((TOK, 4 * QW), BF16),
            jax.ShapeDtypeStruct((TOK, D), BF16),
            jax.ShapeDtypeStruct((2, ROWS, COLS), F32),
        ),
        in_specs=[ANY] * 4,
        out_specs=(ANY,) * 3,
        scratch_shapes=[
            pltpu.VMEM((D, CT), BF16),
            pltpu.VMEM((SHARDS, ROWS, COLS), BF16),
            pltpu.VMEM((Y, ZH, X, ROWS, COLS), BF16),
            pltpu.VMEM((2, CT, HC), BF16),
            pltpu.VMEM((SEQ, QW), BF16),
            pltpu.VMEM((TOK, 4 * QW), BF16),
            pltpu.VMEM((4, X, late, COLS), BF16),
            pltpu.VMEM((ROWS, COLS), BF16),
            pltpu.VMEM((ROWS, COLS), BF16),
            pltpu.VMEM((ROWS, COLS), BF16),
            pltpu.VMEM((2, ROWS, COLS), F32),
            pltpu.VMEM((TOK, D), BF16),
            pltpu.VMEM((TOK, D), BF16),
            pltpu.VMEM((TOK, D), BF16),
            *rings,
            pltpu.SemaphoreType.DMA((N_REDUCE_SEMS,)),
            pltpu.SemaphoreType.DMA((N_REDUCE_SEMS,)),
            pltpu.SemaphoreType.DMA((N_LOCAL_SEMS,)),
        ],
        compiler_params=pltpu.CompilerParams(
            collective_id=1, has_side_effects=True, vmem_limit_bytes=VMEM_LIMIT
        ),
        name="reduce_terms",
    )(xt, w, dkv, dq)


STEPS = 7


def update_kernel(
    tokens, dq_in, dn_in, total, master, moment_one, moment_two,
    dq_out, dn_out, master_out, one_out, two_out,
):
    dq_out[...] = dq_in[...]
    dn_out[...] = dn_in[...]
    for h in range(2):
        cols = pl.ds(h * COLS, COLS)
        grad = total[h] * float(tokens) ** (-0.5)
        first = 0.9 * moment_one[:, cols].astype(F32) + 0.1 * grad
        second = 0.999 * moment_two[:, cols].astype(F32) + 0.001 * grad * grad
        master_out[:, cols] = master[:, cols] - 0.001 * (first / (1.0 - 0.9**3)) / (
            jnp.sqrt(second / (1.0 - 0.999**3)) + 1e-08
        )
        one_out[:, cols] = first.astype(BF16)
        two_out[:, cols] = second.astype(BF16)


def update(tokens, dq, dn, total, master, moment_one, moment_two):
    def across(a):
        return pl.BlockSpec((a.shape[0], a.shape[1] // STEPS), lambda i: (0, i))

    def down(a):
        return pl.BlockSpec((a.shape[0] // STEPS, a.shape[1]), lambda i: (i, 0))

    return pl.pallas_call(
        functools.partial(update_kernel, tokens),
        grid=(STEPS,),
        out_shape=tuple(
            jax.ShapeDtypeStruct(a.shape, a.dtype) for a in (dq, dn, master, moment_one, moment_two)
        ),
        in_specs=[
            across(dq),
            across(dn),
            pl.BlockSpec((2, ROWS // STEPS, COLS), lambda i: (0, i, 0)),
            down(master),
            down(moment_one),
            down(moment_two),
        ],
        out_specs=(across(dq), across(dn), down(master), down(moment_one), down(moment_two)),
        compiler_params=pltpu.CompilerParams(vmem_limit_bytes=VMEM_LIMIT),
        name="update",
    )(dq, dn, total, master, moment_one, moment_two)


def on_device(normed, queries, output_gradient, doc_lengths, master, moment_one, moment_two):
    w, xt, q, do, kv = gather(normed, queries, output_gradient, master)
    dq, dkv = attention(doc_lengths, q, do, kv)
    dq, dn, total = reduce_terms(xt, w, dkv, dq)
    tokens = normed.shape[0] * lax.axis_size("dp") * lax.axis_size("seq")
    return update(tokens, dq, dn, total, master, moment_one, moment_two)


def solution(mesh):
    rows = P(("dp", "seq"), None)
    shard = P("dp", None)
    return jax.shard_map(
        on_device,
        mesh=mesh,
        in_specs=(rows, rows, rows, shard, shard, shard, shard),
        out_specs=(rows, rows, shard, shard, shard),
        check_vma=False,
    )
```

```python
import functools
import math

import jax
import jax.numpy as jnp
from jax import lax
from jax.experimental import pallas as pl
from jax.experimental.pallas import tpu as pltpu
from jax.sharding import PartitionSpec as P

HEAD = 128
GROUP = 7
X, Y, ZH = 4, 4, 2
TOK = 256
CT = 512
D = 7168
SHARDS = X * Y * ZH
ROWS = D // SHARDS
PARTS = (
    (0, 96, ("x", "y"), True),
    (96, 80, ("y", "x"), True),
    (176, 16, ("x", "y"), False),
    (192, 32, ("y", "x"), False),
)
SUM_PARTS = (
    (0, 96, ("x", "y"), True),
    (96, 80, ("y", "x"), True),
    (176, 16, ("x", "y"), False),
    (192, 32, ("y", "x"), False),
)
Z_FIRST = (0, 1)
Z_LAST = (2, 3)
SEQ = 1024
COLS = 512
HC = COLS // 2
QW = 896
ROW_BLOCK = X * ROWS
N_BLOCKS = Y * ZH
CHUNK = 128
N_CHUNKS = 5
LANES = GROUP * CHUNK
VMEM_LIMIT = 58 * 1024 * 1024
MESH = pl.DeviceIdType.MESH
ANY = pl.BlockSpec(memory_space=pl.ANY)
F32 = jnp.float32
BF16 = jnp.bfloat16


def dot(a, b, dims=((1,), (0,))):
    return lax.dot_general(a, b, (dims, ((), ())), preferred_element_type=F32)


class Place:
    def __init__(self):
        dp = lax.axis_index("dp")
        sq = lax.axis_index("seq")
        self.dp, self.sq = dp, sq
        self.x = lax.rem(dp, X)
        self.zh = lax.rem(lax.div(dp, X), ZH)
        self.y = lax.div(dp, X * ZH)
        self.core = lax.rem(sq, 2)
        self.zl = lax.div(sq, 2)

    def dev(self, x=None, y=None, zh=None, zl=None, core=None):
        x = self.x if x is None else x
        y = self.y if y is None else y
        zh = self.zh if zh is None else zh
        zl = self.zl if zl is None else zl
        core = self.core if core is None else core
        return ((y * ZH + zh) * X + x, zl * 2 + core)

    def along(self, axis, step):
        if axis == "x":
            return self.dev(x=lax.rem(self.x + step + X, X))
        return self.dev(y=lax.rem(self.y + step + Y, Y))

    def cross(self):
        return self.dev(zh=1 - self.zh, zl=1 - self.zl)

    def partner(self):
        return self.dev(zl=1 - self.zl)

    def other_core(self):
        return self.dev(core=1 - self.core)

    def greet(self):
        barrier = pltpu.get_barrier_semaphore()
        near = [self.along(a, s) for a in ("x", "y") for s in (1, -1)]
        near += [self.cross(), self.partner(), self.other_core()]
        near.append(self.dev(zl=1 - self.zl, core=1 - self.core))
        for d in near:
            pl.semaphore_signal(barrier, inc=1, device_id=d, device_id_type=MESH)
        pl.semaphore_wait(barrier, len(near))


class Links:
    def __init__(self, send_sem, recv_sem, place):
        self.send_sem, self.recv_sem, self.place = send_sem, recv_sem, place
        self.index = {}
        self.sent = []

    def _copy(self, key, src, dst, dev):
        k = self.index.setdefault(key, len(self.index))
        return pltpu.make_async_remote_copy(
            src_ref=src,
            dst_ref=dst,
            send_sem=self.send_sem.at[k],
            recv_sem=self.recv_sem.at[k],
            device_id=dev,
            device_id_type=MESH,
        )

    def send(self, key, src, dst, dev):
        copy = self._copy(key, src, dst, dev)
        copy.start()
        self.sent.append(copy)

    def recv(self, key, dst):
        self._copy(key, dst, dst, self.place.other_core()).wait_recv()

    def drain(self):
        for copy in self.sent:
            copy.wait_send()


N_GATHER_SEMS = 176
N_LOCAL_SEMS = 40


def gather_kernel(
    normed, queries, out_grad, master,
    w_out, xt_out, q_out, do_out, kv_out,
    w, xs, xt, mas, kv, acc, q_src, do_src, q_all, do_all, send_sem, recv_sem, loc_sem,
):
    here = Place()
    links = Links(send_sem, recv_sem, here)
    n_local = [0]

    def local(src, dst):
        copy = pltpu.make_async_copy(src, dst, loc_sem.at[n_local[0]])
        n_local[0] += 1
        copy.start()
        return copy

    core, zl = here.core, here.zl
    own_rows = pl.ds(pl.multiple_of(core * TOK, TOK), TOK)
    far_rows = pl.ds(pl.multiple_of((1 - core) * TOK, TOK), TOK)

    def seq_rows(sq):
        return pl.ds(pl.multiple_of(sq * TOK, TOK), TOK)

    def head_cols(zl_to, core_to):
        return pl.ds(pl.multiple_of((core_to * 2 + zl_to) * QW, 128), QW)

    get_master = local(master.at[:, pl.ds(pl.multiple_of(core * COLS, COLS), COLS)], mas)
    get_q = local(queries, q_src)
    get_do = local(out_grad, do_src)
    own_normed = local(normed, xs.at[own_rows, :])
    own_q = local(queries.at[:, head_cols(zl, core)], q_all.at[seq_rows(here.sq), :])
    own_do = local(out_grad.at[:, head_cols(zl, core)], do_all.at[seq_rows(here.sq), :])
    pending = []
    here.greet()
    get_master.wait()

    pos = {"x": here.x, "y": here.y}
    size = {"x": X, "y": Y}

    def at_axis(axis, off):
        return lax.rem(pos[axis] + off + size[axis], size[axis])

    def slot(p, da, db, zr, half=None):
        row, rows, axes, _ = PARTS[p]
        at = {axes[0]: at_axis(axes[0], da), axes[1]: at_axis(axes[1], db)}
        zh = here.zh if zr == 0 else 1 - here.zh
        s = (at["y"] * ZH + zh) * X + at["x"]
        cols = pl.ds(0, COLS) if half is None else pl.ds(half * HC, HC)
        return w.at[s, pl.ds(row, rows), cols]

    own = (here.y * ZH + here.zh) * X + here.x
    w[own] = mas[...].astype(BF16)

    def send(key, ref, dev):
        links.send(key, ref, ref, dev)

    def second_from(p, da, zr):
        b = PARTS[p][2][1]
        for step in (1, -1):
            send(("b", p, zr, da, step, 0), slot(p, da, 0, zr), here.along(b, step))

    def start(parts, zr):
        for p in parts:
            a = PARTS[p][2][0]
            for step in (1, -1):
                send(("a", p, zr, step, 0), slot(p, 0, 0, zr), here.along(a, step))
        for p in parts:
            second_from(p, 0, zr)

    def over_z(p, da, db):
        if p in Z_LAST:
            send(("z", p, da, db), slot(p, da, db, 0), here.cross())

    def forward_first(parts, zr):
        for p in parts:
            a = PARTS[p][2][0]
            for step in (1, -1):
                links.recv(("a", p, zr, step, 0), slot(p, -step, 0, zr))
                half = 0 if step == 1 else 1
                send(("a", p, zr, step, 1), slot(p, -step, 0, zr, half), here.along(a, step))
            for step in (1, -1):
                second_from(p, -step, zr)
                over_z(p, -step, 0)

    def finish_first(parts, zr):
        for p in parts:
            for step in (1, -1):
                half = 0 if step == 1 else 1
                links.recv(("a", p, zr, step, 1), slot(p, 2, 0, zr, half))
            second_from(p, 2, zr)
            over_z(p, 2, 0)

    def forward_second(parts, zr, after=None):
        for k, da in enumerate((0, -1, 1, 2)):
            for p in parts:
                b = PARTS[p][2][1]
                for step in (1, -1):
                    links.recv(("b", p, zr, da, step, 0), slot(p, da, -step, zr))
                    half = 0 if step == 1 else 1
                    send(
                        ("b", p, zr, da, step, 1),
                        slot(p, da, -step, zr, half),
                        here.along(b, step),
                    )
                    over_z(p, da, -step)
            if after is not None:
                after(k)

    def finish_second(parts, zr):
        for da in (0, -1, 1, 2):
            for p in parts:
                for step in (1, -1):
                    half = 0 if step == 1 else 1
                    links.recv(("b", p, zr, da, step, 1), slot(p, da, 2, zr, half))
                over_z(p, da, 2)

    def turn(first, last):
        @pl.loop(first, last)
        def _(b):
            at = pl.ds(pl.multiple_of(b * HEAD, HEAD), HEAD)
            xt[at, :] = xs[:, at].T

    start(Z_LAST, 0)
    start(Z_FIRST, 0)
    for p in Z_FIRST:
        send(("z", p), slot(p, 0, 0, 0), here.cross())
    for p in Z_LAST:
        over_z(p, 0, 0)
    links.send("normed", normed, xs.at[own_rows, :], here.other_core())
    get_q.wait()
    get_do.wait()
    others = (("p", 1 - zl, core), ("c", zl, 1 - core), ("d", 1 - zl, 1 - core))
    for name, src, dst in (("q", q_src, q_all), ("do", do_src, do_all)):
        for way, zl_to, core_to in others:
            links.send(
                (name, way),
                src.at[:, head_cols(zl_to, core_to)], dst.at[seq_rows(here.sq), :],
                here.dev(zl=zl_to, core=core_to),
            )
    forward_first(Z_LAST, 0)
    forward_first(Z_FIRST, 0)
    finish_first(Z_LAST, 0)
    for p in Z_FIRST:
        links.recv(("z", p), slot(p, 0, 0, 1))
    start(Z_FIRST, 1)
    finish_first(Z_FIRST, 0)
    own_normed.wait()
    links.recv("normed", xs.at[far_rows, :])
    turn(0, 14)
    forward_second(Z_LAST, 0)
    forward_first(Z_FIRST, 1)
    turn(14, 28)
    finish_second(Z_LAST, 0)
    finish_first(Z_FIRST, 1)
    turn(28, 42)
    forward_second(Z_FIRST, 0)
    turn(42, 56)
    pending.append(local(xt, xt_out))
    finish_second(Z_FIRST, 0)
    acc[...] = jnp.zeros_like(acc)

    def project(y, zh, cols, into):
        at = pl.ds(pl.multiple_of((y * ZH + zh) * ROW_BLOCK, 128), ROW_BLOCK)
        w_t = w[pl.ds((y * ZH + zh) * X, X), :, cols].reshape(ROW_BLOCK, HC)
        acc[into] += dot(xs[:, at], w_t)

    own_head = pl.ds(pl.multiple_of(zl * HC, HC), HC)
    far_head = pl.ds(pl.multiple_of((1 - zl) * HC, HC), HC)

    def own_half(k):
        project(k, here.zh, far_head, 0)
        project(k, here.zh, own_head, 1)

    forward_second(Z_FIRST, 1, own_half)
    finish_second(Z_FIRST, 1)
    for p in Z_LAST:
        for da in (0, -1, 1, 2):
            for db in (0, -1, 1, 2):
                links.recv(("z", p, da, db), slot(p, da, db, 1))
    pending.append(local(w, w_out))

    own_tokens = pl.ds(pl.multiple_of(zl * CT, CT), CT)
    for into, cols in ((0, far_head), (1, own_head)):

        @pl.loop(0, Y)
        def _(y):
            project(y, 1 - here.zh, cols, into)

        kv[into] = acc[into].astype(BF16)
        if into == 0:
            links.send("kv", kv.at[0], kv_out.at[own_tokens, :], here.partner())
        else:
            pending.append(local(kv.at[1], kv_out.at[own_tokens, :]))
    own_q.wait()
    own_do.wait()
    for name, dst in (("q", q_all), ("do", do_all)):
        for way, zl_to, core_to in others:
            links.recv((name, way), dst.at[seq_rows(zl_to * 2 + core_to), :])
    pending.append(local(q_all, q_out))
    pending.append(local(do_all, do_out))
    links.recv("kv", kv_out.at[pl.ds(pl.multiple_of((1 - zl) * CT, CT), CT), :])
    for copy in pending:
        copy.wait()
    links.drain()


def gather(normed, queries, out_grad, master):
    return pl.pallas_call(
        gather_kernel,
        out_shape=(
            jax.ShapeDtypeStruct((SHARDS, ROWS, COLS), BF16),
            jax.ShapeDtypeStruct((D, CT), BF16),
            jax.ShapeDtypeStruct((SEQ, QW), BF16),
            jax.ShapeDtypeStruct((SEQ, QW), BF16),
            jax.ShapeDtypeStruct((SEQ, HC), BF16),
        ),
        in_specs=[ANY] * 4,
        out_specs=(ANY,) * 5,
        scratch_shapes=[
            pltpu.VMEM((SHARDS, ROWS, COLS), BF16),
            pltpu.VMEM((CT, D), BF16),
            pltpu.VMEM((D, CT), BF16),
            pltpu.VMEM((ROWS, COLS), F32),
            pltpu.VMEM((2, CT, HC), BF16),
            pltpu.VMEM((2, CT, HC), F32),
            pltpu.VMEM(queries.shape, BF16),
            pltpu.VMEM(queries.shape, BF16),
            pltpu.VMEM((SEQ, QW), BF16),
            pltpu.VMEM((SEQ, QW), BF16),
            pltpu.SemaphoreType.DMA((N_GATHER_SEMS,)),
            pltpu.SemaphoreType.DMA((N_GATHER_SEMS,)),
            pltpu.SemaphoreType.DMA((N_LOCAL_SEMS,)),
        ],
        compiler_params=pltpu.CompilerParams(
            collective_id=0, has_side_effects=True, vmem_limit_bytes=VMEM_LIMIT
        ),
        name="gather_project",
    )(normed, queries, out_grad, master)


def attention_kernel(
    lengths, q_ref, do_ref, kv_ref, dq_ref, dkv_ref,
    qs, dos, prob, dprob, prob_half, d_scores, dk_acc, dv_acc,
):
    i = pl.program_id(0)
    scale = HEAD ** (-0.5)
    to_base2 = scale * math.log2(math.e)
    ends = []
    total = lengths[0, 0]
    ends.append(total)
    for j in range(1, lengths.shape[1]):
        total = total + lengths[0, j]
        ends.append(total)

    @pl.when(i == 0)
    def _():
        dk_acc[...] = jnp.zeros_like(dk_acc)
        dv_acc[...] = jnp.zeros_like(dv_acc)

    lane = lax.broadcasted_iota(jnp.int32, (1, CHUNK), 1)
    sub = lax.broadcasted_iota(jnp.int32, (CHUNK, 1), 0)
    q_row = i * CHUNK + lane
    doc_start = jnp.zeros_like(q_row)
    first_start = jnp.int32(0)
    for e in ends:
        doc_start = jnp.where(q_row >= e, jnp.maximum(doc_start, e), doc_start)
        first_start = jnp.where(i * CHUNK >= e, jnp.maximum(first_start, e), first_start)
    lowest = lax.div(first_start, CHUNK)
    lowest = jnp.maximum(lowest, i - (N_CHUNKS - 1))
    for a in range(GROUP):
        qs[a * CHUNK : (a + 1) * CHUNK, :] = q_ref[:, a * HEAD : (a + 1) * HEAD]
        dos[a * CHUNK : (a + 1) * CHUNK, :] = do_ref[:, a * HEAD : (a + 1) * HEAD]

    def chunks(n):
        low = i + 1 - n
        keys = pl.ds(pl.multiple_of(low * CHUNK, CHUNK), n * CHUNK)
        here = slice(0, n * CHUNK)
        prob[here, :] = dot(kv_ref[keys, 0:HEAD], qs[...], ((1,), (1,)))
        dprob[here, :] = dot(kv_ref[keys, HEAD : 2 * HEAD], dos[...], ((1,), (1,)))
        for a in range(GROUP):
            cols = slice(a * CHUNK, (a + 1) * CHUNK)
            parts = []
            top = None
            for t in range(n):
                k_row = (low + t) * CHUNK + sub
                keep = k_row >= doc_start
                if t == n - 1:
                    keep = keep & (k_row <= q_row)
                part = jnp.where(keep, prob[t * CHUNK : (t + 1) * CHUNK, cols], -1e30)
                parts.append(part)
                most = jnp.max(part, axis=0, keepdims=True)
                top = most if top is None else jnp.maximum(top, most)
            mass = jnp.zeros((1, CHUNK), F32)
            delta = jnp.zeros((1, CHUNK), F32)
            for t in range(n):
                p = jnp.exp2((parts[t] - top) * to_base2)
                parts[t] = p
                mass = mass + jnp.sum(p, axis=0, keepdims=True)
                dp = dprob[t * CHUNK : (t + 1) * CHUNK, cols]
                delta = delta + jnp.sum(p * dp, axis=0, keepdims=True)
            inv = 1.0 / mass
            delta = delta * inv
            for t in range(n):
                rows = slice(t * CHUNK, (t + 1) * CHUNK)
                p = parts[t] * inv
                prob_half[rows, cols] = p.astype(BF16)
                d_scores[rows, cols] = (p * (dprob[rows, cols] - delta)).astype(BF16)
        dv_acc[keys, :] += dot(prob_half[here, :], dos[...])
        dk_acc[keys, :] += dot(d_scores[here, :], qs[...])
        dq_t = dot(kv_ref[keys, 0:HEAD], d_scores[here, :], ((0,), (0,)))
        for a in range(GROUP):
            part = dq_t[:, a * CHUNK : (a + 1) * CHUNK].T * scale
            dq_ref[:, a * HEAD : (a + 1) * HEAD] = part.astype(BF16)

    for n in range(1, N_CHUNKS + 1):
        pl.when(i + 1 - lowest == n)(functools.partial(chunks, n))

    @pl.when(i == pl.num_programs(0) - 1)
    def _():
        dkv_ref[:, 0:HEAD] = (dk_acc[...] * scale).astype(BF16)
        dkv_ref[:, HEAD : 2 * HEAD] = dv_acc[...].astype(BF16)


def attention(lengths, q, do, kv):
    return pl.pallas_call(
        attention_kernel,
        grid=(SEQ // CHUNK,),
        out_shape=(
            jax.ShapeDtypeStruct((SEQ, QW), BF16),
            jax.ShapeDtypeStruct((SEQ, HC), BF16),
        ),
        in_specs=[
            pl.BlockSpec(memory_space=pltpu.SMEM),
            pl.BlockSpec((CHUNK, QW), lambda i: (i, 0)),
            pl.BlockSpec((CHUNK, QW), lambda i: (i, 0)),
            pl.BlockSpec((SEQ, HC), lambda i: (0, 0)),
        ],
        out_specs=(
            pl.BlockSpec((CHUNK, QW), lambda i: (i, 0)),
            pl.BlockSpec((SEQ, HC), lambda i: (0, 0)),
        ),
        scratch_shapes=[
            pltpu.VMEM((LANES, HEAD), BF16),
            pltpu.VMEM((LANES, HEAD), BF16),
            pltpu.VMEM((N_CHUNKS * CHUNK, LANES), F32),
            pltpu.VMEM((N_CHUNKS * CHUNK, LANES), F32),
            pltpu.VMEM((N_CHUNKS * CHUNK, LANES), BF16),
            pltpu.VMEM((N_CHUNKS * CHUNK, LANES), BF16),
            pltpu.VMEM((SEQ, HEAD), F32),
            pltpu.VMEM((SEQ, HEAD), F32),
        ],
        compiler_params=pltpu.CompilerParams(vmem_limit_bytes=VMEM_LIMIT),
        name="attention_back",
    )(lengths, q, do, kv)


N_REDUCE_SEMS = 176


def reduce_kernel(
    xt_in, w_in, dkv_in, dq_in,
    dq_out, dn_out, grad_out,
    xt, w, term, dkv, dq_src, dq_all, z_early, z_in, l_in, mine, total, dn_send, dn_recv, dn_own,
    *rest,
):
    bufs = [rest[6 * p : 6 * p + 6] for p in range(4)]
    send_sem, recv_sem, loc_sem = rest[24:]
    here = Place()
    links = Links(send_sem, recv_sem, here)
    n_local = [0]

    def local(src, dst):
        copy = pltpu.make_async_copy(src, dst, loc_sem.at[n_local[0]])
        n_local[0] += 1
        copy.start()
        return copy

    core, zl = here.core, here.zl
    own_z, far_z = here.zh, 1 - here.zh
    own_rows = pl.ds(pl.multiple_of(core * TOK, TOK), TOK)
    far_rows = pl.ds(pl.multiple_of((1 - core) * TOK, TOK), TOK)
    own_tokens = pl.ds(pl.multiple_of(zl * CT, CT), CT)
    far_tokens = pl.ds(pl.multiple_of((1 - zl) * CT, CT), CT)

    def seq_rows(sq):
        return pl.ds(pl.multiple_of(sq * TOK, TOK), TOK)

    def head_cols(zl_of, core_of):
        return pl.ds(pl.multiple_of((core_of * 2 + zl_of) * QW, 128), QW)

    get_dkv = local(dkv_in.at[own_tokens, :], dkv.at[zl])
    get_xt = local(xt_in, xt)
    get_dq = local(dq_in, dq_src)
    own_dq = local(dq_in.at[seq_rows(here.sq), :], dq_all.at[:, head_cols(zl, core)])
    here.greet()
    links.send("dkv", dkv_in.at[far_tokens, :], dkv.at[zl], here.partner())
    get_w = local(w_in, w)
    pending = []
    get_dkv.wait()
    get_xt.wait()
    links.recv("dkv", dkv.at[1 - zl])

    pos = {"x": here.x, "y": here.y}
    size = {"x": X, "y": Y}

    def at_axis(axis, off):
        return lax.rem(pos[axis] + off + size[axis], size[axis])

    class Ring:
        def __init__(self, name, axis, slot, opp, low, high):
            self.name, self.axis, self.slot = name, axis, slot
            self.opp, self.low, self.high = opp, low, high

        def half(self, ref, h):
            return ref.at[:, :, pl.ds(h * HC, HC)]

        def send_far(self):
            for h, step in ((0, 1), (1, -1)):
                links.send(
                    (self.name, "far", step),
                    self.half(self.slot(2), h), self.opp(h), here.along(self.axis, step),
                )

        def send_near(self, step):
            h, land = (1, self.low) if step == 1 else (0, self.high)
            links.send(
                (self.name, "near", step),
                self.half(self.slot(step), h), self.half(land(), h), here.along(self.axis, step),
            )

        def forward(self):
            for h, step in ((0, 1), (1, -1)):
                links.recv((self.name, "far", step), self.opp(h))
                here_sum = self.half(self.slot(step), h)
                here_sum[...] = (
                    here_sum[...].astype(F32) + self.opp(h)[...].astype(F32)
                ).astype(BF16)
                land = self.low if step == 1 else self.high
                links.send(
                    (self.name, "sum", step),
                    here_sum, self.half(land(), h), here.along(self.axis, step),
                )

        def finish(self):
            for h, step in ((1, 1), (0, -1)):
                land = self.low if step == 1 else self.high
                links.recv((self.name, "near", step), self.half(land(), h))
                links.recv((self.name, "sum", step), self.half(land(), 1 - h))
            mine_ref = self.slot(0)
            mine_ref[...] = (
                mine_ref[...].astype(F32)
                + self.low()[...].astype(F32)
                + self.high()[...].astype(F32)
            ).astype(BF16)

    def rows_of(p):
        return pl.ds(SUM_PARTS[p][0], SUM_PARTS[p][1])

    def term_at(at, p):
        zs = pl.ds(0, ZH) if p in Z_FIRST else pl.ds(own_z, 1)
        return term.at[at["y"], zs, at["x"], rows_of(p), :]

    def first_ring(p, k, off):
        a, b = SUM_PARTS[p][2]
        opp, low, high = bufs[p][:3]

        def slot(da):
            return term_at({a: at_axis(a, da), b: at_axis(b, off)}, p)

        return Ring(
            ("first", p, k), a, slot,
            lambda h: opp.at[k, h], lambda: low.at[k], lambda: high.at[k],
        )

    def second_ring(p):
        a, b = SUM_PARTS[p][2]
        opp, low, high = bufs[p][3:]

        def slot(db):
            return term_at({a: pos[a], b: at_axis(b, db)}, p)

        return Ring(("second", p), b, slot, lambda h: opp.at[h], lambda: low, lambda: high)

    offs = (2, 1, -1, 0)
    rings = [[first_ring(p, k, off) for k, off in enumerate(offs)] for p in range(4)]
    finals = [second_ring(p) for p in range(4)]
    late = pl.ds(SUM_PARTS[2][0], SUM_PARTS[2][1] + SUM_PARTS[3][1])

    def make_terms(k):
        y = at_axis("y", offs[k])
        for z in (far_z, own_z):
            at = pl.ds(pl.multiple_of((y * ZH + z) * ROW_BLOCK, 128), ROW_BLOCK)
            for h in range(2):
                t = dot(xt[at, :], dkv[h]).astype(BF16)
                term[y, z, :, :, h * HC : (h + 1) * HC] = t.reshape(X, ROWS, HC)
        links.send(
            ("early", k), term.at[y, far_z, :, late, :], z_early.at[k], here.cross()
        )

    def add_early(k):
        y = at_axis("y", offs[k])
        links.recv(("early", k), z_early.at[k])
        into = term.at[y, own_z, :, late, :]
        into[...] = (into[...].astype(F32) + z_early[k].astype(F32)).astype(BF16)

    def launch(k, p_x, p_y):
        rings[p_x][k].send_far()
        for step in (1, -1):
            rings[p_x][k].send_near(step)
        for piece in rings[p_y]:
            if k == 0:
                piece.send_far()
            elif k < 3:
                piece.send_near(offs[k])

    def dn_far(t):
        at = pl.ds(t * ROW_BLOCK, ROW_BLOCK)
        partial = jnp.zeros((TOK, ROW_BLOCK), F32)
        for h in range(2):
            w_t = w[pl.ds(t * X, X), :, h * HC : (h + 1) * HC].reshape(ROW_BLOCK, HC)
            partial += dot(dkv[h, far_rows, :], w_t, ((1,), (1,)))
        dn_send[:, at] = partial.astype(BF16)
        links.send(("dn", t), dn_send.at[:, at], dn_recv.at[:, at], here.other_core())

    def dn_near(t):
        at = pl.ds(t * ROW_BLOCK, ROW_BLOCK)
        links.recv(("dn", t), dn_recv.at[:, at])
        partial = dn_recv[:, at].astype(F32)
        for h in range(2):
            w_t = w[pl.ds(t * X, X), :, h * HC : (h + 1) * HC].reshape(ROW_BLOCK, HC)
            partial += dot(dkv[h, own_rows, :], w_t, ((1,), (1,)))
        dn_own[:, at] = partial.astype(BF16)
        pending.append(local(dn_own.at[:, at], dn_out.at[:, at]))

    for k in range(4):
        make_terms(k)
        launch(k, 0, 1)
    get_dq.wait()
    others = (("p", 1 - zl, core), ("c", zl, 1 - core), ("d", 1 - zl, 1 - core))
    for way, zl_to, core_to in others:
        links.send(
            ("dq", way),
            dq_src.at[seq_rows(zl_to * 2 + core_to), :], dq_all.at[:, head_cols(zl, core)],
            here.dev(zl=zl_to, core=core_to),
        )
    get_w.wait()
    for k in range(4):
        for p in Z_FIRST:
            rings[p][k].forward()
        add_early(k)
        launch(k, 2, 3)
        dn_far(2 * k)
        dn_far(2 * k + 1)

    def end_first(k, parts):
        for p in parts:
            rings[p][k].finish()
            if k == 0:
                finals[p].send_far()
            elif k < 3:
                finals[p].send_near(offs[k])

    for k in range(4):
        for p in Z_LAST:
            rings[p][k].forward()
        end_first(k, Z_FIRST)
        dn_near(2 * k)
        dn_near(2 * k + 1)
    for p in Z_FIRST:
        finals[p].forward()
    for k in range(4):
        end_first(k, Z_LAST)
    for p in Z_FIRST:
        finals[p].finish()
        rows = rows_of(p)
        links.send(
            ("z", p), term.at[here.y, far_z, here.x, rows, :], z_in.at[rows, :], here.cross()
        )
    for p in Z_LAST:
        finals[p].forward()

    def to_partner(p):
        rows = rows_of(p)
        links.send(("l", p), mine.at[rows, :], l_in.at[rows, :], here.partner())

    for p in Z_FIRST:
        rows = rows_of(p)
        links.recv(("z", p), z_in.at[rows, :])
        mine[rows, :] = (
            term[here.y, own_z, here.x, rows, :].astype(F32) + z_in[rows, :].astype(F32)
        ).astype(BF16)
        to_partner(p)
    for p in Z_LAST:
        finals[p].finish()
        rows = rows_of(p)
        mine[rows, :] = term[here.y, own_z, here.x, rows, :]
        to_partner(p)
    for p in range(4):
        rows = rows_of(p)
        links.recv(("l", p), l_in.at[rows, :])
        total[core, rows, :] = mine[rows, :].astype(F32) + l_in[rows, :].astype(F32)
        links.send(
            ("c", p), total.at[core, rows, :], total.at[core, rows, :], here.other_core()
        )
    own_dq.wait()
    for way, zl_to, core_to in others:
        links.recv(("dq", way), dq_all.at[:, head_cols(zl_to, core_to)])
    pending.append(local(dq_all, dq_out))
    for p in range(4):
        links.recv(("c", p), total.at[1 - core, rows_of(p), :])
    pending.append(local(total, grad_out))
    for copy in pending:
        copy.wait()
    links.drain()


def reduce_terms(xt, w, dkv, dq):
    rings = []
    for p, (_, rows, _, both) in enumerate(SUM_PARTS):
        nz = ZH if both else 1
        rings += [
            pltpu.VMEM((4, 2, nz, rows, HC), BF16),
            pltpu.VMEM((4, nz, rows, COLS), BF16),
            pltpu.VMEM((4, nz, rows, COLS), BF16),
            pltpu.VMEM((2, nz, rows, HC), BF16),
            pltpu.VMEM((nz, rows, COLS), BF16),
            pltpu.VMEM((nz, rows, COLS), BF16),
        ]
    late = SUM_PARTS[2][1] + SUM_PARTS[3][1]
    return pl.pallas_call(
        reduce_kernel,
        out_shape=(
            jax.ShapeDtypeStruct((TOK, 4 * QW), BF16),
            jax.ShapeDtypeStruct((TOK, D), BF16),
            jax.ShapeDtypeStruct((2, ROWS, COLS), F32),
        ),
        in_specs=[ANY] * 4,
        out_specs=(ANY,) * 3,
        scratch_shapes=[
            pltpu.VMEM((D, CT), BF16),
            pltpu.VMEM((SHARDS, ROWS, COLS), BF16),
            pltpu.VMEM((Y, ZH, X, ROWS, COLS), BF16),
            pltpu.VMEM((2, CT, HC), BF16),
            pltpu.VMEM((SEQ, QW), BF16),
            pltpu.VMEM((TOK, 4 * QW), BF16),
            pltpu.VMEM((4, X, late, COLS), BF16),
            pltpu.VMEM((ROWS, COLS), BF16),
            pltpu.VMEM((ROWS, COLS), BF16),
            pltpu.VMEM((ROWS, COLS), BF16),
            pltpu.VMEM((2, ROWS, COLS), F32),
            pltpu.VMEM((TOK, D), BF16),
            pltpu.VMEM((TOK, D), BF16),
            pltpu.VMEM((TOK, D), BF16),
            *rings,
            pltpu.SemaphoreType.DMA((N_REDUCE_SEMS,)),
            pltpu.SemaphoreType.DMA((N_REDUCE_SEMS,)),
            pltpu.SemaphoreType.DMA((N_LOCAL_SEMS,)),
        ],
        compiler_params=pltpu.CompilerParams(
            collective_id=1, has_side_effects=True, vmem_limit_bytes=VMEM_LIMIT
        ),
        name="reduce_terms",
    )(xt, w, dkv, dq)


def update_kernel(
    tokens, dq_in, dn_in, total_in, master_in, one_in, two_in,
    dq_out, dn_out, master_out, one_out, two_out,
    dq, dn, total, master, one, two, in_sem, out_sem,
):
    gets, puts = [], []

    def get(src, dst):
        copy = pltpu.make_async_copy(src, dst, in_sem.at[len(gets)])
        copy.start()
        gets.append(copy)
        return copy

    def put(src, dst):
        copy = pltpu.make_async_copy(src, dst, out_sem.at[len(puts)])
        copy.start()
        puts.append(copy)

    first_gets = [get(total_in, total), get(master_in, master), get(one_in, one), get(two_in, two)]
    blocks = []
    for src, mid, dst, n in ((dn_in, dn, dn_out, 4), (dq_in, dq, dq_out, 2)):
        rows = src.shape[0] // n
        for b in range(n):
            at = pl.ds(b * rows, rows)
            blocks.append((get(src.at[at, :], mid.at[at, :]), mid.at[at, :], dst.at[at, :]))
    for copy in first_gets:
        copy.wait()
    rows = ROWS // 2
    for b in range(2):
        at = pl.ds(b * rows, rows)
        for h in range(2):
            cols = pl.ds(h * COLS, COLS)
            grad = total[h, at, :] * float(tokens) ** (-0.5)
            first = 0.9 * one[at, cols].astype(F32) + 0.1 * grad
            second = 0.999 * two[at, cols].astype(F32) + 0.001 * grad * grad
            master[at, cols] = master[at, cols] - 0.001 * (first / (1.0 - 0.9**3)) / (
                jnp.sqrt(second / (1.0 - 0.999**3)) + 1e-08
            )
            one[at, cols] = first.astype(BF16)
            two[at, cols] = second.astype(BF16)
        for mid, dst in ((master, master_out), (one, one_out), (two, two_out)):
            put(mid.at[at, :], dst.at[at, :])
        for copy, mid, dst in blocks[3 * b : 3 * b + 3]:
            copy.wait()
            put(mid, dst)
    for copy in puts:
        copy.wait()


def update(tokens, dq, dn, total, master, moment_one, moment_two):
    results = (dq, dn, master, moment_one, moment_two)
    return pl.pallas_call(
        functools.partial(update_kernel, tokens),
        out_shape=tuple(jax.ShapeDtypeStruct(a.shape, a.dtype) for a in results),
        in_specs=[ANY] * 6,
        out_specs=(ANY,) * 5,
        scratch_shapes=[
            *[pltpu.VMEM(a.shape, a.dtype) for a in (dq, dn, total, master, moment_one, moment_two)],
            pltpu.SemaphoreType.DMA((12,)),
            pltpu.SemaphoreType.DMA((12,)),
        ],
        compiler_params=pltpu.CompilerParams(vmem_limit_bytes=VMEM_LIMIT),
        name="update",
    )(dq, dn, total, master, moment_one, moment_two)


def on_device(normed, queries, output_gradient, doc_lengths, master, moment_one, moment_two):
    w, xt, q, do, kv = gather(normed, queries, output_gradient, master)
    dq, dkv = attention(doc_lengths, q, do, kv)
    dq, dn, total = reduce_terms(xt, w, dkv, dq)
    tokens = normed.shape[0] * lax.axis_size("dp") * lax.axis_size("seq")
    return update(tokens, dq, dn, total, master, moment_one, moment_two)


def solution(mesh):
    rows = P(("dp", "seq"), None)
    shard = P("dp", None)
    return jax.shard_map(
        on_device,
        mesh=mesh,
        in_specs=(rows, rows, rows, shard, shard, shard, shard),
        out_specs=(rows, rows, shard, shard, shard),
        check_vma=False,
    )
```

```python
import functools
import math

import jax
import jax.numpy as jnp
from jax import lax
from jax.experimental import pallas as pl
from jax.experimental.pallas import tpu as pltpu
from jax.sharding import PartitionSpec as P

HEAD = 128
GROUP = 7
X, Y, ZH = 4, 4, 2
TOK = 256
CT = 512
D = 7168
SHARDS = X * Y * ZH
ROWS = D // SHARDS
PARTS = (
    (0, 96, ("x", "y"), True),
    (96, 80, ("y", "x"), True),
    (176, 16, ("x", "y"), False),
    (192, 32, ("y", "x"), False),
)
SUM_PARTS = (
    (0, 80, ("x", "y"), True),
    (80, 80, ("y", "x"), True),
    (160, 32, ("x", "y"), False),
    (192, 32, ("y", "x"), False),
)
Z_FIRST = (0, 1)
Z_LAST = (2, 3)
SEQ = 1024
COLS = 512
HC = COLS // 2
QW = 896
ROW_BLOCK = X * ROWS
N_BLOCKS = Y * ZH
CHUNK = 128
N_CHUNKS = 5
LANES = GROUP * CHUNK
VMEM_LIMIT = 58 * 1024 * 1024
MESH = pl.DeviceIdType.MESH
ANY = pl.BlockSpec(memory_space=pl.ANY)
F32 = jnp.float32
BF16 = jnp.bfloat16


def dot(a, b, dims=((1,), (0,))):
    return lax.dot_general(a, b, (dims, ((), ())), preferred_element_type=F32)


class Place:
    def __init__(self):
        dp = lax.axis_index("dp")
        sq = lax.axis_index("seq")
        self.dp, self.sq = dp, sq
        self.x = lax.rem(dp, X)
        self.zh = lax.rem(lax.div(dp, X), ZH)
        self.y = lax.div(dp, X * ZH)
        self.core = lax.rem(sq, 2)
        self.zl = lax.div(sq, 2)

    def dev(self, x=None, y=None, zh=None, zl=None, core=None):
        x = self.x if x is None else x
        y = self.y if y is None else y
        zh = self.zh if zh is None else zh
        zl = self.zl if zl is None else zl
        core = self.core if core is None else core
        return ((y * ZH + zh) * X + x, zl * 2 + core)

    def along(self, axis, step):
        if axis == "x":
            return self.dev(x=lax.rem(self.x + step + X, X))
        return self.dev(y=lax.rem(self.y + step + Y, Y))

    def cross(self):
        return self.dev(zh=1 - self.zh, zl=1 - self.zl)

    def partner(self):
        return self.dev(zl=1 - self.zl)

    def other_core(self):
        return self.dev(core=1 - self.core)

    def greet(self):
        barrier = pltpu.get_barrier_semaphore()
        near = [self.along(a, s) for a in ("x", "y") for s in (1, -1)]
        near += [self.cross(), self.partner(), self.other_core()]
        near.append(self.dev(zl=1 - self.zl, core=1 - self.core))
        for d in near:
            pl.semaphore_signal(barrier, inc=1, device_id=d, device_id_type=MESH)
        pl.semaphore_wait(barrier, len(near))


class Links:
    def __init__(self, send_sem, recv_sem, place):
        self.send_sem, self.recv_sem, self.place = send_sem, recv_sem, place
        self.index = {}
        self.used = 0
        self.sent = []

    def _copy(self, key, src, dst, dev, half=None):
        if key not in self.index:
            self.index[key] = self.used
            self.used += 1 if half is None else 2
        k = self.index[key] + (0 if half is None else half)
        return pltpu.make_async_remote_copy(
            src_ref=src,
            dst_ref=dst,
            send_sem=self.send_sem.at[k],
            recv_sem=self.recv_sem.at[k],
            device_id=dev,
            device_id_type=MESH,
        )

    def send(self, key, src, dst, dev, half=None):
        copy = self._copy(key, src, dst, dev, half)
        copy.start()
        self.sent.append(copy)

    def recv(self, key, dst, half=None):
        self._copy(key, dst, dst, self.place.other_core(), half).wait_recv()

    def drain(self):
        for copy in self.sent:
            copy.wait_send()


N_GATHER_SEMS = 176
N_LOCAL_SEMS = 40


def gather_kernel(
    normed, queries, out_grad, master,
    w_out, xt_out, q_out, do_out, kv_out,
    w, xs, xt, mas, kv, acc, q_src, do_src, q_all, do_all, send_sem, recv_sem, loc_sem,
):
    here = Place()
    links = Links(send_sem, recv_sem, here)
    n_local = [0]

    def local(src, dst):
        copy = pltpu.make_async_copy(src, dst, loc_sem.at[n_local[0]])
        n_local[0] += 1
        copy.start()
        return copy

    core, zl = here.core, here.zl
    own_rows = pl.ds(pl.multiple_of(core * TOK, TOK), TOK)
    far_rows = pl.ds(pl.multiple_of((1 - core) * TOK, TOK), TOK)

    def seq_rows(sq):
        return pl.ds(pl.multiple_of(sq * TOK, TOK), TOK)

    def head_cols(zl_to, core_to):
        return pl.ds(pl.multiple_of((core_to * 2 + zl_to) * QW, 128), QW)

    get_master = local(master.at[:, pl.ds(pl.multiple_of(core * COLS, COLS), COLS)], mas)
    get_q = local(queries, q_src)
    get_do = local(out_grad, do_src)
    own_normed = local(normed, xs.at[own_rows, :])
    own_q = local(queries.at[:, head_cols(zl, core)], q_all.at[seq_rows(here.sq), :])
    own_do = local(out_grad.at[:, head_cols(zl, core)], do_all.at[seq_rows(here.sq), :])
    pending = []
    here.greet()
    get_master.wait()

    pos = {"x": here.x, "y": here.y}
    size = {"x": X, "y": Y}

    def at_axis(axis, off):
        return lax.rem(pos[axis] + off + size[axis], size[axis])

    def slot(p, da, db, zr, half=None):
        row, rows, axes, _ = PARTS[p]
        at = {axes[0]: at_axis(axes[0], da), axes[1]: at_axis(axes[1], db)}
        zh = here.zh if zr == 0 else 1 - here.zh
        s = (at["y"] * ZH + zh) * X + at["x"]
        cols = pl.ds(0, COLS) if half is None else pl.ds(half * HC, HC)
        return w.at[s, pl.ds(row, rows), cols]

    own = (here.y * ZH + here.zh) * X + here.x
    w[own] = mas[...].astype(BF16)

    def send(key, ref, dev):
        links.send(key, ref, ref, dev)

    def second_from(p, da, zr):
        b = PARTS[p][2][1]
        for step in (1, -1):
            send(("b", p, zr, da, step, 0), slot(p, da, 0, zr), here.along(b, step))

    def start(parts, zr):
        for p in parts:
            a = PARTS[p][2][0]
            for step in (1, -1):
                send(("a", p, zr, step, 0), slot(p, 0, 0, zr), here.along(a, step))
        for p in parts:
            second_from(p, 0, zr)

    def over_z(p, da, db):
        if p in Z_LAST:
            send(("z", p, da, db), slot(p, da, db, 0), here.cross())

    def forward_first(parts, zr):
        for p in parts:
            a = PARTS[p][2][0]
            for step in (1, -1):
                links.recv(("a", p, zr, step, 0), slot(p, -step, 0, zr))
                half = 0 if step == 1 else 1
                send(("a", p, zr, step, 1), slot(p, -step, 0, zr, half), here.along(a, step))
            for step in (1, -1):
                second_from(p, -step, zr)
                over_z(p, -step, 0)

    def finish_first(parts, zr):
        for p in parts:
            for step in (1, -1):
                half = 0 if step == 1 else 1
                links.recv(("a", p, zr, step, 1), slot(p, 2, 0, zr, half))
            second_from(p, 2, zr)
            over_z(p, 2, 0)

    def forward_second(parts, zr, after=None):
        for k, da in enumerate((0, -1, 1, 2)):
            for p in parts:
                b = PARTS[p][2][1]
                for step in (1, -1):
                    links.recv(("b", p, zr, da, step, 0), slot(p, da, -step, zr))
                    half = 0 if step == 1 else 1
                    send(
                        ("b", p, zr, da, step, 1),
                        slot(p, da, -step, zr, half),
                        here.along(b, step),
                    )
                    over_z(p, da, -step)
            if after is not None:
                after(k)

    def finish_second(parts, zr):
        for da in (0, -1, 1, 2):
            for p in parts:
                for step in (1, -1):
                    half = 0 if step == 1 else 1
                    links.recv(("b", p, zr, da, step, 1), slot(p, da, 2, zr, half))
                over_z(p, da, 2)

    def turn(first, last):
        @pl.loop(first, last)
        def _(b):
            at = pl.ds(pl.multiple_of(b * HEAD, HEAD), HEAD)
            xt[at, :] = xs[:, at].T

    start(Z_LAST, 0)
    start(Z_FIRST, 0)
    for p in Z_FIRST:
        send(("z", p), slot(p, 0, 0, 0), here.cross())
    for p in Z_LAST:
        over_z(p, 0, 0)
    links.send("normed", normed, xs.at[own_rows, :], here.other_core())
    get_q.wait()
    get_do.wait()
    others = (("p", 1 - zl, core), ("c", zl, 1 - core), ("d", 1 - zl, 1 - core))
    for name, src, dst in (("q", q_src, q_all), ("do", do_src, do_all)):
        for way, zl_to, core_to in others:
            links.send(
                (name, way),
                src.at[:, head_cols(zl_to, core_to)], dst.at[seq_rows(here.sq), :],
                here.dev(zl=zl_to, core=core_to),
            )
    forward_first(Z_LAST, 0)
    forward_first(Z_FIRST, 0)
    finish_first(Z_LAST, 0)
    for p in Z_FIRST:
        links.recv(("z", p), slot(p, 0, 0, 1))
    start(Z_FIRST, 1)
    finish_first(Z_FIRST, 0)
    own_normed.wait()
    links.recv("normed", xs.at[far_rows, :])
    turn(0, 14)
    forward_second(Z_LAST, 0)
    forward_first(Z_FIRST, 1)
    turn(14, 28)
    finish_second(Z_LAST, 0)
    finish_first(Z_FIRST, 1)
    turn(28, 42)
    forward_second(Z_FIRST, 0)
    turn(42, 56)
    pending.append(local(xt, xt_out))
    finish_second(Z_FIRST, 0)
    acc[...] = jnp.zeros_like(acc)

    def project(y, zh, cols, into):
        at = pl.ds(pl.multiple_of((y * ZH + zh) * ROW_BLOCK, 128), ROW_BLOCK)
        w_t = w[pl.ds((y * ZH + zh) * X, X), :, cols].reshape(ROW_BLOCK, HC)
        acc[into] += dot(xs[:, at], w_t)

    own_head = pl.ds(pl.multiple_of(zl * HC, HC), HC)
    far_head = pl.ds(pl.multiple_of((1 - zl) * HC, HC), HC)

    def own_half(k):
        project(k, here.zh, far_head, 0)
        project(k, here.zh, own_head, 1)

    forward_second(Z_FIRST, 1, own_half)
    finish_second(Z_FIRST, 1)
    for p in Z_LAST:
        for da in (0, -1, 1, 2):
            for db in (0, -1, 1, 2):
                links.recv(("z", p, da, db), slot(p, da, db, 1))
    pending.append(local(w, w_out))

    own_tokens = pl.ds(pl.multiple_of(zl * CT, CT), CT)
    for into, cols in ((0, far_head), (1, own_head)):

        @pl.loop(0, Y)
        def _(y):
            project(y, 1 - here.zh, cols, into)

        kv[into] = acc[into].astype(BF16)
        if into == 0:
            links.send("kv", kv.at[0], kv_out.at[own_tokens, :], here.partner())
        else:
            pending.append(local(kv.at[1], kv_out.at[own_tokens, :]))
    own_q.wait()
    own_do.wait()
    for name, dst in (("q", q_all), ("do", do_all)):
        for way, zl_to, core_to in others:
            links.recv((name, way), dst.at[seq_rows(zl_to * 2 + core_to), :])
    pending.append(local(q_all, q_out))
    pending.append(local(do_all, do_out))
    links.recv("kv", kv_out.at[pl.ds(pl.multiple_of((1 - zl) * CT, CT), CT), :])
    for copy in pending:
        copy.wait()
    links.drain()


def gather(normed, queries, out_grad, master):
    return pl.pallas_call(
        gather_kernel,
        out_shape=(
            jax.ShapeDtypeStruct((SHARDS, ROWS, COLS), BF16),
            jax.ShapeDtypeStruct((D, CT), BF16),
            jax.ShapeDtypeStruct((SEQ, QW), BF16),
            jax.ShapeDtypeStruct((SEQ, QW), BF16),
            jax.ShapeDtypeStruct((SEQ, HC), BF16),
        ),
        in_specs=[ANY] * 4,
        out_specs=(ANY,) * 5,
        scratch_shapes=[
            pltpu.VMEM((SHARDS, ROWS, COLS), BF16),
            pltpu.VMEM((CT, D), BF16),
            pltpu.VMEM((D, CT), BF16),
            pltpu.VMEM((ROWS, COLS), F32),
            pltpu.VMEM((2, CT, HC), BF16),
            pltpu.VMEM((2, CT, HC), F32),
            pltpu.VMEM(queries.shape, BF16),
            pltpu.VMEM(queries.shape, BF16),
            pltpu.VMEM((SEQ, QW), BF16),
            pltpu.VMEM((SEQ, QW), BF16),
            pltpu.SemaphoreType.DMA((N_GATHER_SEMS,)),
            pltpu.SemaphoreType.DMA((N_GATHER_SEMS,)),
            pltpu.SemaphoreType.DMA((N_LOCAL_SEMS,)),
        ],
        compiler_params=pltpu.CompilerParams(
            collective_id=0, has_side_effects=True, vmem_limit_bytes=VMEM_LIMIT
        ),
        name="gather_project",
    )(normed, queries, out_grad, master)


def attention_kernel(
    lengths, q_ref, do_ref, kv_ref, dq_ref, dkv_ref,
    qs, dos, prob, dprob, prob_half, d_scores, dk_acc, dv_acc,
):
    i = pl.program_id(0)
    scale = HEAD ** (-0.5)
    to_base2 = scale * math.log2(math.e)
    ends = []
    total = lengths[0, 0]
    ends.append(total)
    for j in range(1, lengths.shape[1]):
        total = total + lengths[0, j]
        ends.append(total)

    @pl.when(i == 0)
    def _():
        dk_acc[...] = jnp.zeros_like(dk_acc)
        dv_acc[...] = jnp.zeros_like(dv_acc)

    lane = lax.broadcasted_iota(jnp.int32, (1, CHUNK), 1)
    sub = lax.broadcasted_iota(jnp.int32, (CHUNK, 1), 0)
    q_row = i * CHUNK + lane
    doc_start = jnp.zeros_like(q_row)
    first_start = jnp.int32(0)
    for e in ends:
        doc_start = jnp.where(q_row >= e, jnp.maximum(doc_start, e), doc_start)
        first_start = jnp.where(i * CHUNK >= e, jnp.maximum(first_start, e), first_start)
    lowest = lax.div(first_start, CHUNK)
    lowest = jnp.maximum(lowest, i - (N_CHUNKS - 1))
    for a in range(GROUP):
        qs[a * CHUNK : (a + 1) * CHUNK, :] = q_ref[:, a * HEAD : (a + 1) * HEAD]
        dos[a * CHUNK : (a + 1) * CHUNK, :] = do_ref[:, a * HEAD : (a + 1) * HEAD]

    def chunks(n):
        low = i + 1 - n
        keys = pl.ds(pl.multiple_of(low * CHUNK, CHUNK), n * CHUNK)
        here = slice(0, n * CHUNK)
        prob[here, :] = dot(kv_ref[keys, 0:HEAD], qs[...], ((1,), (1,)))
        dprob[here, :] = dot(kv_ref[keys, HEAD : 2 * HEAD], dos[...], ((1,), (1,)))
        for a in range(GROUP):
            cols = slice(a * CHUNK, (a + 1) * CHUNK)
            parts = []
            top = None
            for t in range(n):
                k_row = (low + t) * CHUNK + sub
                keep = k_row >= doc_start
                if t == n - 1:
                    keep = keep & (k_row <= q_row)
                part = jnp.where(keep, prob[t * CHUNK : (t + 1) * CHUNK, cols], -1e30)
                parts.append(part)
                most = jnp.max(part, axis=0, keepdims=True)
                top = most if top is None else jnp.maximum(top, most)
            mass = jnp.zeros((1, CHUNK), F32)
            delta = jnp.zeros((1, CHUNK), F32)
            for t in range(n):
                p = jnp.exp2((parts[t] - top) * to_base2)
                parts[t] = p
                mass = mass + jnp.sum(p, axis=0, keepdims=True)
                dp = dprob[t * CHUNK : (t + 1) * CHUNK, cols]
                delta = delta + jnp.sum(p * dp, axis=0, keepdims=True)
            inv = 1.0 / mass
            delta = delta * inv
            for t in range(n):
                rows = slice(t * CHUNK, (t + 1) * CHUNK)
                p = parts[t] * inv
                prob_half[rows, cols] = p.astype(BF16)
                d_scores[rows, cols] = (p * (dprob[rows, cols] - delta)).astype(BF16)
        dv_acc[keys, :] += dot(prob_half[here, :], dos[...])
        dk_acc[keys, :] += dot(d_scores[here, :], qs[...])
        dq_t = dot(kv_ref[keys, 0:HEAD], d_scores[here, :], ((0,), (0,)))
        for a in range(GROUP):
            part = dq_t[:, a * CHUNK : (a + 1) * CHUNK].T * scale
            dq_ref[:, a * HEAD : (a + 1) * HEAD] = part.astype(BF16)

    for n in range(1, N_CHUNKS + 1):
        pl.when(i + 1 - lowest == n)(functools.partial(chunks, n))

    @pl.when(i == pl.num_programs(0) - 1)
    def _():
        dkv_ref[:, 0:HEAD] = (dk_acc[...] * scale).astype(BF16)
        dkv_ref[:, HEAD : 2 * HEAD] = dv_acc[...].astype(BF16)


def attention(lengths, q, do, kv):
    return pl.pallas_call(
        attention_kernel,
        grid=(SEQ // CHUNK,),
        out_shape=(
            jax.ShapeDtypeStruct((SEQ, QW), BF16),
            jax.ShapeDtypeStruct((SEQ, HC), BF16),
        ),
        in_specs=[
            pl.BlockSpec(memory_space=pltpu.SMEM),
            pl.BlockSpec((CHUNK, QW), lambda i: (i, 0)),
            pl.BlockSpec((CHUNK, QW), lambda i: (i, 0)),
            pl.BlockSpec((SEQ, HC), lambda i: (0, 0)),
        ],
        out_specs=(
            pl.BlockSpec((CHUNK, QW), lambda i: (i, 0)),
            pl.BlockSpec((SEQ, HC), lambda i: (0, 0)),
        ),
        scratch_shapes=[
            pltpu.VMEM((LANES, HEAD), BF16),
            pltpu.VMEM((LANES, HEAD), BF16),
            pltpu.VMEM((N_CHUNKS * CHUNK, LANES), F32),
            pltpu.VMEM((N_CHUNKS * CHUNK, LANES), F32),
            pltpu.VMEM((N_CHUNKS * CHUNK, LANES), BF16),
            pltpu.VMEM((N_CHUNKS * CHUNK, LANES), BF16),
            pltpu.VMEM((SEQ, HEAD), F32),
            pltpu.VMEM((SEQ, HEAD), F32),
        ],
        compiler_params=pltpu.CompilerParams(vmem_limit_bytes=VMEM_LIMIT),
        name="attention_back",
    )(lengths, q, do, kv)


N_REDUCE_SEMS = 176


def reduce_kernel(
    xt_in, w_in, dkv_in, dq_in,
    dq_out, dn_out, grad_out,
    xt, w, term, dkv, dq_src, dq_all, z_early, z_in, l_in, mine, total, dn_send, dn_recv, dn_own,
    *rest,
):
    bufs = [rest[4 * p : 4 * p + 4] for p in range(4)]
    send_sem, recv_sem, loc_sem = rest[16:]
    here = Place()
    links = Links(send_sem, recv_sem, here)
    n_local = [0]

    def local(src, dst):
        copy = pltpu.make_async_copy(src, dst, loc_sem.at[n_local[0]])
        n_local[0] += 1
        copy.start()
        return copy

    core, zl = here.core, here.zl
    own_z, far_z = here.zh, 1 - here.zh
    own_rows = pl.ds(pl.multiple_of(core * TOK, TOK), TOK)
    far_rows = pl.ds(pl.multiple_of((1 - core) * TOK, TOK), TOK)
    own_tokens = pl.ds(pl.multiple_of(zl * CT, CT), CT)
    far_tokens = pl.ds(pl.multiple_of((1 - zl) * CT, CT), CT)

    def seq_rows(sq):
        return pl.ds(pl.multiple_of(sq * TOK, TOK), TOK)

    def head_cols(zl_of, core_of):
        return pl.ds(pl.multiple_of((core_of * 2 + zl_of) * QW, 128), QW)

    get_dkv = local(dkv_in.at[own_tokens, :], dkv.at[zl])
    offs = (2, 1, -1, 0)
    get_xt = []
    for off in offs:
        y = lax.rem(here.y + off + Y, Y)
        at = pl.ds(pl.multiple_of(y * ZH * ROW_BLOCK, 128), ZH * ROW_BLOCK)
        get_xt.append(local(xt_in.at[at, :], xt.at[at, :]))
    get_dq = local(dq_in, dq_src)
    own_dq = local(dq_in.at[seq_rows(here.sq), :], dq_all.at[:, head_cols(zl, core)])
    here.greet()
    links.send("dkv", dkv_in.at[far_tokens, :], dkv.at[zl], here.partner())
    get_w = local(w_in, w)
    pending = []
    get_dkv.wait()

    pos = {"x": here.x, "y": here.y}
    size = {"x": X, "y": Y}

    def at_axis(axis, off):
        return lax.rem(pos[axis] + off + size[axis], size[axis])

    class Ring:
        def __init__(self, name, axis, slot, opp, land):
            self.name, self.axis, self.slot = name, axis, slot
            self.opp, self.land = opp, land

        def half(self, ref, h):
            start = h * HC if isinstance(h, int) else pl.multiple_of(h * HC, HC)
            return ref.at[:, :, pl.ds(start, HC)]

        def send_far(self, h):
            links.send(
                (self.name, "far"),
                self.half(self.slot(2), h), self.opp(h), here.along(self.axis, 1 - 2 * h), h,
            )

        def send_near(self, h):
            step = 2 * h - 1
            links.send(
                (self.name, "near"),
                self.half(self.slot(step), h), self.half(self.land(1 - h), h),
                here.along(self.axis, step), h,
            )

        def forward(self):
            for h, step in ((0, 1), (1, -1)):
                links.recv((self.name, "far"), self.opp(h), h)
                here_sum = self.half(self.slot(step), h)
                here_sum[...] = (
                    here_sum[...].astype(F32) + self.opp(h)[...].astype(F32)
                ).astype(BF16)
                links.send(
                    (self.name, "sum"),
                    here_sum, self.half(self.land(h), h), here.along(self.axis, step), h,
                )

        def finish(self):
            for h in range(2):
                links.recv((self.name, "near"), self.half(self.land(1 - h), h), h)
                links.recv((self.name, "sum"), self.half(self.land(h), h), h)
            mine_ref = self.slot(0)
            mine_ref[...] = (
                mine_ref[...].astype(F32)
                + self.land(0)[...].astype(F32)
                + self.land(1)[...].astype(F32)
            ).astype(BF16)

    def rows_of(p):
        return pl.ds(SUM_PARTS[p][0], SUM_PARTS[p][1])

    def term_at(at, p):
        zs = pl.ds(0, ZH) if p in Z_FIRST else pl.ds(own_z, 1)
        return term.at[at["y"], zs, at["x"], rows_of(p), :]

    def first_ring(p, k, off):
        a, b = SUM_PARTS[p][2]
        opp, land = bufs[p][:2]

        def slot(da):
            return term_at({a: at_axis(a, da), b: at_axis(b, off)}, p)

        return Ring(
            ("first", p, k), a, slot,
            lambda h: opp.at[k, h], lambda side: land.at[k, side],
        )

    def second_ring(p):
        a, b = SUM_PARTS[p][2]
        opp, land = bufs[p][2:]

        def slot(db):
            return term_at({a: pos[a], b: at_axis(b, db)}, p)

        return Ring(("second", p), b, slot, lambda h: opp.at[h], lambda side: land.at[side])

    rings = [[first_ring(p, k, off) for k, off in enumerate(offs)] for p in range(4)]
    finals = [second_ring(p) for p in range(4)]
    late = pl.ds(SUM_PARTS[2][0], SUM_PARTS[2][1] + SUM_PARTS[3][1])

    def make_terms(k, h):
        y = at_axis("y", offs[k])
        cols = pl.ds(pl.multiple_of(h * HC, HC), HC)
        for z in (far_z, own_z):
            at = pl.ds(pl.multiple_of((y * ZH + z) * ROW_BLOCK, 128), ROW_BLOCK)
            t = dot(xt[at, :], dkv[h]).astype(BF16)
            term[y, z, :, :, cols] = t.reshape(X, ROWS, HC)
        links.send(
            ("early", k),
            term.at[y, far_z, :, late, cols], z_early.at[k, :, :, cols], here.cross(), h,
        )

    def add_early(k):
        y = at_axis("y", offs[k])
        for h in range(2):
            links.recv(("early", k), z_early.at[k, :, :, pl.ds(h * HC, HC)], h)
        into = term.at[y, own_z, :, late, :]
        into[...] = (into[...].astype(F32) + z_early[k].astype(F32)).astype(BF16)

    def launch(k, p_x, p_y, h):
        rings[p_x][k].send_far(h)
        rings[p_x][k].send_near(h)
        for piece in rings[p_y]:
            if k == 0:
                piece.send_far(h)
            elif k == 2:
                piece.send_near(h)

    def dn_far(t):
        at = pl.ds(t * ROW_BLOCK, ROW_BLOCK)
        partial = jnp.zeros((TOK, ROW_BLOCK), F32)
        for h in range(2):
            w_t = w[pl.ds(t * X, X), :, h * HC : (h + 1) * HC].reshape(ROW_BLOCK, HC)
            partial += dot(dkv[h, far_rows, :], w_t, ((1,), (1,)))
        dn_send[:, at] = partial.astype(BF16)
        links.send(("dn", t), dn_send.at[:, at], dn_recv.at[:, at], here.other_core())

    def dn_near(t):
        at = pl.ds(t * ROW_BLOCK, ROW_BLOCK)
        links.recv(("dn", t), dn_recv.at[:, at])
        partial = dn_recv[:, at].astype(F32)
        for h in range(2):
            w_t = w[pl.ds(t * X, X), :, h * HC : (h + 1) * HC].reshape(ROW_BLOCK, HC)
            partial += dot(dkv[h, own_rows, :], w_t, ((1,), (1,)))
        dn_own[:, at] = partial.astype(BF16)
        pending.append(local(dn_own.at[:, at], dn_out.at[:, at]))

    for k in range(4):
        get_xt[k].wait()
        make_terms(k, zl)
        launch(k, 0, 1, zl)
    links.recv("dkv", dkv.at[1 - zl])
    for k in range(4):
        make_terms(k, 1 - zl)
        launch(k, 0, 1, 1 - zl)
    get_dq.wait()
    others = (("p", 1 - zl, core), ("c", zl, 1 - core), ("d", 1 - zl, 1 - core))
    for way, zl_to, core_to in others:
        links.send(
            ("dq", way),
            dq_src.at[seq_rows(zl_to * 2 + core_to), :], dq_all.at[:, head_cols(zl, core)],
            here.dev(zl=zl_to, core=core_to),
        )
    get_w.wait()
    for k in range(4):
        for p in Z_FIRST:
            rings[p][k].forward()
        add_early(k)
        for h in range(2):
            launch(k, 2, 3, h)
        dn_far(2 * k)
        dn_far(2 * k + 1)

    def end_first(k, parts):
        for p in parts:
            rings[p][k].finish()
            for h in range(2):
                if k == 0:
                    finals[p].send_far(h)
                elif k < 3 and offs[k] == 2 * h - 1:
                    finals[p].send_near(h)

    for k in range(4):
        for p in Z_LAST:
            rings[p][k].forward()
        end_first(k, Z_FIRST)
        dn_near(2 * k)
        dn_near(2 * k + 1)
    for p in Z_FIRST:
        finals[p].forward()
    for k in range(4):
        end_first(k, Z_LAST)
    for p in Z_FIRST:
        finals[p].finish()
        rows = rows_of(p)
        links.send(
            ("z", p), term.at[here.y, far_z, here.x, rows, :], z_in.at[rows, :], here.cross()
        )
    for p in Z_LAST:
        finals[p].forward()

    def to_partner(p):
        rows = rows_of(p)
        links.send(("l", p), mine.at[rows, :], l_in.at[rows, :], here.partner())

    for p in Z_FIRST:
        rows = rows_of(p)
        links.recv(("z", p), z_in.at[rows, :])
        mine[rows, :] = (
            term[here.y, own_z, here.x, rows, :].astype(F32) + z_in[rows, :].astype(F32)
        ).astype(BF16)
        to_partner(p)
    for p in Z_LAST:
        finals[p].finish()
        rows = rows_of(p)
        mine[rows, :] = term[here.y, own_z, here.x, rows, :]
        to_partner(p)
    for p in range(4):
        rows = rows_of(p)
        links.recv(("l", p), l_in.at[rows, :])
        total[core, rows, :] = mine[rows, :].astype(F32) + l_in[rows, :].astype(F32)
        links.send(
            ("c", p), total.at[core, rows, :], total.at[core, rows, :], here.other_core()
        )
    own_dq.wait()
    for way, zl_to, core_to in others:
        links.recv(("dq", way), dq_all.at[:, head_cols(zl_to, core_to)])
    pending.append(local(dq_all, dq_out))
    for p in range(4):
        links.recv(("c", p), total.at[1 - core, rows_of(p), :])
    pending.append(local(total, grad_out))
    for copy in pending:
        copy.wait()
    links.drain()


def reduce_terms(xt, w, dkv, dq):
    rings = []
    for p, (_, rows, _, both) in enumerate(SUM_PARTS):
        nz = ZH if both else 1
        rings += [
            pltpu.VMEM((4, 2, nz, rows, HC), BF16),
            pltpu.VMEM((4, 2, nz, rows, COLS), BF16),
            pltpu.VMEM((2, nz, rows, HC), BF16),
            pltpu.VMEM((2, nz, rows, COLS), BF16),
        ]
    late = SUM_PARTS[2][1] + SUM_PARTS[3][1]
    return pl.pallas_call(
        reduce_kernel,
        out_shape=(
            jax.ShapeDtypeStruct((TOK, 4 * QW), BF16),
            jax.ShapeDtypeStruct((TOK, D), BF16),
            jax.ShapeDtypeStruct((2, ROWS, COLS), F32),
        ),
        in_specs=[ANY] * 4,
        out_specs=(ANY,) * 3,
        scratch_shapes=[
            pltpu.VMEM((D, CT), BF16),
            pltpu.VMEM((SHARDS, ROWS, COLS), BF16),
            pltpu.VMEM((Y, ZH, X, ROWS, COLS), BF16),
            pltpu.VMEM((2, CT, HC), BF16),
            pltpu.VMEM((SEQ, QW), BF16),
            pltpu.VMEM((TOK, 4 * QW), BF16),
            pltpu.VMEM((4, X, late, COLS), BF16),
            pltpu.VMEM((ROWS, COLS), BF16),
            pltpu.VMEM((ROWS, COLS), BF16),
            pltpu.VMEM((ROWS, COLS), BF16),
            pltpu.VMEM((2, ROWS, COLS), F32),
            pltpu.VMEM((TOK, D), BF16),
            pltpu.VMEM((TOK, D), BF16),
            pltpu.VMEM((TOK, D), BF16),
            *rings,
            pltpu.SemaphoreType.DMA((N_REDUCE_SEMS,)),
            pltpu.SemaphoreType.DMA((N_REDUCE_SEMS,)),
            pltpu.SemaphoreType.DMA((N_LOCAL_SEMS,)),
        ],
        compiler_params=pltpu.CompilerParams(
            collective_id=1, has_side_effects=True, vmem_limit_bytes=VMEM_LIMIT
        ),
        name="reduce_terms",
    )(xt, w, dkv, dq)


def update_kernel(
    tokens, dq_in, dn_in, total_in, master_in, one_in, two_in,
    dq_out, dn_out, master_out, one_out, two_out,
    dq, dn, total, master, one, two, in_sem, out_sem,
):
    gets, puts = [], []

    def get(src, dst):
        copy = pltpu.make_async_copy(src, dst, in_sem.at[len(gets)])
        copy.start()
        gets.append(copy)
        return copy

    def put(src, dst):
        copy = pltpu.make_async_copy(src, dst, out_sem.at[len(puts)])
        copy.start()
        puts.append(copy)

    first_gets = [get(total_in, total), get(master_in, master), get(one_in, one), get(two_in, two)]
    blocks = []
    for src, mid, dst, n in ((dn_in, dn, dn_out, 4), (dq_in, dq, dq_out, 2)):
        rows = src.shape[0] // n
        for b in range(n):
            at = pl.ds(b * rows, rows)
            blocks.append((get(src.at[at, :], mid.at[at, :]), mid.at[at, :], dst.at[at, :]))
    for copy in first_gets:
        copy.wait()
    rows = ROWS // 2
    for b in range(2):
        at = pl.ds(b * rows, rows)
        for h in range(2):
            cols = pl.ds(h * COLS, COLS)
            grad = total[h, at, :] * float(tokens) ** (-0.5)
            first = 0.9 * one[at, cols].astype(F32) + 0.1 * grad
            second = 0.999 * two[at, cols].astype(F32) + 0.001 * grad * grad
            master[at, cols] = master[at, cols] - 0.001 * (first / (1.0 - 0.9**3)) / (
                jnp.sqrt(second / (1.0 - 0.999**3)) + 1e-08
            )
            one[at, cols] = first.astype(BF16)
            two[at, cols] = second.astype(BF16)
        for mid, dst in ((master, master_out), (one, one_out), (two, two_out)):
            put(mid.at[at, :], dst.at[at, :])
        for copy, mid, dst in blocks[3 * b : 3 * b + 3]:
            copy.wait()
            put(mid, dst)
    for copy in puts:
        copy.wait()


def update(tokens, dq, dn, total, master, moment_one, moment_two):
    results = (dq, dn, master, moment_one, moment_two)
    return pl.pallas_call(
        functools.partial(update_kernel, tokens),
        out_shape=tuple(jax.ShapeDtypeStruct(a.shape, a.dtype) for a in results),
        in_specs=[ANY] * 6,
        out_specs=(ANY,) * 5,
        scratch_shapes=[
            *[pltpu.VMEM(a.shape, a.dtype) for a in (dq, dn, total, master, moment_one, moment_two)],
            pltpu.SemaphoreType.DMA((12,)),
            pltpu.SemaphoreType.DMA((12,)),
        ],
        compiler_params=pltpu.CompilerParams(vmem_limit_bytes=VMEM_LIMIT),
        name="update",
    )(dq, dn, total, master, moment_one, moment_two)


def on_device(normed, queries, output_gradient, doc_lengths, master, moment_one, moment_two):
    w, xt, q, do, kv = gather(normed, queries, output_gradient, master)
    dq, dkv = attention(doc_lengths, q, do, kv)
    dq, dn, total = reduce_terms(xt, w, dkv, dq)
    tokens = normed.shape[0] * lax.axis_size("dp") * lax.axis_size("seq")
    return update(tokens, dq, dn, total, master, moment_one, moment_two)


def solution(mesh):
    rows = P(("dp", "seq"), None)
    shard = P("dp", None)
    return jax.shard_map(
        on_device,
        mesh=mesh,
        in_specs=(rows, rows, rows, shard, shard, shard, shard),
        out_specs=(rows, rows, shard, shard, shard),
        check_vma=False,
    )
```

```python
import functools
import math

import jax
import jax.numpy as jnp
from jax import lax
from jax.experimental import pallas as pl
from jax.experimental.pallas import tpu as pltpu
from jax.sharding import PartitionSpec as P

HEAD = 128
GROUP = 7
X, Y, ZH = 4, 4, 2
TOK = 256
CT = 512
D = 7168
SHARDS = X * Y * ZH
ROWS = D // SHARDS
PARTS = (
    (0, 96, ("x", "y"), True),
    (96, 80, ("y", "x"), True),
    (176, 16, ("x", "y"), False),
    (192, 32, ("y", "x"), False),
)
SUM_PARTS = (
    (0, 80, ("x", "y"), True),
    (80, 80, ("y", "x"), True),
    (160, 32, ("x", "y"), False),
    (192, 32, ("y", "x"), False),
)
Z_FIRST = (0, 1)
Z_LAST = (2, 3)
SEQ = 1024
COLS = 512
HC = COLS // 2
QW = 896
ROW_BLOCK = X * ROWS
N_BLOCKS = Y * ZH
CHUNK = 128
N_CHUNKS = 5
LANES = GROUP * CHUNK
VMEM_LIMIT = 58 * 1024 * 1024
MESH = pl.DeviceIdType.MESH
ANY = pl.BlockSpec(memory_space=pl.ANY)
F32 = jnp.float32
BF16 = jnp.bfloat16


def dot(a, b, dims=((1,), (0,))):
    return lax.dot_general(a, b, (dims, ((), ())), preferred_element_type=F32)


class Place:
    def __init__(self):
        dp = lax.axis_index("dp")
        sq = lax.axis_index("seq")
        self.dp, self.sq = dp, sq
        self.x = lax.rem(dp, X)
        self.zh = lax.rem(lax.div(dp, X), ZH)
        self.y = lax.div(dp, X * ZH)
        self.core = lax.rem(sq, 2)
        self.zl = lax.div(sq, 2)

    def dev(self, x=None, y=None, zh=None, zl=None, core=None):
        x = self.x if x is None else x
        y = self.y if y is None else y
        zh = self.zh if zh is None else zh
        zl = self.zl if zl is None else zl
        core = self.core if core is None else core
        return ((y * ZH + zh) * X + x, zl * 2 + core)

    def along(self, axis, step):
        if axis == "x":
            return self.dev(x=lax.rem(self.x + step + X, X))
        return self.dev(y=lax.rem(self.y + step + Y, Y))

    def cross(self):
        return self.dev(zh=1 - self.zh, zl=1 - self.zl)

    def partner(self):
        return self.dev(zl=1 - self.zl)

    def other_core(self):
        return self.dev(core=1 - self.core)

    def greet(self):
        barrier = pltpu.get_barrier_semaphore()
        near = [self.along(a, s) for a in ("x", "y") for s in (1, -1)]
        near += [self.cross(), self.partner(), self.other_core()]
        near.append(self.dev(zl=1 - self.zl, core=1 - self.core))
        for d in near:
            pl.semaphore_signal(barrier, inc=1, device_id=d, device_id_type=MESH)
        return len(near)

    def all_in(self, count):
        pl.semaphore_wait(pltpu.get_barrier_semaphore(), count)


class Links:
    def __init__(self, send_sem, recv_sem, place):
        self.send_sem, self.recv_sem, self.place = send_sem, recv_sem, place
        self.index = {}
        self.used = 0
        self.sent = []

    def _copy(self, key, src, dst, dev, half=None):
        if key not in self.index:
            self.index[key] = self.used
            self.used += 1 if half is None else 2
        k = self.index[key] + (0 if half is None else half)
        return pltpu.make_async_remote_copy(
            src_ref=src,
            dst_ref=dst,
            send_sem=self.send_sem.at[k],
            recv_sem=self.recv_sem.at[k],
            device_id=dev,
            device_id_type=MESH,
        )

    def send(self, key, src, dst, dev, half=None):
        copy = self._copy(key, src, dst, dev, half)
        copy.start()
        self.sent.append(copy)

    def recv(self, key, dst, half=None):
        self._copy(key, dst, dst, self.place.other_core(), half).wait_recv()

    def drain(self):
        for copy in self.sent:
            copy.wait_send()


N_GATHER_SEMS = 176
N_LOCAL_SEMS = 40


def gather_kernel(
    normed, queries, out_grad, master,
    w_out, xt_out, q_out, do_out, kv_out,
    w, xs, xt, mas, kv, acc, q_src, do_src, q_all, do_all, send_sem, recv_sem, loc_sem,
):
    here = Place()
    links = Links(send_sem, recv_sem, here)
    n_local = [0]

    def local(src, dst):
        copy = pltpu.make_async_copy(src, dst, loc_sem.at[n_local[0]])
        n_local[0] += 1
        copy.start()
        return copy

    core, zl = here.core, here.zl
    own_rows = pl.ds(pl.multiple_of(core * TOK, TOK), TOK)
    far_rows = pl.ds(pl.multiple_of((1 - core) * TOK, TOK), TOK)

    def seq_rows(sq):
        return pl.ds(pl.multiple_of(sq * TOK, TOK), TOK)

    def head_cols(zl_to, core_to):
        return pl.ds(pl.multiple_of((core_to * 2 + zl_to) * QW, 128), QW)

    get_master = local(master.at[:, pl.ds(pl.multiple_of(core * COLS, COLS), COLS)], mas)
    get_q = local(queries, q_src)
    get_do = local(out_grad, do_src)
    own_normed = local(normed, xs.at[own_rows, :])
    own_q = local(queries.at[:, head_cols(zl, core)], q_all.at[seq_rows(here.sq), :])
    own_do = local(out_grad.at[:, head_cols(zl, core)], do_all.at[seq_rows(here.sq), :])
    pending = []
    count = here.greet()
    own = (here.y * ZH + here.zh) * X + here.x
    get_master.wait()
    w[own] = mas[...].astype(BF16)
    get_q.wait()
    get_do.wait()
    here.all_in(count)
    others = (("p", 1 - zl, core), ("d", 1 - zl, 1 - core), ("c", zl, 1 - core))

    def send_heads(ways):
        for name, src, dst in (("q", q_src, q_all), ("do", do_src, do_all)):
            for way, zl_to, core_to in ways:
                links.send(
                    (name, way),
                    src.at[:, head_cols(zl_to, core_to)], dst.at[seq_rows(here.sq), :],
                    here.dev(zl=zl_to, core=core_to),
                )

    send_heads(others[:2])
    pos = {"x": here.x, "y": here.y}
    size = {"x": X, "y": Y}

    def at_axis(axis, off):
        return lax.rem(pos[axis] + off + size[axis], size[axis])

    def slot(p, da, db, zr, half=None):
        row, rows, axes, _ = PARTS[p]
        at = {axes[0]: at_axis(axes[0], da), axes[1]: at_axis(axes[1], db)}
        zh = here.zh if zr == 0 else 1 - here.zh
        s = (at["y"] * ZH + zh) * X + at["x"]
        cols = pl.ds(0, COLS) if half is None else pl.ds(half * HC, HC)
        return w.at[s, pl.ds(row, rows), cols]

    def send(key, ref, dev):
        links.send(key, ref, ref, dev)

    def second_from(p, da, zr):
        b = PARTS[p][2][1]
        for step in (1, -1):
            send(("b", p, zr, da, step, 0), slot(p, da, 0, zr), here.along(b, step))

    def start(parts, zr):
        for p in parts:
            a = PARTS[p][2][0]
            for step in (1, -1):
                send(("a", p, zr, step, 0), slot(p, 0, 0, zr), here.along(a, step))
        for p in parts:
            second_from(p, 0, zr)

    def over_z(p, da, db):
        if p in Z_LAST:
            send(("z", p, da, db), slot(p, da, db, 0), here.cross())

    def forward_first(parts, zr):
        for p in parts:
            a = PARTS[p][2][0]
            for step in (1, -1):
                links.recv(("a", p, zr, step, 0), slot(p, -step, 0, zr))
                half = 0 if step == 1 else 1
                send(("a", p, zr, step, 1), slot(p, -step, 0, zr, half), here.along(a, step))
            for step in (1, -1):
                second_from(p, -step, zr)
                over_z(p, -step, 0)

    def finish_first(parts, zr):
        for p in parts:
            for step in (1, -1):
                half = 0 if step == 1 else 1
                links.recv(("a", p, zr, step, 1), slot(p, 2, 0, zr, half))
            second_from(p, 2, zr)
            over_z(p, 2, 0)

    def forward_second(parts, zr, after=None):
        for k, da in enumerate((0, -1, 1, 2)):
            for p in parts:
                b = PARTS[p][2][1]
                for step in (1, -1):
                    links.recv(("b", p, zr, da, step, 0), slot(p, da, -step, zr))
                    half = 0 if step == 1 else 1
                    send(
                        ("b", p, zr, da, step, 1),
                        slot(p, da, -step, zr, half),
                        here.along(b, step),
                    )
                    over_z(p, da, -step)
            if after is not None:
                after(k)

    def finish_second(parts, zr):
        for da in (0, -1, 1, 2):
            for p in parts:
                for step in (1, -1):
                    half = 0 if step == 1 else 1
                    links.recv(("b", p, zr, da, step, 1), slot(p, da, 2, zr, half))
                over_z(p, da, 2)

    def turn(first, last):
        @pl.loop(first, last)
        def _(b):
            at = pl.ds(pl.multiple_of(b * HEAD, HEAD), HEAD)
            xt[at, :] = xs[:, at].T

    start(Z_LAST, 0)
    start(Z_FIRST, 0)
    for p in Z_FIRST:
        send(("z", p), slot(p, 0, 0, 0), here.cross())
    for p in Z_LAST:
        over_z(p, 0, 0)
    links.send("normed", normed, xs.at[own_rows, :], here.other_core())
    send_heads(others[2:])
    forward_first(Z_LAST, 0)
    forward_first(Z_FIRST, 0)
    finish_first(Z_LAST, 0)
    for p in Z_FIRST:
        links.recv(("z", p), slot(p, 0, 0, 1))
    start(Z_FIRST, 1)
    finish_first(Z_FIRST, 0)
    own_normed.wait()
    links.recv("normed", xs.at[far_rows, :])
    turn(0, 14)
    forward_second(Z_LAST, 0)
    forward_first(Z_FIRST, 1)
    turn(14, 28)
    finish_second(Z_LAST, 0)
    finish_first(Z_FIRST, 1)
    turn(28, 42)
    forward_second(Z_FIRST, 0)
    turn(42, 56)
    pending.append(local(xt, xt_out))
    finish_second(Z_FIRST, 0)
    acc[...] = jnp.zeros_like(acc)

    def project(y, zh, cols, into):
        at = pl.ds(pl.multiple_of((y * ZH + zh) * ROW_BLOCK, 128), ROW_BLOCK)
        w_t = w[pl.ds((y * ZH + zh) * X, X), :, cols].reshape(ROW_BLOCK, HC)
        acc[into] += dot(xs[:, at], w_t)

    own_head = pl.ds(pl.multiple_of(zl * HC, HC), HC)
    far_head = pl.ds(pl.multiple_of((1 - zl) * HC, HC), HC)

    def own_half(k):
        project(k, here.zh, far_head, 0)
        project(k, here.zh, own_head, 1)

    forward_second(Z_FIRST, 1, own_half)
    finish_second(Z_FIRST, 1)
    for p in Z_LAST:
        for da in (0, -1, 1, 2):
            for db in (0, -1, 1, 2):
                links.recv(("z", p, da, db), slot(p, da, db, 1))
    pending.append(local(w, w_out))

    own_tokens = pl.ds(pl.multiple_of(zl * CT, CT), CT)
    for into, cols in ((0, far_head), (1, own_head)):

        @pl.loop(0, Y)
        def _(y):
            project(y, 1 - here.zh, cols, into)

        kv[into] = acc[into].astype(BF16)
        if into == 0:
            links.send("kv", kv.at[0], kv_out.at[own_tokens, :], here.partner())
        else:
            pending.append(local(kv.at[1], kv_out.at[own_tokens, :]))
    own_q.wait()
    own_do.wait()
    for name, dst in (("q", q_all), ("do", do_all)):
        for way, zl_to, core_to in others:
            links.recv((name, way), dst.at[seq_rows(zl_to * 2 + core_to), :])
    pending.append(local(q_all, q_out))
    pending.append(local(do_all, do_out))
    links.recv("kv", kv_out.at[pl.ds(pl.multiple_of((1 - zl) * CT, CT), CT), :])
    for copy in pending:
        copy.wait()
    links.drain()


def gather(normed, queries, out_grad, master):
    return pl.pallas_call(
        gather_kernel,
        out_shape=(
            jax.ShapeDtypeStruct((SHARDS, ROWS, COLS), BF16),
            jax.ShapeDtypeStruct((D, CT), BF16),
            jax.ShapeDtypeStruct((SEQ, QW), BF16),
            jax.ShapeDtypeStruct((SEQ, QW), BF16),
            jax.ShapeDtypeStruct((SEQ, HC), BF16),
        ),
        in_specs=[ANY] * 4,
        out_specs=(ANY,) * 5,
        scratch_shapes=[
            pltpu.VMEM((SHARDS, ROWS, COLS), BF16),
            pltpu.VMEM((CT, D), BF16),
            pltpu.VMEM((D, CT), BF16),
            pltpu.VMEM((ROWS, COLS), F32),
            pltpu.VMEM((2, CT, HC), BF16),
            pltpu.VMEM((2, CT, HC), F32),
            pltpu.VMEM(queries.shape, BF16),
            pltpu.VMEM(queries.shape, BF16),
            pltpu.VMEM((SEQ, QW), BF16),
            pltpu.VMEM((SEQ, QW), BF16),
            pltpu.SemaphoreType.DMA((N_GATHER_SEMS,)),
            pltpu.SemaphoreType.DMA((N_GATHER_SEMS,)),
            pltpu.SemaphoreType.DMA((N_LOCAL_SEMS,)),
        ],
        compiler_params=pltpu.CompilerParams(
            collective_id=0, has_side_effects=True, vmem_limit_bytes=VMEM_LIMIT
        ),
        name="gather_project",
    )(normed, queries, out_grad, master)


def attention_kernel(
    lengths, q_ref, do_ref, kv_ref, dq_ref, dkv_ref,
    qs, dos, prob, dprob, prob_half, d_scores, dk_acc, dv_acc,
):
    i = pl.program_id(0)
    scale = HEAD ** (-0.5)
    to_base2 = scale * math.log2(math.e)
    ends = []
    total = lengths[0, 0]
    ends.append(total)
    for j in range(1, lengths.shape[1]):
        total = total + lengths[0, j]
        ends.append(total)

    @pl.when(i == 0)
    def _():
        dk_acc[...] = jnp.zeros_like(dk_acc)
        dv_acc[...] = jnp.zeros_like(dv_acc)

    lane = lax.broadcasted_iota(jnp.int32, (1, CHUNK), 1)
    sub = lax.broadcasted_iota(jnp.int32, (CHUNK, 1), 0)
    q_row = i * CHUNK + lane
    doc_start = jnp.zeros_like(q_row)
    first_start = jnp.int32(0)
    for e in ends:
        doc_start = jnp.where(q_row >= e, jnp.maximum(doc_start, e), doc_start)
        first_start = jnp.where(i * CHUNK >= e, jnp.maximum(first_start, e), first_start)
    lowest = lax.div(first_start, CHUNK)
    lowest = jnp.maximum(lowest, i - (N_CHUNKS - 1))
    for a in range(GROUP):
        qs[a * CHUNK : (a + 1) * CHUNK, :] = q_ref[:, a * HEAD : (a + 1) * HEAD]
        dos[a * CHUNK : (a + 1) * CHUNK, :] = do_ref[:, a * HEAD : (a + 1) * HEAD]

    def chunks(n):
        low = i + 1 - n
        keys = pl.ds(pl.multiple_of(low * CHUNK, CHUNK), n * CHUNK)
        here = slice(0, n * CHUNK)
        prob[here, :] = dot(kv_ref[keys, 0:HEAD], qs[...], ((1,), (1,)))
        dprob[here, :] = dot(kv_ref[keys, HEAD : 2 * HEAD], dos[...], ((1,), (1,)))
        for a in range(GROUP):
            cols = slice(a * CHUNK, (a + 1) * CHUNK)
            parts = []
            top = None
            for t in range(n):
                k_row = (low + t) * CHUNK + sub
                keep = k_row >= doc_start
                if t == n - 1:
                    keep = keep & (k_row <= q_row)
                part = jnp.where(keep, prob[t * CHUNK : (t + 1) * CHUNK, cols], -1e30)
                parts.append(part)
                most = jnp.max(part, axis=0, keepdims=True)
                top = most if top is None else jnp.maximum(top, most)
            mass = jnp.zeros((1, CHUNK), F32)
            delta = jnp.zeros((1, CHUNK), F32)
            for t in range(n):
                p = jnp.exp2((parts[t] - top) * to_base2)
                parts[t] = p
                mass = mass + jnp.sum(p, axis=0, keepdims=True)
                dp = dprob[t * CHUNK : (t + 1) * CHUNK, cols]
                delta = delta + jnp.sum(p * dp, axis=0, keepdims=True)
            inv = 1.0 / mass
            delta = delta * inv
            for t in range(n):
                rows = slice(t * CHUNK, (t + 1) * CHUNK)
                p = parts[t] * inv
                prob_half[rows, cols] = p.astype(BF16)
                d_scores[rows, cols] = (p * (dprob[rows, cols] - delta)).astype(BF16)
        dv_acc[keys, :] += dot(prob_half[here, :], dos[...])
        dk_acc[keys, :] += dot(d_scores[here, :], qs[...])
        dq_t = dot(kv_ref[keys, 0:HEAD], d_scores[here, :], ((0,), (0,)))
        for a in range(GROUP):
            part = (dq_t[:, a * CHUNK : (a + 1) * CHUNK] * scale).astype(BF16)
            dq_ref[:, a * HEAD : (a + 1) * HEAD] = part.T

    for n in range(1, N_CHUNKS + 1):
        pl.when(i + 1 - lowest == n)(functools.partial(chunks, n))

    @pl.when(i == pl.num_programs(0) - 1)
    def _():
        dkv_ref[:, 0:HEAD] = (dk_acc[...] * scale).astype(BF16)
        dkv_ref[:, HEAD : 2 * HEAD] = dv_acc[...].astype(BF16)


def attention(lengths, q, do, kv):
    return pl.pallas_call(
        attention_kernel,
        grid=(SEQ // CHUNK,),
        out_shape=(
            jax.ShapeDtypeStruct((SEQ, QW), BF16),
            jax.ShapeDtypeStruct((SEQ, HC), BF16),
        ),
        in_specs=[
            pl.BlockSpec(memory_space=pltpu.SMEM),
            pl.BlockSpec((CHUNK, QW), lambda i: (i, 0)),
            pl.BlockSpec((CHUNK, QW), lambda i: (i, 0)),
            pl.BlockSpec((SEQ, HC), lambda i: (0, 0)),
        ],
        out_specs=(
            pl.BlockSpec((CHUNK, QW), lambda i: (i, 0)),
            pl.BlockSpec((SEQ, HC), lambda i: (0, 0)),
        ),
        scratch_shapes=[
            pltpu.VMEM((LANES, HEAD), BF16),
            pltpu.VMEM((LANES, HEAD), BF16),
            pltpu.VMEM((N_CHUNKS * CHUNK, LANES), F32),
            pltpu.VMEM((N_CHUNKS * CHUNK, LANES), F32),
            pltpu.VMEM((N_CHUNKS * CHUNK, LANES), BF16),
            pltpu.VMEM((N_CHUNKS * CHUNK, LANES), BF16),
            pltpu.VMEM((SEQ, HEAD), F32),
            pltpu.VMEM((SEQ, HEAD), F32),
        ],
        compiler_params=pltpu.CompilerParams(vmem_limit_bytes=VMEM_LIMIT),
        name="attention_back",
    )(lengths, q, do, kv)


N_REDUCE_SEMS = 176


def reduce_kernel(
    xt_in, w_in, dkv_in, dq_in,
    dq_out, dn_out, grad_out,
    xt, w, term, dkv, dq_src, dq_all, z_early, z_in, l_in, mine, total, dn_send, dn_recv, dn_own,
    *rest,
):
    bufs = [rest[4 * p : 4 * p + 4] for p in range(4)]
    send_sem, recv_sem, loc_sem = rest[16:]
    here = Place()
    links = Links(send_sem, recv_sem, here)
    n_local = [0]

    def local(src, dst):
        copy = pltpu.make_async_copy(src, dst, loc_sem.at[n_local[0]])
        n_local[0] += 1
        copy.start()
        return copy

    core, zl = here.core, here.zl
    own_z, far_z = here.zh, 1 - here.zh
    own_rows = pl.ds(pl.multiple_of(core * TOK, TOK), TOK)
    far_rows = pl.ds(pl.multiple_of((1 - core) * TOK, TOK), TOK)
    own_tokens = pl.ds(pl.multiple_of(zl * CT, CT), CT)
    far_tokens = pl.ds(pl.multiple_of((1 - zl) * CT, CT), CT)

    def seq_rows(sq):
        return pl.ds(pl.multiple_of(sq * TOK, TOK), TOK)

    def head_cols(zl_of, core_of):
        return pl.ds(pl.multiple_of((core_of * 2 + zl_of) * QW, 128), QW)

    get_dkv = local(dkv_in.at[own_tokens, :], dkv.at[zl])
    offs = (2, 1, -1, 0)
    get_xt = []
    for off in offs:
        y = lax.rem(here.y + off + Y, Y)
        at = pl.ds(pl.multiple_of(y * ZH * ROW_BLOCK, 128), ZH * ROW_BLOCK)
        get_xt.append(local(xt_in.at[at, :], xt.at[at, :]))
    get_dq = local(dq_in, dq_src)
    own_dq = local(dq_in.at[seq_rows(here.sq), :], dq_all.at[:, head_cols(zl, core)])
    count = here.greet()
    get_w = local(w_in, w)
    pending = []
    get_dkv.wait()

    pos = {"x": here.x, "y": here.y}
    size = {"x": X, "y": Y}

    def at_axis(axis, off):
        return lax.rem(pos[axis] + off + size[axis], size[axis])

    class Ring:
        def __init__(self, name, axis, slot, opp, land):
            self.name, self.axis, self.slot = name, axis, slot
            self.opp, self.land = opp, land

        def half(self, ref, h):
            start = h * HC if isinstance(h, int) else pl.multiple_of(h * HC, HC)
            return ref.at[:, :, pl.ds(start, HC)]

        def send_far(self, h):
            links.send(
                (self.name, "far"),
                self.half(self.slot(2), h), self.opp(h), here.along(self.axis, 1 - 2 * h), h,
            )

        def send_near(self, h):
            step = 2 * h - 1
            links.send(
                (self.name, "near"),
                self.half(self.slot(step), h), self.half(self.land(1 - h), h),
                here.along(self.axis, step), h,
            )

        def forward(self):
            for h, step in ((0, 1), (1, -1)):
                links.recv((self.name, "far"), self.opp(h), h)
                here_sum = self.half(self.slot(step), h)
                here_sum[...] = (
                    here_sum[...].astype(F32) + self.opp(h)[...].astype(F32)
                ).astype(BF16)
                links.send(
                    (self.name, "sum"),
                    here_sum, self.half(self.land(h), h), here.along(self.axis, step), h,
                )

        def finish(self):
            for h in range(2):
                links.recv((self.name, "near"), self.half(self.land(1 - h), h), h)
                links.recv((self.name, "sum"), self.half(self.land(h), h), h)
            mine_ref = self.slot(0)
            mine_ref[...] = (
                mine_ref[...].astype(F32)
                + self.land(0)[...].astype(F32)
                + self.land(1)[...].astype(F32)
            ).astype(BF16)

    def rows_of(p):
        return pl.ds(SUM_PARTS[p][0], SUM_PARTS[p][1])

    def term_at(at, p):
        zs = pl.ds(0, ZH) if p in Z_FIRST else pl.ds(own_z, 1)
        return term.at[at["y"], zs, at["x"], rows_of(p), :]

    def first_ring(p, k, off):
        a, b = SUM_PARTS[p][2]
        opp, land = bufs[p][:2]

        def slot(da):
            return term_at({a: at_axis(a, da), b: at_axis(b, off)}, p)

        return Ring(
            ("first", p, k), a, slot,
            lambda h: opp.at[k, h], lambda side: land.at[k, side],
        )

    def second_ring(p):
        a, b = SUM_PARTS[p][2]
        opp, land = bufs[p][2:]

        def slot(db):
            return term_at({a: pos[a], b: at_axis(b, db)}, p)

        return Ring(("second", p), b, slot, lambda h: opp.at[h], lambda side: land.at[side])

    rings = [[first_ring(p, k, off) for k, off in enumerate(offs)] for p in range(4)]
    finals = [second_ring(p) for p in range(4)]
    late = pl.ds(SUM_PARTS[2][0], SUM_PARTS[2][1] + SUM_PARTS[3][1])

    def make_terms(k, h):
        y = at_axis("y", offs[k])
        cols = pl.ds(pl.multiple_of(h * HC, HC), HC)
        for z in (far_z, own_z):
            at = pl.ds(pl.multiple_of((y * ZH + z) * ROW_BLOCK, 128), ROW_BLOCK)
            t = dot(xt[at, :], dkv[h]).astype(BF16)
            term[y, z, :, :, cols] = t.reshape(X, ROWS, HC)

    def send_early(k, h):
        y = at_axis("y", offs[k])
        cols = pl.ds(pl.multiple_of(h * HC, HC), HC)
        links.send(
            ("early", k),
            term.at[y, far_z, :, late, cols], z_early.at[k, :, :, cols], here.cross(), h,
        )

    def add_early(k):
        y = at_axis("y", offs[k])
        for h in range(2):
            links.recv(("early", k), z_early.at[k, :, :, pl.ds(h * HC, HC)], h)
        into = term.at[y, own_z, :, late, :]
        into[...] = (into[...].astype(F32) + z_early[k].astype(F32)).astype(BF16)

    def launch(k, p_x, p_y, h):
        rings[p_x][k].send_far(h)
        rings[p_x][k].send_near(h)
        for piece in rings[p_y]:
            if k == 0:
                piece.send_far(h)
            elif k == 2:
                piece.send_near(h)

    def dn_far(t):
        at = pl.ds(t * ROW_BLOCK, ROW_BLOCK)
        partial = jnp.zeros((TOK, ROW_BLOCK), F32)
        for h in range(2):
            w_t = w[pl.ds(t * X, X), :, h * HC : (h + 1) * HC].reshape(ROW_BLOCK, HC)
            partial += dot(dkv[h, far_rows, :], w_t, ((1,), (1,)))
        dn_send[:, at] = partial.astype(BF16)
        links.send(("dn", t), dn_send.at[:, at], dn_recv.at[:, at], here.other_core())

    def dn_near(t):
        at = pl.ds(t * ROW_BLOCK, ROW_BLOCK)
        links.recv(("dn", t), dn_recv.at[:, at])
        partial = dn_recv[:, at].astype(F32)
        for h in range(2):
            w_t = w[pl.ds(t * X, X), :, h * HC : (h + 1) * HC].reshape(ROW_BLOCK, HC)
            partial += dot(dkv[h, own_rows, :], w_t, ((1,), (1,)))
        dn_own[:, at] = partial.astype(BF16)
        pending.append(local(dn_own.at[:, at], dn_out.at[:, at]))

    for k in range(4):
        get_xt[k].wait()
        make_terms(k, zl)
        if k == 0:
            here.all_in(count)
            links.send("dkv", dkv_in.at[far_tokens, :], dkv.at[zl], here.partner())
        send_early(k, zl)
        launch(k, 0, 1, zl)
    links.recv("dkv", dkv.at[1 - zl])
    for k in range(4):
        make_terms(k, 1 - zl)
        send_early(k, 1 - zl)
        launch(k, 0, 1, 1 - zl)
    get_dq.wait()
    others = (("p", 1 - zl, core), ("c", zl, 1 - core), ("d", 1 - zl, 1 - core))
    for way, zl_to, core_to in others:
        links.send(
            ("dq", way),
            dq_src.at[seq_rows(zl_to * 2 + core_to), :], dq_all.at[:, head_cols(zl, core)],
            here.dev(zl=zl_to, core=core_to),
        )
    get_w.wait()
    for k in range(4):
        for p in Z_FIRST:
            rings[p][k].forward()
        add_early(k)
        for h in range(2):
            launch(k, 2, 3, h)
        dn_far(2 * k)
        dn_far(2 * k + 1)

    def end_first(k, parts):
        for p in parts:
            rings[p][k].finish()
            for h in range(2):
                if k == 0:
                    finals[p].send_far(h)
                elif k < 3 and offs[k] == 2 * h - 1:
                    finals[p].send_near(h)

    for k in range(4):
        for p in Z_LAST:
            rings[p][k].forward()
        end_first(k, Z_FIRST)
        dn_near(2 * k)
        dn_near(2 * k + 1)
    for p in Z_FIRST:
        finals[p].forward()
    for k in range(4):
        end_first(k, Z_LAST)
    for p in Z_FIRST:
        finals[p].finish()
        rows = rows_of(p)
        links.send(
            ("z", p), term.at[here.y, far_z, here.x, rows, :], z_in.at[rows, :], here.cross()
        )
    for p in Z_LAST:
        finals[p].forward()

    def to_partner(p):
        rows = rows_of(p)
        links.send(("l", p), mine.at[rows, :], l_in.at[rows, :], here.partner())

    for p in Z_FIRST:
        rows = rows_of(p)
        links.recv(("z", p), z_in.at[rows, :])
        mine[rows, :] = (
            term[here.y, own_z, here.x, rows, :].astype(F32) + z_in[rows, :].astype(F32)
        ).astype(BF16)
        to_partner(p)
    for p in Z_LAST:
        finals[p].finish()
        rows = rows_of(p)
        mine[rows, :] = term[here.y, own_z, here.x, rows, :]
        to_partner(p)
    for p in range(4):
        rows = rows_of(p)
        links.recv(("l", p), l_in.at[rows, :])
        total[core, rows, :] = mine[rows, :].astype(F32) + l_in[rows, :].astype(F32)
        links.send(
            ("c", p), total.at[core, rows, :], total.at[core, rows, :], here.other_core()
        )
    own_dq.wait()
    for way, zl_to, core_to in others:
        links.recv(("dq", way), dq_all.at[:, head_cols(zl_to, core_to)])
    pending.append(local(dq_all, dq_out))
    for p in range(4):
        links.recv(("c", p), total.at[1 - core, rows_of(p), :])
    pending.append(local(total, grad_out))
    for copy in pending:
        copy.wait()
    links.drain()


def reduce_terms(xt, w, dkv, dq):
    rings = []
    for p, (_, rows, _, both) in enumerate(SUM_PARTS):
        nz = ZH if both else 1
        rings += [
            pltpu.VMEM((4, 2, nz, rows, HC), BF16),
            pltpu.VMEM((4, 2, nz, rows, COLS), BF16),
            pltpu.VMEM((2, nz, rows, HC), BF16),
            pltpu.VMEM((2, nz, rows, COLS), BF16),
        ]
    late = SUM_PARTS[2][1] + SUM_PARTS[3][1]
    return pl.pallas_call(
        reduce_kernel,
        out_shape=(
            jax.ShapeDtypeStruct((TOK, 4 * QW), BF16),
            jax.ShapeDtypeStruct((TOK, D), BF16),
            jax.ShapeDtypeStruct((2, ROWS, COLS), F32),
        ),
        in_specs=[ANY] * 4,
        out_specs=(ANY,) * 3,
        scratch_shapes=[
            pltpu.VMEM((D, CT), BF16),
            pltpu.VMEM((SHARDS, ROWS, COLS), BF16),
            pltpu.VMEM((Y, ZH, X, ROWS, COLS), BF16),
            pltpu.VMEM((2, CT, HC), BF16),
            pltpu.VMEM((SEQ, QW), BF16),
            pltpu.VMEM((TOK, 4 * QW), BF16),
            pltpu.VMEM((4, X, late, COLS), BF16),
            pltpu.VMEM((ROWS, COLS), BF16),
            pltpu.VMEM((ROWS, COLS), BF16),
            pltpu.VMEM((ROWS, COLS), BF16),
            pltpu.VMEM((2, ROWS, COLS), F32),
            pltpu.VMEM((TOK, D), BF16),
            pltpu.VMEM((TOK, D), BF16),
            pltpu.VMEM((TOK, D), BF16),
            *rings,
            pltpu.SemaphoreType.DMA((N_REDUCE_SEMS,)),
            pltpu.SemaphoreType.DMA((N_REDUCE_SEMS,)),
            pltpu.SemaphoreType.DMA((N_LOCAL_SEMS,)),
        ],
        compiler_params=pltpu.CompilerParams(
            collective_id=1, has_side_effects=True, vmem_limit_bytes=VMEM_LIMIT
        ),
        name="reduce_terms",
    )(xt, w, dkv, dq)


def update_kernel(
    tokens, dq_in, dn_in, total_in, master_in, one_in, two_in,
    dq_out, dn_out, master_out, one_out, two_out,
    dq, dn, total, master, one, two, in_sem, out_sem,
):
    gets, puts = [], []

    def get(src, dst):
        copy = pltpu.make_async_copy(src, dst, in_sem.at[len(gets)])
        copy.start()
        gets.append(copy)
        return copy

    def put(src, dst):
        copy = pltpu.make_async_copy(src, dst, out_sem.at[len(puts)])
        copy.start()
        puts.append(copy)

    first_gets = [get(total_in, total), get(master_in, master), get(one_in, one), get(two_in, two)]
    blocks = []
    for src, mid, dst, n in ((dn_in, dn, dn_out, 4), (dq_in, dq, dq_out, 2)):
        rows = src.shape[0] // n
        for b in range(n):
            at = pl.ds(b * rows, rows)
            blocks.append((get(src.at[at, :], mid.at[at, :]), mid.at[at, :], dst.at[at, :]))
    for copy in first_gets:
        copy.wait()
    rows = ROWS // 2
    for b in range(2):
        at = pl.ds(b * rows, rows)
        for h in range(2):
            cols = pl.ds(h * COLS, COLS)
            grad = total[h, at, :] * float(tokens) ** (-0.5)
            first = 0.9 * one[at, cols].astype(F32) + 0.1 * grad
            second = 0.999 * two[at, cols].astype(F32) + 0.001 * grad * grad
            master[at, cols] = master[at, cols] - 0.001 * (first / (1.0 - 0.9**3)) / (
                jnp.sqrt(second / (1.0 - 0.999**3)) + 1e-08
            )
            one[at, cols] = first.astype(BF16)
            two[at, cols] = second.astype(BF16)
        for mid, dst in ((master, master_out), (one, one_out), (two, two_out)):
            put(mid.at[at, :], dst.at[at, :])
        for copy, mid, dst in blocks[3 * b : 3 * b + 3]:
            copy.wait()
            put(mid, dst)
    for copy in puts:
        copy.wait()


def update(tokens, dq, dn, total, master, moment_one, moment_two):
    results = (dq, dn, master, moment_one, moment_two)
    return pl.pallas_call(
        functools.partial(update_kernel, tokens),
        out_shape=tuple(jax.ShapeDtypeStruct(a.shape, a.dtype) for a in results),
        in_specs=[ANY] * 6,
        out_specs=(ANY,) * 5,
        scratch_shapes=[
            *[pltpu.VMEM(a.shape, a.dtype) for a in (dq, dn, total, master, moment_one, moment_two)],
            pltpu.SemaphoreType.DMA((12,)),
            pltpu.SemaphoreType.DMA((12,)),
        ],
        compiler_params=pltpu.CompilerParams(vmem_limit_bytes=VMEM_LIMIT),
        name="update",
    )(dq, dn, total, master, moment_one, moment_two)


def on_device(normed, queries, output_gradient, doc_lengths, master, moment_one, moment_two):
    w, xt, q, do, kv = gather(normed, queries, output_gradient, master)
    dq, dkv = attention(doc_lengths, q, do, kv)
    dq, dn, total = reduce_terms(xt, w, dkv, dq)
    tokens = normed.shape[0] * lax.axis_size("dp") * lax.axis_size("seq")
    return update(tokens, dq, dn, total, master, moment_one, moment_two)


def solution(mesh):
    rows = P(("dp", "seq"), None)
    shard = P("dp", None)
    return jax.shard_map(
        on_device,
        mesh=mesh,
        in_specs=(rows, rows, rows, shard, shard, shard, shard),
        out_specs=(rows, rows, shard, shard, shard),
        check_vma=False,
    )
```

```python
import functools
import math

import jax
import jax.numpy as jnp
from jax import lax
from jax.experimental import pallas as pl
from jax.experimental.pallas import tpu as pltpu
from jax.sharding import PartitionSpec as P

HEAD = 128
GROUP = 7
X, Y, ZH = 4, 4, 2
TOK = 256
CT = 512
D = 7168
SHARDS = X * Y * ZH
ROWS = D // SHARDS
PARTS = (
    (0, 96, ("x", "y"), True),
    (96, 80, ("y", "x"), True),
    (176, 16, ("x", "y"), False),
    (192, 32, ("y", "x"), False),
)
SUM_PARTS = (
    (0, 80, ("x", "y"), True),
    (80, 80, ("y", "x"), True),
    (160, 32, ("x", "y"), False),
    (192, 32, ("y", "x"), False),
)
Z_FIRST = (0, 1)
Z_LAST = (2, 3)
SEQ = 1024
COLS = 512
HC = COLS // 2
QW = 896
ROW_BLOCK = X * ROWS
N_BLOCKS = Y * ZH
CHUNK = 128
N_CHUNKS = 5
LANES = GROUP * CHUNK
VMEM_LIMIT = 58 * 1024 * 1024
MESH = pl.DeviceIdType.MESH
ANY = pl.BlockSpec(memory_space=pl.ANY)
F32 = jnp.float32
BF16 = jnp.bfloat16


def dot(a, b, dims=((1,), (0,))):
    return lax.dot_general(a, b, (dims, ((), ())), preferred_element_type=F32)


class Place:
    def __init__(self):
        dp = lax.axis_index("dp")
        sq = lax.axis_index("seq")
        self.dp, self.sq = dp, sq
        self.x = lax.rem(dp, X)
        self.zh = lax.rem(lax.div(dp, X), ZH)
        self.y = lax.div(dp, X * ZH)
        self.core = lax.rem(sq, 2)
        self.zl = lax.div(sq, 2)

    def dev(self, x=None, y=None, zh=None, zl=None, core=None):
        x = self.x if x is None else x
        y = self.y if y is None else y
        zh = self.zh if zh is None else zh
        zl = self.zl if zl is None else zl
        core = self.core if core is None else core
        return ((y * ZH + zh) * X + x, zl * 2 + core)

    def along(self, axis, step):
        if axis == "x":
            return self.dev(x=lax.rem(self.x + step + X, X))
        return self.dev(y=lax.rem(self.y + step + Y, Y))

    def cross(self):
        return self.dev(zh=1 - self.zh, zl=1 - self.zl)

    def partner(self):
        return self.dev(zl=1 - self.zl)

    def other_core(self):
        return self.dev(core=1 - self.core)

    def greet(self):
        barrier = pltpu.get_barrier_semaphore()
        near = [self.along(a, s) for a in ("x", "y") for s in (1, -1)]
        near += [self.cross(), self.partner(), self.other_core()]
        near.append(self.dev(zl=1 - self.zl, core=1 - self.core))
        for d in near:
            pl.semaphore_signal(barrier, inc=1, device_id=d, device_id_type=MESH)
        return len(near)

    def all_in(self, count):
        pl.semaphore_wait(pltpu.get_barrier_semaphore(), count)


class Links:
    def __init__(self, send_sem, recv_sem, place):
        self.send_sem, self.recv_sem, self.place = send_sem, recv_sem, place
        self.index = {}
        self.used = 0
        self.sent = []

    def _copy(self, key, src, dst, dev, half=None):
        if key not in self.index:
            self.index[key] = self.used
            self.used += 1 if half is None else 2
        k = self.index[key] + (0 if half is None else half)
        return pltpu.make_async_remote_copy(
            src_ref=src,
            dst_ref=dst,
            send_sem=self.send_sem.at[k],
            recv_sem=self.recv_sem.at[k],
            device_id=dev,
            device_id_type=MESH,
        )

    def send(self, key, src, dst, dev, half=None):
        copy = self._copy(key, src, dst, dev, half)
        copy.start()
        self.sent.append(copy)

    def recv(self, key, dst, half=None):
        self._copy(key, dst, dst, self.place.other_core(), half).wait_recv()

    def drain(self):
        for copy in self.sent:
            copy.wait_send()


N_GATHER_SEMS = 176
N_LOCAL_SEMS = 40


def gather_kernel(
    normed, queries, out_grad, master,
    w_out, xt_out, q_out, do_out, kv_out,
    w, xs, xt, mas, kv, acc, q_src, do_src, q_all, do_all, send_sem, recv_sem, loc_sem,
):
    here = Place()
    links = Links(send_sem, recv_sem, here)
    n_local = [0]

    def local(src, dst):
        copy = pltpu.make_async_copy(src, dst, loc_sem.at[n_local[0]])
        n_local[0] += 1
        copy.start()
        return copy

    core, zl = here.core, here.zl
    own_rows = pl.ds(pl.multiple_of(core * TOK, TOK), TOK)
    far_rows = pl.ds(pl.multiple_of((1 - core) * TOK, TOK), TOK)

    def seq_rows(sq):
        return pl.ds(pl.multiple_of(sq * TOK, TOK), TOK)

    def head_cols(zl_to, core_to):
        return pl.ds(pl.multiple_of((core_to * 2 + zl_to) * QW, 128), QW)

    get_master = local(master.at[:, pl.ds(pl.multiple_of(core * COLS, COLS), COLS)], mas)
    get_q = local(queries, q_src)
    get_do = local(out_grad, do_src)
    own_normed = local(normed, xs.at[own_rows, :])
    own_q = local(queries.at[:, head_cols(zl, core)], q_all.at[seq_rows(here.sq), :])
    own_do = local(out_grad.at[:, head_cols(zl, core)], do_all.at[seq_rows(here.sq), :])
    pending = []
    count = here.greet()
    own = (here.y * ZH + here.zh) * X + here.x
    get_master.wait()
    w[own] = mas[...].astype(BF16)
    get_q.wait()
    get_do.wait()
    here.all_in(count)
    others = (("p", 1 - zl, core), ("d", 1 - zl, 1 - core), ("c", zl, 1 - core))

    def send_heads(ways):
        for name, src, dst in (("q", q_src, q_all), ("do", do_src, do_all)):
            for way, zl_to, core_to in ways:
                links.send(
                    (name, way),
                    src.at[:, head_cols(zl_to, core_to)], dst.at[seq_rows(here.sq), :],
                    here.dev(zl=zl_to, core=core_to),
                )

    send_heads(others[:2])
    pos = {"x": here.x, "y": here.y}
    size = {"x": X, "y": Y}

    def at_axis(axis, off):
        return lax.rem(pos[axis] + off + size[axis], size[axis])

    def slot(p, da, db, zr, half=None):
        row, rows, axes, _ = PARTS[p]
        at = {axes[0]: at_axis(axes[0], da), axes[1]: at_axis(axes[1], db)}
        zh = here.zh if zr == 0 else 1 - here.zh
        s = (at["y"] * ZH + zh) * X + at["x"]
        cols = pl.ds(0, COLS) if half is None else pl.ds(half * HC, HC)
        return w.at[s, pl.ds(row, rows), cols]

    def send(key, ref, dev):
        links.send(key, ref, ref, dev)

    def second_from(p, da, zr):
        b = PARTS[p][2][1]
        for step in (1, -1):
            send(("b", p, zr, da, step, 0), slot(p, da, 0, zr), here.along(b, step))

    def start(parts, zr):
        for p in parts:
            a = PARTS[p][2][0]
            for step in (1, -1):
                send(("a", p, zr, step, 0), slot(p, 0, 0, zr), here.along(a, step))
        for p in parts:
            second_from(p, 0, zr)

    def over_z(p, da, db):
        if p in Z_LAST:
            send(("z", p, da, db), slot(p, da, db, 0), here.cross())

    def forward_first(parts, zr):
        for p in parts:
            a = PARTS[p][2][0]
            for step in (1, -1):
                links.recv(("a", p, zr, step, 0), slot(p, -step, 0, zr))
                half = 0 if step == 1 else 1
                send(("a", p, zr, step, 1), slot(p, -step, 0, zr, half), here.along(a, step))
            for step in (1, -1):
                second_from(p, -step, zr)
                over_z(p, -step, 0)

    def finish_first(parts, zr):
        for p in parts:
            for step in (1, -1):
                half = 0 if step == 1 else 1
                links.recv(("a", p, zr, step, 1), slot(p, 2, 0, zr, half))
            second_from(p, 2, zr)
            over_z(p, 2, 0)

    def forward_second(parts, zr, after=None):
        for k, da in enumerate((0, -1, 1, 2)):
            for p in parts:
                b = PARTS[p][2][1]
                for step in (1, -1):
                    links.recv(("b", p, zr, da, step, 0), slot(p, da, -step, zr))
                    half = 0 if step == 1 else 1
                    send(
                        ("b", p, zr, da, step, 1),
                        slot(p, da, -step, zr, half),
                        here.along(b, step),
                    )
                    over_z(p, da, -step)
            if after is not None:
                after(k)

    def finish_second(parts, zr):
        for da in (0, -1, 1, 2):
            for p in parts:
                for step in (1, -1):
                    half = 0 if step == 1 else 1
                    links.recv(("b", p, zr, da, step, 1), slot(p, da, 2, zr, half))
                over_z(p, da, 2)

    def turn(first, last):
        @pl.loop(first, last)
        def _(b):
            at = pl.ds(pl.multiple_of(b * HEAD, HEAD), HEAD)
            xt[at, :] = xs[:, at].T

    start(Z_LAST, 0)
    start(Z_FIRST, 0)
    for p in Z_FIRST:
        send(("z", p), slot(p, 0, 0, 0), here.cross())
    for p in Z_LAST:
        over_z(p, 0, 0)
    links.send("normed", normed, xs.at[own_rows, :], here.other_core())
    send_heads(others[2:])
    forward_first(Z_LAST, 0)
    forward_first(Z_FIRST, 0)
    finish_first(Z_LAST, 0)
    for p in Z_FIRST:
        links.recv(("z", p), slot(p, 0, 0, 1))
    start(Z_FIRST, 1)
    finish_first(Z_FIRST, 0)
    own_normed.wait()
    links.recv("normed", xs.at[far_rows, :])
    turn(0, 14)
    forward_second(Z_LAST, 0)
    forward_first(Z_FIRST, 1)
    turn(14, 28)
    finish_second(Z_LAST, 0)
    finish_first(Z_FIRST, 1)
    turn(28, 42)
    forward_second(Z_FIRST, 0)
    turn(42, 56)
    pending.append(local(xt, xt_out))
    finish_second(Z_FIRST, 0)
    acc[...] = jnp.zeros_like(acc)

    def project(y, zh, cols, into):
        at = pl.ds(pl.multiple_of((y * ZH + zh) * ROW_BLOCK, 128), ROW_BLOCK)
        w_t = w[pl.ds((y * ZH + zh) * X, X), :, cols].reshape(ROW_BLOCK, HC)
        acc[into] += dot(xs[:, at], w_t)

    own_head = pl.ds(pl.multiple_of(zl * HC, HC), HC)
    far_head = pl.ds(pl.multiple_of((1 - zl) * HC, HC), HC)

    def own_half(k):
        project(k, here.zh, far_head, 0)
        project(k, here.zh, own_head, 1)

    forward_second(Z_FIRST, 1, own_half)
    finish_second(Z_FIRST, 1)
    for p in Z_LAST:
        for da in (0, -1, 1, 2):
            for db in (0, -1, 1, 2):
                links.recv(("z", p, da, db), slot(p, da, db, 1))
    pending.append(local(w, w_out))

    own_tokens = pl.ds(pl.multiple_of(zl * CT, CT), CT)
    for into, cols in ((0, far_head), (1, own_head)):

        @pl.loop(0, Y)
        def _(y):
            project(y, 1 - here.zh, cols, into)

        kv[into] = acc[into].astype(BF16)
        if into == 0:
            links.send("kv", kv.at[0], kv_out.at[own_tokens, :], here.partner())
        else:
            pending.append(local(kv.at[1], kv_out.at[own_tokens, :]))
    own_q.wait()
    own_do.wait()
    for name, dst in (("q", q_all), ("do", do_all)):
        for way, zl_to, core_to in others:
            links.recv((name, way), dst.at[seq_rows(zl_to * 2 + core_to), :])
    pending.append(local(q_all, q_out))
    pending.append(local(do_all, do_out))
    links.recv("kv", kv_out.at[pl.ds(pl.multiple_of((1 - zl) * CT, CT), CT), :])
    for copy in pending:
        copy.wait()
    links.drain()


def gather(normed, queries, out_grad, master):
    return pl.pallas_call(
        gather_kernel,
        out_shape=(
            jax.ShapeDtypeStruct((SHARDS, ROWS, COLS), BF16),
            jax.ShapeDtypeStruct((D, CT), BF16),
            jax.ShapeDtypeStruct((SEQ, QW), BF16),
            jax.ShapeDtypeStruct((SEQ, QW), BF16),
            jax.ShapeDtypeStruct((SEQ, HC), BF16),
        ),
        in_specs=[ANY] * 4,
        out_specs=(ANY,) * 5,
        scratch_shapes=[
            pltpu.VMEM((SHARDS, ROWS, COLS), BF16),
            pltpu.VMEM((CT, D), BF16),
            pltpu.VMEM((D, CT), BF16),
            pltpu.VMEM((ROWS, COLS), F32),
            pltpu.VMEM((2, CT, HC), BF16),
            pltpu.VMEM((2, CT, HC), F32),
            pltpu.VMEM(queries.shape, BF16),
            pltpu.VMEM(queries.shape, BF16),
            pltpu.VMEM((SEQ, QW), BF16),
            pltpu.VMEM((SEQ, QW), BF16),
            pltpu.SemaphoreType.DMA((N_GATHER_SEMS,)),
            pltpu.SemaphoreType.DMA((N_GATHER_SEMS,)),
            pltpu.SemaphoreType.DMA((N_LOCAL_SEMS,)),
        ],
        compiler_params=pltpu.CompilerParams(
            collective_id=0, has_side_effects=True, vmem_limit_bytes=VMEM_LIMIT
        ),
        name="gather_project",
    )(normed, queries, out_grad, master)


def attention_kernel(
    lengths, q_ref, do_ref, kv_ref, dq_ref, dkv_ref,
    qs, dos, prob, dprob, prob_half, d_scores, dk_acc, dv_acc,
):
    i = pl.program_id(0)
    scale = HEAD ** (-0.5)
    to_base2 = scale * math.log2(math.e)
    ends = []
    total = lengths[0, 0]
    ends.append(total)
    for j in range(1, lengths.shape[1]):
        total = total + lengths[0, j]
        ends.append(total)

    @pl.when(i == 0)
    def _():
        dk_acc[...] = jnp.zeros_like(dk_acc)
        dv_acc[...] = jnp.zeros_like(dv_acc)

    lane = lax.broadcasted_iota(jnp.int32, (1, CHUNK), 1)
    sub = lax.broadcasted_iota(jnp.int32, (CHUNK, 1), 0)
    q_row = i * CHUNK + lane
    doc_start = jnp.zeros_like(q_row)
    first_start = jnp.int32(0)
    for e in ends:
        doc_start = jnp.where(q_row >= e, jnp.maximum(doc_start, e), doc_start)
        first_start = jnp.where(i * CHUNK >= e, jnp.maximum(first_start, e), first_start)
    lowest = lax.div(first_start, CHUNK)
    lowest = jnp.maximum(lowest, i - (N_CHUNKS - 1))
    for a in range(GROUP):
        qs[a * CHUNK : (a + 1) * CHUNK, :] = q_ref[:, a * HEAD : (a + 1) * HEAD]
        dos[a * CHUNK : (a + 1) * CHUNK, :] = do_ref[:, a * HEAD : (a + 1) * HEAD]

    def chunks(n):
        low = i + 1 - n
        keys = pl.ds(pl.multiple_of(low * CHUNK, CHUNK), n * CHUNK)
        here = slice(0, n * CHUNK)
        prob[here, :] = dot(kv_ref[keys, 0:HEAD], qs[...], ((1,), (1,)))
        dprob[here, :] = dot(kv_ref[keys, HEAD : 2 * HEAD], dos[...], ((1,), (1,)))
        for a in range(GROUP):
            cols = slice(a * CHUNK, (a + 1) * CHUNK)
            parts = []
            top = None
            for t in range(n):
                k_row = (low + t) * CHUNK + sub
                keep = k_row >= doc_start
                if t == n - 1:
                    keep = keep & (k_row <= q_row)
                part = jnp.where(keep, prob[t * CHUNK : (t + 1) * CHUNK, cols], -1e30)
                parts.append(part)
                most = jnp.max(part, axis=0, keepdims=True)
                top = most if top is None else jnp.maximum(top, most)
            mass = jnp.zeros((1, CHUNK), F32)
            delta = jnp.zeros((1, CHUNK), F32)
            for t in range(n):
                p = jnp.exp2((parts[t] - top) * to_base2)
                parts[t] = p
                mass = mass + jnp.sum(p, axis=0, keepdims=True)
                dp = dprob[t * CHUNK : (t + 1) * CHUNK, cols]
                delta = delta + jnp.sum(p * dp, axis=0, keepdims=True)
            inv = 1.0 / mass
            delta = delta * inv
            for t in range(n):
                rows = slice(t * CHUNK, (t + 1) * CHUNK)
                p = parts[t] * inv
                prob_half[rows, cols] = p.astype(BF16)
                d_scores[rows, cols] = (p * (dprob[rows, cols] - delta)).astype(BF16)
        dv_acc[keys, :] += dot(prob_half[here, :], dos[...])
        dk_acc[keys, :] += dot(d_scores[here, :], qs[...])
        dq_t = dot(kv_ref[keys, 0:HEAD], d_scores[here, :], ((0,), (0,)))
        for a in range(GROUP):
            part = (dq_t[:, a * CHUNK : (a + 1) * CHUNK] * scale).astype(BF16)
            dq_ref[:, a * HEAD : (a + 1) * HEAD] = part.T

    for n in range(1, N_CHUNKS + 1):
        pl.when(i + 1 - lowest == n)(functools.partial(chunks, n))

    @pl.when(i == pl.num_programs(0) - 1)
    def _():
        dkv_ref[:, 0:HEAD] = (dk_acc[...] * scale).astype(BF16)
        dkv_ref[:, HEAD : 2 * HEAD] = dv_acc[...].astype(BF16)


def attention(lengths, q, do, kv):
    return pl.pallas_call(
        attention_kernel,
        grid=(SEQ // CHUNK,),
        out_shape=(
            jax.ShapeDtypeStruct((SEQ, QW), BF16),
            jax.ShapeDtypeStruct((SEQ, HC), BF16),
        ),
        in_specs=[
            pl.BlockSpec(memory_space=pltpu.SMEM),
            pl.BlockSpec((CHUNK, QW), lambda i: (i, 0)),
            pl.BlockSpec((CHUNK, QW), lambda i: (i, 0)),
            pl.BlockSpec((SEQ, HC), lambda i: (0, 0)),
        ],
        out_specs=(
            pl.BlockSpec((CHUNK, QW), lambda i: (i, 0)),
            pl.BlockSpec((SEQ, HC), lambda i: (0, 0)),
        ),
        scratch_shapes=[
            pltpu.VMEM((LANES, HEAD), BF16),
            pltpu.VMEM((LANES, HEAD), BF16),
            pltpu.VMEM((N_CHUNKS * CHUNK, LANES), F32),
            pltpu.VMEM((N_CHUNKS * CHUNK, LANES), F32),
            pltpu.VMEM((N_CHUNKS * CHUNK, LANES), BF16),
            pltpu.VMEM((N_CHUNKS * CHUNK, LANES), BF16),
            pltpu.VMEM((SEQ, HEAD), F32),
            pltpu.VMEM((SEQ, HEAD), F32),
        ],
        compiler_params=pltpu.CompilerParams(vmem_limit_bytes=VMEM_LIMIT),
        name="attention_back",
    )(lengths, q, do, kv)


N_REDUCE_SEMS = 176


def reduce_kernel(
    xt_in, w_in, dkv_in, dq_in,
    dq_out, dn_out, grad_out,
    xt, w, term, dkv, dq_src, dq_all, z_early, z_in, l_in, mine, total, dn_send, dn_recv, dn_own,
    *rest,
):
    bufs = [rest[4 * p : 4 * p + 4] for p in range(4)]
    send_sem, recv_sem, loc_sem = rest[16:]
    here = Place()
    links = Links(send_sem, recv_sem, here)
    n_local = [0]

    def local(src, dst):
        copy = pltpu.make_async_copy(src, dst, loc_sem.at[n_local[0]])
        n_local[0] += 1
        copy.start()
        return copy

    core, zl = here.core, here.zl
    own_z, far_z = here.zh, 1 - here.zh
    own_rows = pl.ds(pl.multiple_of(core * TOK, TOK), TOK)
    far_rows = pl.ds(pl.multiple_of((1 - core) * TOK, TOK), TOK)
    own_tokens = pl.ds(pl.multiple_of(zl * CT, CT), CT)
    far_tokens = pl.ds(pl.multiple_of((1 - zl) * CT, CT), CT)

    def seq_rows(sq):
        return pl.ds(pl.multiple_of(sq * TOK, TOK), TOK)

    def head_cols(zl_of, core_of):
        return pl.ds(pl.multiple_of((core_of * 2 + zl_of) * QW, 128), QW)

    get_dkv = local(dkv_in.at[own_tokens, :], dkv.at[zl])
    offs = (2, 1, -1, 0)
    get_xt = []
    for off in offs:
        y = lax.rem(here.y + off + Y, Y)
        at = pl.ds(pl.multiple_of(y * ZH * ROW_BLOCK, 128), ZH * ROW_BLOCK)
        get_xt.append(local(xt_in.at[at, :], xt.at[at, :]))
    get_dq = local(dq_in, dq_src)
    own_dq = local(dq_in.at[seq_rows(here.sq), :], dq_all.at[:, head_cols(zl, core)])
    count = here.greet()
    get_w = local(w_in, w)
    pending = []
    get_dkv.wait()

    pos = {"x": here.x, "y": here.y}
    size = {"x": X, "y": Y}

    def at_axis(axis, off):
        return lax.rem(pos[axis] + off + size[axis], size[axis])

    class Ring:
        def __init__(self, name, axis, slot, opp, land):
            self.name, self.axis, self.slot = name, axis, slot
            self.opp, self.land = opp, land

        def half(self, ref, h):
            start = h * HC if isinstance(h, int) else pl.multiple_of(h * HC, HC)
            return ref.at[:, :, pl.ds(start, HC)]

        def send_far(self, h):
            links.send(
                (self.name, "far"),
                self.half(self.slot(2), h), self.opp(h), here.along(self.axis, 1 - 2 * h), h,
            )

        def send_near(self, h):
            step = 2 * h - 1
            links.send(
                (self.name, "near"),
                self.half(self.slot(step), h), self.half(self.land(1 - h), h),
                here.along(self.axis, step), h,
            )

        def forward(self):
            for h, step in ((0, 1), (1, -1)):
                links.recv((self.name, "far"), self.opp(h), h)
                here_sum = self.half(self.slot(step), h)
                here_sum[...] = (
                    here_sum[...].astype(F32) + self.opp(h)[...].astype(F32)
                ).astype(BF16)
                links.send(
                    (self.name, "sum"),
                    here_sum, self.half(self.land(h), h), here.along(self.axis, step), h,
                )

        def finish(self):
            for h in range(2):
                links.recv((self.name, "near"), self.half(self.land(1 - h), h), h)
                links.recv((self.name, "sum"), self.half(self.land(h), h), h)
            mine_ref = self.slot(0)
            mine_ref[...] = (
                mine_ref[...].astype(F32)
                + self.land(0)[...].astype(F32)
                + self.land(1)[...].astype(F32)
            ).astype(BF16)

    def rows_of(p):
        return pl.ds(SUM_PARTS[p][0], SUM_PARTS[p][1])

    def term_at(at, p):
        zs = pl.ds(0, ZH) if p in Z_FIRST else pl.ds(own_z, 1)
        return term.at[at["y"], zs, at["x"], rows_of(p), :]

    def first_ring(p, k, off):
        a, b = SUM_PARTS[p][2]
        opp, land = bufs[p][:2]

        def slot(da):
            return term_at({a: at_axis(a, da), b: at_axis(b, off)}, p)

        return Ring(
            ("first", p, k), a, slot,
            lambda h: opp.at[k, h], lambda side: land.at[k, side],
        )

    def second_ring(p):
        a, b = SUM_PARTS[p][2]
        opp, land = bufs[p][2:]

        def slot(db):
            return term_at({a: pos[a], b: at_axis(b, db)}, p)

        return Ring(("second", p), b, slot, lambda h: opp.at[h], lambda side: land.at[side])

    rings = [[first_ring(p, k, off) for k, off in enumerate(offs)] for p in range(4)]
    finals = [second_ring(p) for p in range(4)]
    late = pl.ds(SUM_PARTS[2][0], SUM_PARTS[2][1] + SUM_PARTS[3][1])

    def make_terms(k, h):
        y = at_axis("y", offs[k])
        cols = pl.ds(pl.multiple_of(h * HC, HC), HC)
        for z in (far_z, own_z):
            at = pl.ds(pl.multiple_of((y * ZH + z) * ROW_BLOCK, 128), ROW_BLOCK)
            t = dot(xt[at, :], dkv[h]).astype(BF16)
            term[y, z, :, :, cols] = t.reshape(X, ROWS, HC)

    def send_early(k, h):
        y = at_axis("y", offs[k])
        cols = pl.ds(pl.multiple_of(h * HC, HC), HC)
        links.send(
            ("early", k),
            term.at[y, far_z, :, late, cols], z_early.at[k, :, :, cols], here.cross(), h,
        )

    def add_early(k):
        y = at_axis("y", offs[k])
        for h in range(2):
            links.recv(("early", k), z_early.at[k, :, :, pl.ds(h * HC, HC)], h)
        into = term.at[y, own_z, :, late, :]
        into[...] = (into[...].astype(F32) + z_early[k].astype(F32)).astype(BF16)

    def launch(k, p_x, p_y, h):
        rings[p_x][k].send_far(h)
        rings[p_x][k].send_near(h)
        for piece in rings[p_y]:
            if k == 0:
                piece.send_far(h)
            elif k == 2:
                piece.send_near(h)

    def dn_far(t):
        at = pl.ds(t * ROW_BLOCK, ROW_BLOCK)
        partial = jnp.zeros((TOK, ROW_BLOCK), F32)
        for h in range(2):
            w_t = w[pl.ds(t * X, X), :, h * HC : (h + 1) * HC].reshape(ROW_BLOCK, HC)
            partial += dot(dkv[h, far_rows, :], w_t, ((1,), (1,)))
        dn_send[:, at] = partial.astype(BF16)
        links.send(("dn", t), dn_send.at[:, at], dn_recv.at[:, at], here.other_core())

    def dn_near(t):
        at = pl.ds(t * ROW_BLOCK, ROW_BLOCK)
        links.recv(("dn", t), dn_recv.at[:, at])
        partial = dn_recv[:, at].astype(F32)
        for h in range(2):
            w_t = w[pl.ds(t * X, X), :, h * HC : (h + 1) * HC].reshape(ROW_BLOCK, HC)
            partial += dot(dkv[h, own_rows, :], w_t, ((1,), (1,)))
        dn_own[:, at] = partial.astype(BF16)
        pending.append(local(dn_own.at[:, at], dn_out.at[:, at]))

    for k in range(4):
        get_xt[k].wait()
        make_terms(k, zl)
        if k == 0:
            here.all_in(count)
            links.send("dkv", dkv_in.at[far_tokens, :], dkv.at[zl], here.partner())
        send_early(k, zl)
        launch(k, 0, 1, zl)
    links.recv("dkv", dkv.at[1 - zl])
    for k in range(4):
        make_terms(k, 1 - zl)
        send_early(k, 1 - zl)
        launch(k, 0, 1, 1 - zl)
    get_dq.wait()
    others = (("p", 1 - zl, core), ("c", zl, 1 - core), ("d", 1 - zl, 1 - core))
    for way, zl_to, core_to in others:
        links.send(
            ("dq", way),
            dq_src.at[seq_rows(zl_to * 2 + core_to), :], dq_all.at[:, head_cols(zl, core)],
            here.dev(zl=zl_to, core=core_to),
        )
    get_w.wait()
    for k in range(4):
        for p in Z_FIRST:
            rings[p][k].forward()
        add_early(k)
        for h in range(2):
            launch(k, 2, 3, h)
        dn_far(2 * k)
        dn_far(2 * k + 1)

    def end_first(k, parts):
        for p in parts:
            rings[p][k].finish()
            for h in range(2):
                if k == 0:
                    finals[p].send_far(h)
                elif k < 3 and offs[k] == 2 * h - 1:
                    finals[p].send_near(h)

    for k in range(4):
        for p in Z_LAST:
            rings[p][k].forward()
        end_first(k, Z_FIRST)
        dn_near(2 * k)
        dn_near(2 * k + 1)
    for p in Z_FIRST:
        finals[p].forward()
    for k in range(4):
        end_first(k, Z_LAST)
    for p in Z_FIRST:
        finals[p].finish()
        rows = rows_of(p)
        links.send(
            ("z", p), term.at[here.y, far_z, here.x, rows, :], z_in.at[rows, :], here.cross()
        )
    for p in Z_LAST:
        finals[p].forward()

    def to_partner(p):
        rows = rows_of(p)
        links.send(("l", p), mine.at[rows, :], l_in.at[rows, :], here.partner())

    for p in Z_FIRST:
        rows = rows_of(p)
        links.recv(("z", p), z_in.at[rows, :])
        mine[rows, :] = (
            term[here.y, own_z, here.x, rows, :].astype(F32) + z_in[rows, :].astype(F32)
        ).astype(BF16)
        to_partner(p)
    for p in Z_LAST:
        finals[p].finish()
        rows = rows_of(p)
        mine[rows, :] = term[here.y, own_z, here.x, rows, :]
        to_partner(p)
    for p in range(4):
        rows = rows_of(p)
        links.recv(("l", p), l_in.at[rows, :])
        total[core, rows, :] = mine[rows, :].astype(F32) + l_in[rows, :].astype(F32)
        links.send(
            ("c", p), total.at[core, rows, :], total.at[core, rows, :], here.other_core()
        )
    own_dq.wait()
    for way, zl_to, core_to in others:
        links.recv(("dq", way), dq_all.at[:, head_cols(zl_to, core_to)])
    pending.append(local(dq_all, dq_out))
    for p in range(4):
        links.recv(("c", p), total.at[1 - core, rows_of(p), :])
    pending.append(local(total, grad_out))
    for copy in pending:
        copy.wait()
    links.drain()


def reduce_terms(xt, w, dkv, dq):
    rings = []
    for p, (_, rows, _, both) in enumerate(SUM_PARTS):
        nz = ZH if both else 1
        rings += [
            pltpu.VMEM((4, 2, nz, rows, HC), BF16),
            pltpu.VMEM((4, 2, nz, rows, COLS), BF16),
            pltpu.VMEM((2, nz, rows, HC), BF16),
            pltpu.VMEM((2, nz, rows, COLS), BF16),
        ]
    late = SUM_PARTS[2][1] + SUM_PARTS[3][1]
    return pl.pallas_call(
        reduce_kernel,
        out_shape=(
            jax.ShapeDtypeStruct((TOK, 4 * QW), BF16),
            jax.ShapeDtypeStruct((TOK, D), BF16),
            jax.ShapeDtypeStruct((2, ROWS, COLS), F32),
        ),
        in_specs=[ANY] * 4,
        out_specs=(ANY,) * 3,
        scratch_shapes=[
            pltpu.VMEM((D, CT), BF16),
            pltpu.VMEM((SHARDS, ROWS, COLS), BF16),
            pltpu.VMEM((Y, ZH, X, ROWS, COLS), BF16),
            pltpu.VMEM((2, CT, HC), BF16),
            pltpu.VMEM((SEQ, QW), BF16),
            pltpu.VMEM((TOK, 4 * QW), BF16),
            pltpu.VMEM((4, X, late, COLS), BF16),
            pltpu.VMEM((ROWS, COLS), BF16),
            pltpu.VMEM((ROWS, COLS), BF16),
            pltpu.VMEM((ROWS, COLS), BF16),
            pltpu.VMEM((2, ROWS, COLS), F32),
            pltpu.VMEM((TOK, D), BF16),
            pltpu.VMEM((TOK, D), BF16),
            pltpu.VMEM((TOK, D), BF16),
            *rings,
            pltpu.SemaphoreType.DMA((N_REDUCE_SEMS,)),
            pltpu.SemaphoreType.DMA((N_REDUCE_SEMS,)),
            pltpu.SemaphoreType.DMA((N_LOCAL_SEMS,)),
        ],
        compiler_params=pltpu.CompilerParams(
            collective_id=1, has_side_effects=True, vmem_limit_bytes=VMEM_LIMIT
        ),
        name="reduce_terms",
    )(xt, w, dkv, dq)


def update_kernel(
    tokens, dq_in, dn_in, total_in, master_in, one_in, two_in,
    dq_out, dn_out, master_out, one_out, two_out,
    dq, dn, total, master, one, two, in_sem, out_sem,
):
    gets, puts = [], []

    def get(src, dst):
        copy = pltpu.make_async_copy(src, dst, in_sem.at[len(gets)])
        copy.start()
        gets.append(copy)
        return copy

    def put(src, dst):
        copy = pltpu.make_async_copy(src, dst, out_sem.at[len(puts)])
        copy.start()
        puts.append(copy)

    adam = ((total_in, total), (master_in, master), (one_in, one), (two_in, two))
    blocks = []
    for src, mid, dst, n in ((dn_in, dn, dn_out, 4), (dq_in, dq, dq_out, 2)):
        rows = src.shape[0] // n
        for b in range(n):
            at = pl.ds(b * rows, rows)
            blocks.append((get(src.at[at, :], mid.at[at, :]), mid.at[at, :], dst.at[at, :]))
            if len(blocks) == 2:
                first_gets = [get(near, far) for near, far in adam]
    for copy, mid, dst in blocks[:2]:
        copy.wait()
        put(mid, dst)
    for copy in first_gets:
        copy.wait()
    rows = ROWS // 2
    for b in range(2):
        at = pl.ds(b * rows, rows)
        for h in range(2):
            cols = pl.ds(h * COLS, COLS)
            grad = total[h, at, :] * float(tokens) ** (-0.5)
            first = 0.9 * one[at, cols].astype(F32) + 0.1 * grad
            second = 0.999 * two[at, cols].astype(F32) + 0.001 * grad * grad
            master[at, cols] = master[at, cols] - 0.001 * (first / (1.0 - 0.9**3)) / (
                jnp.sqrt(second / (1.0 - 0.999**3)) + 1e-08
            )
            one[at, cols] = first.astype(BF16)
            two[at, cols] = second.astype(BF16)
        for mid, dst in ((master, master_out), (one, one_out), (two, two_out)):
            put(mid.at[at, :], dst.at[at, :])
        for copy, mid, dst in blocks[2 * b + 2 : 2 * b + 4]:
            copy.wait()
            put(mid, dst)
    for copy in puts:
        copy.wait()


def update(tokens, dq, dn, total, master, moment_one, moment_two):
    results = (dq, dn, master, moment_one, moment_two)
    return pl.pallas_call(
        functools.partial(update_kernel, tokens),
        out_shape=tuple(jax.ShapeDtypeStruct(a.shape, a.dtype) for a in results),
        in_specs=[ANY] * 6,
        out_specs=(ANY,) * 5,
        scratch_shapes=[
            *[pltpu.VMEM(a.shape, a.dtype) for a in (dq, dn, total, master, moment_one, moment_two)],
            pltpu.SemaphoreType.DMA((12,)),
            pltpu.SemaphoreType.DMA((12,)),
        ],
        compiler_params=pltpu.CompilerParams(vmem_limit_bytes=VMEM_LIMIT),
        name="update",
    )(dq, dn, total, master, moment_one, moment_two)


def on_device(normed, queries, output_gradient, doc_lengths, master, moment_one, moment_two):
    w, xt, q, do, kv = gather(normed, queries, output_gradient, master)
    dq, dkv = attention(doc_lengths, q, do, kv)
    dq, dn, total = reduce_terms(xt, w, dkv, dq)
    tokens = normed.shape[0] * lax.axis_size("dp") * lax.axis_size("seq")
    return update(tokens, dq, dn, total, master, moment_one, moment_two)


def solution(mesh):
    rows = P(("dp", "seq"), None)
    shard = P("dp", None)
    return jax.shard_map(
        on_device,
        mesh=mesh,
        in_specs=(rows, rows, rows, shard, shard, shard, shard),
        out_specs=(rows, rows, shard, shard, shard),
        check_vma=False,
    )
```
